32 devices in a mesh: rows: 8 (over z, x), sub: 4 (over y, core).
Axes of the slice: x: 2, y: 2, z: 4, core: 2. Of those that a mesh axis runs over, the one named last changes fastest.
Arguments:
- diag_blocks: bfloat16 [512, 128, 128], P(('rows', 'sub')), may hold values from -1 to 4
- off_blocks: bfloat16 [512, 8, 128, 128], P(('rows', 'sub')), may hold values from -0.5 to 0.5
- col_blocks: int32 [512, 8], P(('rows', 'sub')), may hold values from 0 to 511, as said below
- sketch: bfloat16 [65536, 256], P(('rows', 'sub')), may hold values from -6 to 6
Outputs:
- basis: float32 [65536, 256], P(('rows', 'sub'))
- factor: float32 [256, 256], replicated
The draws below stay inside these ranges and needn't reach their ends.
Inputs may be any that keep to these rules, and one draw needn't show every extreme that they name: `col_blocks`: in the 128 entries of the rows of one device (16 block rows), at most 8 lie in the range of any one device's 16 block rows; in every draw the range of some device receives exactly 8 from every device.
All inputs are finite; a program needn't handle non-finite values.
Results may differ from the reference program's by a relative error of at most 0.002.
Values may be sent and summed in bfloat16 or wider, within the bound.
No kernel may reach another device: no remote copies, remote signals or barrier semaphores. Data moves between devices by JAX's collectives and lax.ppermute only.
A program may use at most 256 MiB of HBM per device.

```python
import jax
import jax.numpy as jnp
from jax import lax

BLOCK = 128
SKETCH = 256
K = 8
BR = 16
DEVICE_TOTAL = 32
MAX_COLUMN_HITS = 8
NB = 512
ROWS = 65536


def draw_diag_blocks(key, part):
    noise = jax.random.normal(key, (NB, BLOCK, BLOCK), jnp.float32)
    scale_sym = 0.3 / (2.0 * (2.0 * BLOCK) ** 0.5)
    symmetric = (noise + jnp.transpose(noise, (0, 2, 1))) * scale_sym
    position = jnp.arange(NB).astype(jnp.float32) / max(NB - 1, 1)
    level = 1.0 + 2.0 * position
    identity = jnp.eye(BLOCK, dtype=jnp.float32)
    return (identity[None, :, :] * level[:, None, None] + symmetric).astype(jnp.bfloat16)


def draw_col_blocks(key, part):
    key_extra = jax.random.fold_in(key, 11)
    key_hot = jax.random.fold_in(key, 12)
    key_rest = jax.random.fold_in(key, 13)
    target_positions = DEVICE_TOTAL * MAX_COLUMN_HITS
    extra_weight = jax.random.randint(key_extra, (DEVICE_TOTAL,), 0, 4) * target_positions
    busiest_device = jax.random.randint(key_hot, (), 0, DEVICE_TOTAL)
    extra_weight = jnp.where(jnp.arange(DEVICE_TOTAL) == busiest_device, 8 * target_positions, extra_weight)
    extra_positions = jnp.repeat(extra_weight, MAX_COLUMN_HITS)

    def one_device(device):
        device_key = jax.random.fold_in(key_rest, device)
        key_first = jax.random.fold_in(device_key, 1)
        key_two = jax.random.fold_in(device_key, 2)
        key_three = jax.random.fold_in(device_key, 3)
        device_scores = extra_positions + jax.random.permutation(key_first, target_positions)
        unused, chosen = lax.top_k(device_scores, BR * K)
        chosen = chosen[jax.random.permutation(key_two, BR * K)]
        owners = chosen // MAX_COLUMN_HITS
        local = jax.random.randint(key_three, (BR * K,), 0, BR)
        return (owners * BR + local).reshape(BR, K)
    return jax.vmap(one_device)(jnp.arange(DEVICE_TOTAL)).reshape(NB, K).astype(jnp.int32)


def block_levels(own_key, extent, pieces, low, top_value):
    gain, own = 1.0, jax.random.fold_in(own_key, 6)
    for dim, parts in pieces:
        steps = jnp.exp(jax.random.uniform(jax.random.fold_in(own, dim), (parts,), jnp.float32, low / len(pieces), top_value / len(pieces)))
        gain = gain * jnp.repeat(steps, extent[dim] // parts).reshape([-1 if axis == dim else 1 for axis in range(len(extent))])
    return gain


def gaussian(stream_key, extent, scale, reach, pieces=(), kind=jnp.bfloat16):
    gain = block_levels(stream_key, extent, pieces, -0.22, 0.18) if pieces else 1.0
    array = jax.random.normal(stream_key, extent, jnp.float32) * scale * gain
    return jnp.minimum(jnp.maximum(array, -reach), reach).astype(kind)


def setup_inputs(seed: int = 0) -> dict:
    seeds = jax.random.split(jax.random.key(seed), 5)
    return {
        "diag_blocks": draw_diag_blocks(jax.random.fold_in(seeds[4], 71), 0),
        "off_blocks": gaussian(seeds[1], (NB, K, BLOCK, BLOCK), BLOCK ** -0.5, 0.5, ((0, 32),)),
        "col_blocks": draw_col_blocks(jax.random.fold_in(seeds[4], 71), 0),
        "sketch": gaussian(seeds[3], (ROWS, SKETCH), 1.0, 6.0, ((0, 32),)),
    }


def reference(diag_blocks, off_blocks, col_blocks, sketch):
    omega = sketch.reshape(NB, BLOCK, SKETCH)

    def advance(index, image):
        blocks = off_blocks[index].astype(jnp.float32)
        targets = col_blocks[index].astype(jnp.int32)
        here = omega[index].astype(jnp.float32)
        near = jnp.dot(diag_blocks[index].astype(jnp.float32), omega[index].astype(jnp.float32), preferred_element_type=jnp.float32)
        remote = omega[targets].astype(jnp.float32)
        far = jnp.einsum('kij,kjc->ic', blocks, remote)
        mirror = jnp.einsum('kji,jc->kic', blocks, here).astype(jnp.bfloat16)
        mirror = lax.optimization_barrier(mirror).astype(jnp.float32)
        image = image.at[index].add(near + far)
        return image.at[targets].add(mirror)
    image = lax.fori_loop(0, NB, advance, jnp.zeros((NB, BLOCK, SKETCH), jnp.float32))
    image = image.reshape(ROWS, SKETCH)
    gram = jnp.dot(image.T.astype(jnp.float32), image.astype(jnp.float32), precision=lax.Precision.HIGHEST, preferred_element_type=jnp.float32) / ROWS
    lower = jnp.linalg.cholesky(gram)
    basis = lax.linalg.triangular_solve(lower, image, left_side=False, lower=True, transpose_a=True)
    return (basis, lower.T)
```

```python
import functools
import math

import jax
import jax.numpy as jnp
from jax import lax
from jax.experimental import pallas as pl
from jax.experimental.pallas import tpu as pltpu
from jax.sharding import Mesh
from jax.sharding import PartitionSpec as P

LINE = "z"
PLANE = ("x", "y", "c")
ALL = (LINE,) + PLANE
VMEM_LIMIT = 48 * 1024 * 1024
TAIL = 16


def dot(a, b, contract=((1,), (0,)), precision=None):
    return lax.dot_general(
        a, b, (contract, ((), ())), precision=precision, preferred_element_type=jnp.float32
    )


def params():
    return pltpu.CompilerParams(vmem_limit_bytes=VMEM_LIMIT)


def pack_kernel(plane_ref, slot_ref, off_ref, label_ref, out_ref, sem, label_sem):
    count, edge, _ = off_ref.shape
    tail = label_ref.shape[1]
    last = out_ref.shape[1] - tail
    labels = pltpu.make_async_copy(label_ref, out_ref.at[:, pl.ds(last, tail), :], label_sem)
    labels.start()

    def send(entry, carry):
        row = pl.multiple_of(slot_ref[entry] * edge, edge)
        pltpu.make_async_copy(
            off_ref.at[entry], out_ref.at[plane_ref[entry], pl.ds(row, edge), :], sem
        ).start()
        return carry

    lax.fori_loop(0, count, send, 0)
    pltpu.make_async_copy(off_ref, off_ref, sem).wait()
    labels.wait()


def pack(off, to_plane, to_slot, labels, slots):
    count, edge, _ = off.shape
    planes, tail, _ = labels.shape
    return pl.pallas_call(
        pack_kernel,
        out_shape=jax.ShapeDtypeStruct((planes, slots * edge + tail, edge), off.dtype),
        grid_spec=pltpu.PrefetchScalarGridSpec(
            num_scalar_prefetch=2,
            grid=(),
            in_specs=[pl.BlockSpec(memory_space=pl.ANY), pl.BlockSpec(memory_space=pl.ANY)],
            out_specs=pl.BlockSpec(memory_space=pl.ANY),
            scratch_shapes=[pltpu.SemaphoreType.DMA, pltpu.SemaphoreType.DMA],
        ),
        compiler_params=params(),
        name="pack",
    )(to_plane, to_slot, off, labels)


def mirror_kernel(shift, most, row_ref, col_ref, block_ref, omega_ref, out_ref, total):
    source = pl.program_id(0)
    edge = block_ref.shape[2]

    @pl.when(source == 0)
    def _():
        total[...] = jnp.zeros_like(total)

    def one(m, carry):
        row = row_ref[source, shift * most + m]
        col = col_ref[source, shift * most + m]

        @pl.when(row >= 0)
        def _():
            block = block_ref[0, pl.ds(pl.multiple_of(m * edge, edge), edge), :]
            omega = omega_ref[0, pl.ds(pl.multiple_of(row * edge, edge), edge), :]
            total[col] += dot(block, omega, ((0,), (0,)))

        return carry

    lax.fori_loop(0, most, one, 0)

    @pl.when(source == pl.num_programs(0) - 1)
    def _():
        out_ref[...] = total[...].reshape(out_ref.shape).astype(out_ref.dtype)


def mirror_sum(blocks, omegas, rows, cols, shift, most, block_rows, dtype):
    planes, _, edge = blocks.shape
    _, height, columns = omegas.shape
    return pl.pallas_call(
        functools.partial(mirror_kernel, shift, most),
        out_shape=jax.ShapeDtypeStruct((height, columns), dtype),
        grid_spec=pltpu.PrefetchScalarGridSpec(
            num_scalar_prefetch=2,
            grid=(planes,),
            in_specs=[
                pl.BlockSpec((1, most * edge, edge), lambda p, *_: (p, shift, 0)),
                pl.BlockSpec((1, height, columns), lambda p, *_: (p, 0, 0)),
            ],
            out_specs=pl.BlockSpec((height, columns), lambda p, *_: (0, 0)),
            scratch_shapes=[pltpu.VMEM((block_rows, edge, columns), jnp.float32)],
        ),
        compiler_params=params(),
        cost_estimate=pl.CostEstimate(
            flops=2 * planes * most * edge * edge * columns,
            bytes_accessed=planes * (most * edge * edge + height * columns) * 2,
            transcendentals=0,
        ),
        name="mirror",
    )(rows, cols, blocks, omegas)


def far_kernel(most, row_ref, col_ref, block_ref, *rest):
    *omega_refs, out_ref, total = rest
    source = pl.program_id(0)
    edge = block_ref.shape[2]
    total[...] = jnp.zeros_like(total)
    for shift, omega_ref in enumerate(omega_refs):

        def one(m, carry, shift=shift, omega_ref=omega_ref):
            slot = shift * most + m
            row = row_ref[source, slot]
            col = col_ref[source, slot]

            @pl.when(row >= 0)
            def _():
                block = block_ref[0, pl.ds(pl.multiple_of(slot * edge, edge), edge), :]
                omega = omega_ref[pl.ds(pl.multiple_of(col * edge, edge), edge), :]
                total[row] += dot(block, omega)

            return carry

        lax.fori_loop(0, most, one, 0)
    out_ref[0] = total[...].reshape(out_ref.shape[1:]).astype(out_ref.dtype)


def far_sum(blocks, omegas, rows, cols, most, block_rows):
    planes, length, edge = blocks.shape
    height, columns = omegas[0].shape
    return pl.pallas_call(
        functools.partial(far_kernel, most),
        out_shape=jax.ShapeDtypeStruct((planes, height, columns), jnp.bfloat16),
        grid_spec=pltpu.PrefetchScalarGridSpec(
            num_scalar_prefetch=2,
            grid=(planes,),
            in_specs=[pl.BlockSpec((1, length, edge), lambda p, *_: (p, 0, 0))]
            + [pl.BlockSpec((height, columns), lambda p, *_: (0, 0))] * len(omegas),
            out_specs=pl.BlockSpec((1, height, columns), lambda p, *_: (p, 0, 0)),
            scratch_shapes=[pltpu.VMEM((block_rows, edge, columns), jnp.float32)],
        ),
        compiler_params=params(),
        cost_estimate=pl.CostEstimate(
            flops=2 * planes * length * edge * columns,
            bytes_accessed=planes * (length * edge + height * columns) * 2,
            transcendentals=0,
        ),
        name="far",
    )(rows, cols, blocks, *omegas)


def image_kernel(scale, diag_ref, omega_ref, far_ref, own_ref, *rest):
    *mirror_refs, image_ref, gram_ref = rest
    image = dot(diag_ref[0], omega_ref[...]) + own_ref[...]
    for source in range(far_ref.shape[0]):
        image += far_ref[source].astype(jnp.float32)
    for mirror_ref in mirror_refs:
        image += mirror_ref[...].astype(jnp.float32)
    image_ref[...] = image

    @pl.when(pl.program_id(0) == 0)
    def _():
        gram_ref[...] = jnp.zeros_like(gram_ref)

    gram_ref[...] += dot(image, image, ((0,), (0,)), lax.Precision.HIGHEST) * scale


def image_and_gram(diag, sketch, far, own, mirrors, total_rows):
    block_rows, edge, _ = diag.shape
    planes, height, columns = far.shape
    rows = pl.BlockSpec((edge, columns), lambda b: (b, 0))
    return pl.pallas_call(
        functools.partial(image_kernel, 1.0 / total_rows),
        out_shape=(
            jax.ShapeDtypeStruct((height, columns), jnp.float32),
            jax.ShapeDtypeStruct((columns, columns), jnp.float32),
        ),
        grid=(block_rows,),
        in_specs=[
            pl.BlockSpec((1, edge, edge), lambda b: (b, 0, 0)),
            rows,
            pl.BlockSpec((planes, edge, columns), lambda b: (0, b, 0)),
            rows,
        ]
        + [rows] * len(mirrors),
        out_specs=(rows, pl.BlockSpec((columns, columns), lambda b: (0, 0))),
        compiler_params=params(),
        name="image",
    )(diag, sketch, far, own, *mirrors)


def sum_over_devices(part, peers):
    rows, columns = part.shape
    pieces = lax.all_to_all(part.reshape(peers, rows // peers, columns), ALL, 0, 0, tiled=True)
    mine = jnp.broadcast_to(jnp.sum(pieces, axis=0), pieces.shape)
    return lax.all_to_all(mine, ALL, 0, 0, tiled=True).reshape(rows, columns)


def on_device(diag_blocks, off_blocks, col_blocks, sketch):
    block_rows, per_row = col_blocks.shape
    edge = diag_blocks.shape[1]
    layers = lax.axis_size(LINE)
    planes = lax.axis_size(PLANE)
    peers = layers * planes
    requests = block_rows * per_row
    most = max(2, (2 * requests + peers - 1) // peers)
    slots = layers * most
    layer = lax.axis_index(LINE)

    flat = col_blocks.reshape(requests)
    owners = flat // block_rows
    order = jnp.arange(requests)
    earlier = (owners[:, None] == owners[None, :]) & (order[None, :] < order[:, None])
    ranks = jnp.sum(earlier.astype(jnp.int32), axis=1)
    to_plane = owners % planes
    to_slot = lax.rem(owners // planes - layer + layers, layers) * most + ranks
    place = to_plane * slots + to_slot
    hit = place[:, None] == jnp.arange(planes * slots)[None, :]
    row_label = jnp.sum(jnp.where(hit, (order // per_row + 1)[:, None], 0), axis=0) - 1
    col_label = jnp.sum(jnp.where(hit, (flat % block_rows)[:, None], 0), axis=0)
    labels = jnp.stack([row_label.reshape(planes, slots), col_label.reshape(planes, slots)], axis=1)
    labels = jnp.pad(labels, ((0, 0), (0, TAIL - 2), (0, edge - slots))).astype(jnp.bfloat16)
    outgoing = pack(off_blocks.reshape(requests, edge, edge), to_plane, to_slot, labels, slots)

    blocks = lax.all_to_all(outgoing, PLANE, 0, 0, tiled=True)
    plane_omegas = lax.all_gather(sketch, PLANE)
    line_omegas = [sketch]
    for shift in range(1, layers):
        steps = [(z, (z - shift) % layers) for z in range(layers)]
        line_omegas.append(lax.ppermute(sketch, LINE, steps))
    rows = blocks[:, slots * edge, :slots].astype(jnp.int32)
    cols = blocks[:, slots * edge + 1, :slots].astype(jnp.int32)

    mirrors = []
    for shift in range(1, layers):
        part = mirror_sum(
            blocks, plane_omegas, rows, cols, shift, most, block_rows, jnp.bfloat16
        )
        steps = [(z, (z + shift) % layers) for z in range(layers)]
        mirrors.append(lax.ppermute(part, LINE, steps))
    far = far_sum(blocks, line_omegas, rows, cols, most, block_rows)
    far = lax.all_to_all(far, PLANE, 0, 0, tiled=True)
    own = mirror_sum(blocks, plane_omegas, rows, cols, 0, most, block_rows, jnp.float32)

    image, part = image_and_gram(
        diag_blocks, sketch, far, own, mirrors, block_rows * edge * peers
    )
    gram = sum_over_devices(part, peers)
    lower = jnp.linalg.cholesky(gram)
    basis = lax.linalg.triangular_solve(lower, image, left_side=False, lower=True, transpose_a=True)
    return basis, lower.T


def solution(mesh):
    rows, sub = mesh.devices.shape
    layers, cores = math.gcd(rows, 4), math.gcd(sub, 2)
    devices = mesh.devices.reshape(layers, rows // layers, sub // cores, cores)
    placed = (P(ALL, None, None), P(ALL, None, None, None), P(ALL, None), P(ALL, None))
    return jax.shard_map(
        on_device,
        mesh=Mesh(devices, ALL),
        in_specs=placed,
        out_specs=(P(ALL, None), P()),
        check_vma=False,
    )
```

```python
import functools
import math

import jax
import jax.numpy as jnp
from jax import lax
from jax.experimental import pallas as pl
from jax.experimental.pallas import tpu as pltpu
from jax.sharding import Mesh
from jax.sharding import PartitionSpec as P

LINE = "z"
PLANE = ("x", "y", "c")
ALL = (LINE,) + PLANE
VMEM_LIMIT = 48 * 1024 * 1024
TAIL = 16


def dot(a, b, contract=((1,), (0,)), precision=None):
    return lax.dot_general(
        a, b, (contract, ((), ())), precision=precision, preferred_element_type=jnp.float32
    )


NT = ((1,), (1,))
TN = ((0,), (0,))


def params():
    return pltpu.CompilerParams(vmem_limit_bytes=VMEM_LIMIT)


def split(a):
    high = a.astype(jnp.bfloat16)
    return high, (a - high.astype(jnp.float32)).astype(jnp.bfloat16)

def dot3(a, b, contract=((1,), (0,))):
    (ah, al), (bh, bl) = a, b
    return dot(ah, bh, contract) + (dot(ah, bl, contract) + dot(al, bh, contract))

def pack_kernel(plane_ref, slot_ref, off_ref, label_ref, out_ref, sem, label_sem):
    count, edge, _ = off_ref.shape
    tail = label_ref.shape[1]
    last = out_ref.shape[1] - tail
    labels = pltpu.make_async_copy(label_ref, out_ref.at[:, pl.ds(last, tail), :], label_sem)
    labels.start()

    def send(entry, carry):
        row = pl.multiple_of(slot_ref[entry] * edge, edge)
        pltpu.make_async_copy(
            off_ref.at[entry], out_ref.at[plane_ref[entry], pl.ds(row, edge), :], sem
        ).start()
        return carry

    lax.fori_loop(0, count, send, 0)
    pltpu.make_async_copy(off_ref, off_ref, sem).wait()
    labels.wait()


def pack(off, to_plane, to_slot, labels, slots):
    count, edge, _ = off.shape
    planes, tail, _ = labels.shape
    return pl.pallas_call(
        pack_kernel,
        out_shape=jax.ShapeDtypeStruct((planes, slots * edge + tail, edge), off.dtype),
        grid_spec=pltpu.PrefetchScalarGridSpec(
            num_scalar_prefetch=2,
            grid=(),
            in_specs=[pl.BlockSpec(memory_space=pl.ANY), pl.BlockSpec(memory_space=pl.ANY)],
            out_specs=pl.BlockSpec(memory_space=pl.ANY),
            scratch_shapes=[pltpu.SemaphoreType.DMA, pltpu.SemaphoreType.DMA],
        ),
        compiler_params=params(),
        name="pack",
    )(to_plane, to_slot, off, labels)


def mirror_kernel(shift, most, row_ref, col_ref, block_ref, omega_ref, out_ref, total):
    source = pl.program_id(0)
    edge = block_ref.shape[2]
    spare = total.shape[0] - 1

    @pl.when(source == 0)
    def _():
        total[...] = jnp.zeros_like(total)

    for m in range(most):
        row = jnp.minimum(row_ref[source, shift * most + m], spare - 1)
        col = col_ref[source, shift * most + m]
        block = block_ref[0, m * edge : (m + 1) * edge, :]
        omega = omega_ref[0, pl.ds(pl.multiple_of(row * edge, edge), edge), :]
        product = dot(block, omega, ((0,), (0,))).astype(jnp.bfloat16)
        total[col] += product.astype(jnp.float32)

    @pl.when(source == pl.num_programs(0) - 1)
    def _():
        out_ref[...] = total[:spare].reshape(out_ref.shape).astype(out_ref.dtype)


def mirror_sum(blocks, omegas, rows, cols, shift, most, block_rows, dtype):
    planes, _, edge = blocks.shape
    _, height, columns = omegas.shape
    return pl.pallas_call(
        functools.partial(mirror_kernel, shift, most),
        out_shape=jax.ShapeDtypeStruct((height, columns), dtype),
        grid_spec=pltpu.PrefetchScalarGridSpec(
            num_scalar_prefetch=2,
            grid=(planes,),
            in_specs=[
                pl.BlockSpec((1, most * edge, edge), lambda p, *_: (p, shift, 0)),
                pl.BlockSpec((1, height, columns), lambda p, *_: (p, 0, 0)),
            ],
            out_specs=pl.BlockSpec((height, columns), lambda p, *_: (0, 0)),
            scratch_shapes=[pltpu.VMEM((block_rows + 1, edge, columns), jnp.float32)],
        ),
        compiler_params=params(),
        cost_estimate=pl.CostEstimate(
            flops=2 * planes * most * edge * edge * columns,
            bytes_accessed=planes * (most * edge * edge + height * columns) * 2,
            transcendentals=0,
        ),
        name="mirror",
    )(rows, cols, blocks, omegas)


def far_kernel(most, row_ref, col_ref, block_ref, *rest):
    *omega_refs, out_ref, total = rest
    source = pl.program_id(0)
    edge = block_ref.shape[2]
    spare = total.shape[0] - 1
    total[...] = jnp.zeros_like(total)
    for shift, omega_ref in enumerate(omega_refs):
        for slot in range(shift * most, (shift + 1) * most):
            row = row_ref[source, slot]
            col = jnp.minimum(col_ref[source, slot], spare - 1)
            block = block_ref[0, slot * edge : (slot + 1) * edge, :]
            omega = omega_ref[pl.ds(pl.multiple_of(col * edge, edge), edge), :]
            total[row] += dot(block, omega)
    out_ref[0] = total[:spare].reshape(out_ref.shape[1:]).astype(out_ref.dtype)


def far_sum(blocks, omegas, rows, cols, most, block_rows):
    planes, length, edge = blocks.shape
    height, columns = omegas[0].shape
    return pl.pallas_call(
        functools.partial(far_kernel, most),
        out_shape=jax.ShapeDtypeStruct((planes, height, columns), jnp.bfloat16),
        grid_spec=pltpu.PrefetchScalarGridSpec(
            num_scalar_prefetch=2,
            grid=(planes,),
            in_specs=[pl.BlockSpec((1, length, edge), lambda p, *_: (p, 0, 0))]
            + [pl.BlockSpec((height, columns), lambda p, *_: (0, 0))] * len(omegas),
            out_specs=pl.BlockSpec((1, height, columns), lambda p, *_: (p, 0, 0)),
            scratch_shapes=[pltpu.VMEM((block_rows + 1, edge, columns), jnp.float32)],
        ),
        compiler_params=params(),
        cost_estimate=pl.CostEstimate(
            flops=2 * planes * length * edge * columns,
            bytes_accessed=planes * (length * edge + height * columns) * 2,
            transcendentals=0,
        ),
        name="far",
    )(rows, cols, blocks, *omegas)


def image_kernel(scale, diag_ref, omega_ref, far_ref, own_ref, *rest):
    *mirror_refs, image_ref, gram_ref, cross = rest
    step = pl.program_id(0)
    edge = diag_ref.shape[1]
    near = [
        dot(diag_ref[b], omega_ref[b * edge : (b + 1) * edge, :]) for b in range(diag_ref.shape[0])
    ]
    image = jnp.concatenate(near, axis=0) + own_ref[...]
    for source in range(far_ref.shape[0]):
        image += far_ref[source].astype(jnp.float32)
    for mirror_ref in mirror_refs:
        image += mirror_ref[...].astype(jnp.float32)
    image_ref[...] = image

    @pl.when(step == 0)
    def _():
        gram_ref[...] = jnp.zeros_like(gram_ref)
        cross[...] = jnp.zeros_like(cross)

    high, low = split(image)
    gram_ref[...] += dot(high, high, TN)
    cross[...] += dot(high, low, TN)

    @pl.when(step == pl.num_programs(0) - 1)
    def _():
        gram_ref[...] = (gram_ref[...] + (cross[...] + cross[...].T)) * scale


def image_and_gram(diag, sketch, far, own, mirrors, total_rows):
    block_rows, edge, _ = diag.shape
    planes, height, columns = far.shape
    together = math.gcd(block_rows, 2)
    rows = pl.BlockSpec((together * edge, columns), lambda b: (b, 0))
    return pl.pallas_call(
        functools.partial(image_kernel, 1.0 / total_rows),
        out_shape=(
            jax.ShapeDtypeStruct((height, columns), jnp.float32),
            jax.ShapeDtypeStruct((columns, columns), jnp.float32),
        ),
        grid=(block_rows // together,),
        in_specs=[
            pl.BlockSpec((together, edge, edge), lambda b: (b, 0, 0)),
            rows,
            pl.BlockSpec((planes, together * edge, columns), lambda b: (0, b, 0)),
            rows,
        ]
        + [rows] * len(mirrors),
        out_specs=(rows, pl.BlockSpec((columns, columns), lambda b: (0, 0))),
        scratch_shapes=[pltpu.VMEM((columns, columns), jnp.float32)],
        compiler_params=params(),
        name="image",
    )(diag, sketch, far, own, *mirrors)


def factor_kernel(rounds, gram_ref, image_ref, basis_ref, factor_ref, inverse, work):
    n = gram_ref.shape[0]
    exact = lax.Precision.HIGHEST

    @pl.when(pl.program_id(0) == 0)
    def _():
        gram = gram_ref[...]
        row = lax.broadcasted_iota(jnp.int32, (n, n), 0)
        col = lax.broadcasted_iota(jnp.int32, (n, n), 1)
        weight = jnp.where(row > col, 1.0, jnp.where(row == col, 0.5, 0.0))
        one = jnp.where(row == col, 1.0, 0.0)
        diagonal = jnp.where(row == col, gram, 0.0)
        down = lax.rsqrt(jnp.sum(diagonal, axis=1, keepdims=True))
        across = lax.rsqrt(jnp.sum(diagonal, axis=0, keepdims=True))
        scaled = gram * down * across
        step = one - weight * (scaled - one)
        guess = step
        for turn in range(rounds):
            if turn == rounds - 1:
                error = dot(dot(guess, scaled, precision=exact), guess, NT, precision=exact) - one
                step = weight * error
                guess = guess - dot(step, guess, precision=exact)
            else:
                g3 = split(guess)
                error = dot3(split(dot3(g3, split(scaled))), g3, NT) - one
                guess = guess - dot3(split(weight * error), g3)
        guess = jnp.where(row >= col, guess, 0.0)
        inverse[...] = guess * across
        factor_ref[...] = jnp.where(row <= col, dot(inverse[...], gram, precision=exact), 0.0)
        size = jnp.sum(error * error)

        @pl.when(jnp.logical_not(size < 1e-6))
        def _():
            work[...] = gram
            inverse[...] = one
            lane = lax.broadcasted_iota(jnp.int32, (1, n), 1)

            def eliminate(j, carry):
                line = work[pl.ds(j, 1), :]
                pivot = jnp.sum(jnp.where(lane == j, line, 0.0), axis=1, keepdims=True)
                scale = lax.rsqrt(pivot)
                line = jnp.where(lane >= j, line * scale, 0.0)
                other = inverse[pl.ds(j, 1), :] * scale
                below = jnp.where(lane > j, line, 0.0)
                work[...] -= dot(below, line, TN, exact)
                inverse[...] -= dot(below, other, TN, exact)
                inverse[pl.ds(j, 1), :] = other
                factor_ref[pl.ds(j, 1), :] = line
                return carry

            lax.fori_loop(0, n, eliminate, 0)

    basis_ref[...] = dot3(split(image_ref[...]), split(inverse[...]), NT)

def factor_and_basis(gram, image, tile=256, rounds=3):
    height, n = image.shape
    whole = pl.BlockSpec((n, n), lambda b: (0, 0))
    tiles = pl.BlockSpec((tile, n), lambda b: (b, 0))
    return pl.pallas_call(
        functools.partial(factor_kernel, rounds),
        out_shape=(jax.ShapeDtypeStruct((height, n), jnp.float32), jax.ShapeDtypeStruct((n, n), jnp.float32)),
        grid=(height // tile,),
        in_specs=[whole, tiles],
        out_specs=(tiles, whole),
        scratch_shapes=[pltpu.VMEM((n, n), jnp.float32)] * 2,
        compiler_params=params(),
        name="factor",
    )(gram, image)


def sum_over_devices(part, peers):
    rows, columns = part.shape
    pieces = lax.all_to_all(part.reshape(peers, rows // peers, columns), ALL, 0, 0, tiled=True)
    mine = jnp.broadcast_to(jnp.sum(pieces, axis=0), pieces.shape)
    return lax.all_to_all(mine, ALL, 0, 0, tiled=True).reshape(rows, columns)


def on_device(diag_blocks, off_blocks, col_blocks, sketch):
    block_rows, per_row = col_blocks.shape
    edge = diag_blocks.shape[1]
    layers = lax.axis_size(LINE)
    planes = lax.axis_size(PLANE)
    peers = layers * planes
    requests = block_rows * per_row
    most = max(2, (2 * requests + peers - 1) // peers)
    slots = layers * most
    layer = lax.axis_index(LINE)

    flat = col_blocks.reshape(requests)
    owners = flat // block_rows
    order = jnp.arange(requests)
    earlier = (owners[:, None] == owners[None, :]) & (order[None, :] < order[:, None])
    ranks = jnp.sum(earlier.astype(jnp.int32), axis=1)
    to_plane = owners % planes
    to_slot = lax.rem(owners // planes - layer + layers, layers) * most + ranks
    place = to_plane * slots + to_slot
    hit = place[:, None] == jnp.arange(planes * slots)[None, :]
    row_label = block_rows + jnp.sum(
        jnp.where(hit, (order // per_row - block_rows)[:, None], 0), axis=0
    )
    col_label = block_rows + jnp.sum(
        jnp.where(hit, (flat % block_rows - block_rows)[:, None], 0), axis=0
    )
    labels = jnp.stack([row_label.reshape(planes, slots), col_label.reshape(planes, slots)], axis=1)
    labels = jnp.pad(labels, ((0, 0), (0, TAIL - 2), (0, edge - slots))).astype(jnp.bfloat16)
    outgoing = pack(off_blocks.reshape(requests, edge, edge), to_plane, to_slot, labels, slots)

    blocks = lax.all_to_all(outgoing, PLANE, 0, 0, tiled=True)
    plane_omegas = lax.all_gather(sketch, PLANE)
    line_omegas = [sketch]
    for shift in range(1, layers):
        steps = [(z, (z - shift) % layers) for z in range(layers)]
        line_omegas.append(lax.ppermute(sketch, LINE, steps))
    rows = blocks[:, slots * edge, :slots].astype(jnp.int32)
    cols = blocks[:, slots * edge + 1, :slots].astype(jnp.int32)

    mirrors = []
    for shift in range(1, layers):
        part = mirror_sum(
            blocks, plane_omegas, rows, cols, shift, most, block_rows, jnp.bfloat16
        )
        steps = [(z, (z + shift) % layers) for z in range(layers)]
        mirrors.append(lax.ppermute(part, LINE, steps))
    far = far_sum(blocks, line_omegas, rows, cols, most, block_rows)
    far = lax.all_to_all(far, PLANE, 0, 0, tiled=True)
    own = mirror_sum(blocks, plane_omegas, rows, cols, 0, most, block_rows, jnp.float32)

    image, part = image_and_gram(
        diag_blocks, sketch, far, own, mirrors, block_rows * edge * peers
    )
    gram = sum_over_devices(part, peers)
    return factor_and_basis(gram, image)


def solution(mesh):
    rows, sub = mesh.devices.shape
    layers, cores = math.gcd(rows, 4), math.gcd(sub, 2)
    devices = mesh.devices.reshape(layers, rows // layers, sub // cores, cores)
    placed = (P(ALL, None, None), P(ALL, None, None, None), P(ALL, None), P(ALL, None))
    return jax.shard_map(
        on_device,
        mesh=Mesh(devices, ALL),
        in_specs=placed,
        out_specs=(P(ALL, None), P()),
        check_vma=False,
    )
```

```python
import functools
import math

import jax
import jax.numpy as jnp
from jax import lax
from jax.experimental import pallas as pl
from jax.experimental.pallas import tpu as pltpu
from jax.sharding import Mesh
from jax.sharding import PartitionSpec as P

LINE = "z"
PLANE = ("x", "y", "c")
ALL = (LINE,) + PLANE
CHIPS, CORE = PLANE[:2], PLANE[2]
VMEM_LIMIT = 48 * 1024 * 1024
COST = pl.CostEstimate(flops=10**12, bytes_accessed=10**11, transcendentals=0)
TAIL = 16


def dot(a, b, contract=((1,), (0,)), precision=None):
    return lax.dot_general(
        a, b, (contract, ((), ())), precision=precision, preferred_element_type=jnp.float32
    )


NT = ((1,), (1,))
TN = ((0,), (0,))


def params():
    return pltpu.CompilerParams(vmem_limit_bytes=VMEM_LIMIT)


def split(a):
    high = a.astype(jnp.bfloat16)
    return high, (a - high.astype(jnp.float32)).astype(jnp.bfloat16)

def dot3(a, b, contract=((1,), (0,))):
    (ah, al), (bh, bl) = a, b
    return dot(ah, bh, contract) + (dot(ah, bl, contract) + dot(al, bh, contract))

def pack_kernel(entry_ref, plane_ref, slot_ref, count_ref, off_ref, label_ref, *rest):
    *out_refs, sem, label_sem = rest
    _, edge, _ = off_ref.shape
    tail = label_ref.shape[1]
    first = out_refs[0]
    labels = pltpu.make_async_copy(
        label_ref, first.at[:, pl.ds(first.shape[1] - tail, tail), :], label_sem
    )
    labels.start()
    for part, out_ref in enumerate(out_refs):

        def send(place, carry, out_ref=out_ref):
            row = pl.multiple_of(slot_ref[place] * edge, edge)
            pltpu.make_async_copy(
                off_ref.at[entry_ref[place]], out_ref.at[plane_ref[place], pl.ds(row, edge), :], sem
            ).start()
            return carry

        lax.fori_loop(count_ref[part], count_ref[part + 1], send, 0)
    pltpu.make_async_copy(off_ref, off_ref, sem).wait()
    labels.wait()


def pack(off, route, labels, parts):
    count, edge, _ = off.shape
    planes, tail, _ = labels.shape
    lengths = [slots * edge + (tail if index == 0 else 0) for index, slots in enumerate(parts)]
    anywhere = pl.BlockSpec(memory_space=pl.ANY)
    return pl.pallas_call(
        pack_kernel,
        out_shape=[jax.ShapeDtypeStruct((planes, length, edge), off.dtype) for length in lengths],
        grid_spec=pltpu.PrefetchScalarGridSpec(
            num_scalar_prefetch=len(route),
            grid=(),
            in_specs=[pl.BlockSpec(memory_space=pltpu.VMEM), anywhere],
            out_specs=[anywhere] * len(parts),
            scratch_shapes=[pltpu.SemaphoreType.DMA, pltpu.SemaphoreType.DMA],
        ),
        compiler_params=params(),
        cost_estimate=COST,
        name="pack",
    )(*route, off, labels)


def hold_kernel(x_ref, *rest):
    del x_ref, rest


def hold(x, after):
    anywhere = pl.BlockSpec(memory_space=pl.ANY)
    return pl.pallas_call(
        hold_kernel,
        out_shape=jax.ShapeDtypeStruct(x.shape, x.dtype),
        in_specs=[anywhere] * (1 + len(after)),
        out_specs=anywhere,
        input_output_aliases={0: 0},
        cost_estimate=COST,
        name="hold",
    )(x, *after)


def mirror_kernel(begin, most, row_ref, col_ref, block_ref, omega_ref, *rest):
    out_ref, total = rest[-2:]
    source = pl.program_id(0)
    edge = block_ref.shape[2]
    spare = total.shape[0] - 1

    @pl.when(source == 0)
    def _():
        total[...] = jnp.zeros_like(total)

    for m in range(most):
        row = jnp.minimum(row_ref[source, begin + m], spare - 1)
        col = col_ref[source, begin + m]
        block = block_ref[0, m * edge : (m + 1) * edge, :]
        omega = omega_ref[0, pl.ds(pl.multiple_of(row * edge, edge), edge), :]
        product = dot(block, omega, ((0,), (0,))).astype(jnp.bfloat16)
        total[col] += product.astype(jnp.float32)

    @pl.when(source == pl.num_programs(0) - 1)
    def _():
        out_ref[...] = total[:spare].reshape(out_ref.shape).astype(out_ref.dtype)


def mirror_sum(blocks, omegas, rows, cols, inside, begin, most, block_rows, dtype, after=()):
    planes, _, edge = blocks.shape
    _, height, columns = omegas.shape
    return pl.pallas_call(
        functools.partial(mirror_kernel, begin, most),
        out_shape=jax.ShapeDtypeStruct((height, columns), dtype),
        grid_spec=pltpu.PrefetchScalarGridSpec(
            num_scalar_prefetch=2,
            grid=(planes,),
            in_specs=[
                pl.BlockSpec((1, most * edge, edge), lambda p, *_: (p, inside, 0)),
                pl.BlockSpec((1, height, columns), lambda p, *_: (p, 0, 0)),
            ]
            + [pl.BlockSpec(memory_space=pl.ANY)] * len(after),
            out_specs=pl.BlockSpec((height, columns), lambda p, *_: (0, 0)),
            scratch_shapes=[pltpu.VMEM((block_rows + 1, edge, columns), jnp.float32)],
        ),
        compiler_params=params(),
        cost_estimate=COST,
        name="mirror",
    )(rows, cols, blocks, omegas, *after)


def far_kernel(most, parts, lines, added, source_ref, place_ref, row_ref, col_ref, *rest):
    del place_ref
    part_refs, omega_refs = rest[:parts], rest[parts : parts + lines]
    out_ref, total = rest[-2:]
    source = source_ref[pl.program_id(0)]
    edge = part_refs[0].shape[2]
    spare = total.shape[0] - 1
    if added:
        total[:spare] = rest[parts + lines][0].reshape(spare, edge, -1)
    else:
        total[...] = jnp.zeros_like(total)
    each = len(omega_refs) // parts
    for index, omega_ref in enumerate(omega_refs):
        for m in range(most):
            row = row_ref[source, index * most + m]
            col = jnp.minimum(col_ref[source, index * most + m], spare - 1)
            slot = index % each * most + m
            block = part_refs[index // each][0, slot * edge : (slot + 1) * edge, :]
            omega = omega_ref[pl.ds(pl.multiple_of(col * edge, edge), edge), :]
            total[row] += dot(block, omega)
    out_ref[0] = total[:spare].reshape(out_ref.shape[1:]).astype(out_ref.dtype)


def far_sum(
    sources, places, slots, parts, omegas, rows, cols, most, block_rows, dtype, add=None, after=()
):
    edge = parts[0].shape[2]
    height, columns = omegas[0].shape
    more = [] if add is None else [add]
    return pl.pallas_call(
        functools.partial(far_kernel, most, len(parts), len(omegas), len(more)),
        out_shape=jax.ShapeDtypeStruct((slots, height, columns), dtype),
        grid_spec=pltpu.PrefetchScalarGridSpec(
            num_scalar_prefetch=4,
            grid=sources.shape,
            in_specs=[
                pl.BlockSpec((1, part.shape[1], edge), lambda k, source, *_: (source[k], 0, 0))
                for part in parts
            ]
            + [pl.BlockSpec((height, columns), lambda k, *_: (0, 0))] * len(omegas)
            + [pl.BlockSpec((1, height, columns), lambda k, *_: (k, 0, 0))] * len(more)
            + [pl.BlockSpec(memory_space=pl.ANY)] * len(after),
            out_specs=pl.BlockSpec(
                (1, height, columns), lambda k, source, place, *_: (place[k], 0, 0)
            ),
            scratch_shapes=[pltpu.VMEM((block_rows + 1, edge, columns), jnp.float32)],
        ),
        compiler_params=params(),
        cost_estimate=COST,
        name="far",
    )(sources, places, rows, cols, *parts, *omegas, *more, *after)


def image_kernel(scale, chip_ref, diag_ref, omega_ref, far_ref, *rest):
    *piece_refs, image_ref, gram_ref, cross = rest
    step = pl.program_id(0)
    edge = diag_ref.shape[1]
    near = [
        dot(diag_ref[b], omega_ref[b * edge : (b + 1) * edge, :]) for b in range(diag_ref.shape[0])
    ]
    image = jnp.concatenate(near, axis=0)
    for piece_ref in piece_refs:
        image += piece_ref[...].astype(jnp.float32)
    for chip in range(far_ref.shape[0]):
        piece = far_ref[chip].astype(jnp.float32)
        image += jnp.where(chip == chip_ref[0], 0.0, piece)
    image_ref[...] = image

    @pl.when(step == 0)
    def _():
        gram_ref[...] = jnp.zeros_like(gram_ref)
        cross[...] = jnp.zeros_like(cross)

    high, low = split(image)
    gram_ref[...] += dot(high, high, TN)
    cross[...] += dot(high, low, TN)

    @pl.when(step == pl.num_programs(0) - 1)
    def _():
        gram_ref[...] = (gram_ref[...] + (cross[...] + cross[...].T)) * scale


def image_and_gram(diag, sketch, chip, far, pieces, total_rows):
    block_rows, edge, _ = diag.shape
    height, columns = sketch.shape
    together = math.gcd(block_rows, 2)
    rows = pl.BlockSpec((together * edge, columns), lambda b, _: (b, 0))
    return pl.pallas_call(
        functools.partial(image_kernel, 1.0 / total_rows),
        out_shape=(
            jax.ShapeDtypeStruct((height, columns), jnp.float32),
            jax.ShapeDtypeStruct((columns, columns), jnp.float32),
        ),
        grid_spec=pltpu.PrefetchScalarGridSpec(
            num_scalar_prefetch=1,
            grid=(block_rows // together,),
            in_specs=[
                pl.BlockSpec((together, edge, edge), lambda b, _: (b, 0, 0)),
                rows,
                pl.BlockSpec((far.shape[0], together * edge, columns), lambda b, _: (0, b, 0)),
            ]
            + [rows] * len(pieces),
            out_specs=(rows, pl.BlockSpec((columns, columns), lambda b, _: (0, 0))),
            scratch_shapes=[pltpu.VMEM((columns, columns), jnp.float32)],
        ),
        compiler_params=params(),
        cost_estimate=COST,
        name="image",
    )(chip.reshape(1), diag, sketch, far, *pieces)


def factor_kernel(rounds, gram_ref, image_ref, basis_ref, factor_ref, inverse, work):
    n = gram_ref.shape[0]
    exact = lax.Precision.HIGHEST

    @pl.when(pl.program_id(0) == 0)
    def _():
        gram = gram_ref[...]
        row = lax.broadcasted_iota(jnp.int32, (n, n), 0)
        col = lax.broadcasted_iota(jnp.int32, (n, n), 1)
        weight = jnp.where(row > col, 1.0, jnp.where(row == col, 0.5, 0.0))
        one = jnp.where(row == col, 1.0, 0.0)
        diagonal = jnp.where(row == col, gram, 0.0)
        down = lax.rsqrt(jnp.sum(diagonal, axis=1, keepdims=True))
        across = lax.rsqrt(jnp.sum(diagonal, axis=0, keepdims=True))
        scaled = gram * down * across
        step = one - weight * (scaled - one)
        guess = step
        for turn in range(rounds):
            if turn == rounds - 1:
                error = dot(dot(guess, scaled, precision=exact), guess, NT, precision=exact) - one
                step = weight * error
                guess = guess - dot(step, guess, precision=exact)
            else:
                g3 = split(guess)
                error = dot3(split(dot3(g3, split(scaled))), g3, NT) - one
                guess = guess - dot3(split(weight * error), g3)
        guess = jnp.where(row >= col, guess, 0.0)
        inverse[...] = guess * across
        factor_ref[...] = jnp.where(row <= col, dot(inverse[...], gram, precision=exact), 0.0)
        size = jnp.sum(error * error)

        @pl.when(jnp.logical_not(size < 1e-6))
        def _():
            work[...] = gram
            inverse[...] = one
            lane = lax.broadcasted_iota(jnp.int32, (1, n), 1)

            def eliminate(j, carry):
                line = work[pl.ds(j, 1), :]
                pivot = jnp.sum(jnp.where(lane == j, line, 0.0), axis=1, keepdims=True)
                scale = lax.rsqrt(pivot)
                line = jnp.where(lane >= j, line * scale, 0.0)
                other = inverse[pl.ds(j, 1), :] * scale
                below = jnp.where(lane > j, line, 0.0)
                work[...] -= dot(below, line, TN, exact)
                inverse[...] -= dot(below, other, TN, exact)
                inverse[pl.ds(j, 1), :] = other
                factor_ref[pl.ds(j, 1), :] = line
                return carry

            lax.fori_loop(0, n, eliminate, 0)

    basis_ref[...] = dot3(split(image_ref[...]), split(inverse[...]), NT)

def factor_and_basis(gram, image, tile=256, rounds=3):
    height, n = image.shape
    whole = pl.BlockSpec((n, n), lambda b: (0, 0))
    tiles = pl.BlockSpec((tile, n), lambda b: (b, 0))
    return pl.pallas_call(
        functools.partial(factor_kernel, rounds),
        out_shape=(jax.ShapeDtypeStruct((height, n), jnp.float32), jax.ShapeDtypeStruct((n, n), jnp.float32)),
        grid=(height // tile,),
        in_specs=[whole, tiles],
        out_specs=(tiles, whole),
        scratch_shapes=[pltpu.VMEM((n, n), jnp.float32)] * 2,
        compiler_params=params(),
        name="factor",
    )(gram, image)


def sum_over_devices(part, peers):
    rows, columns = part.shape
    pieces = lax.all_to_all(part.reshape(peers, rows // peers, columns), ALL, 0, 0, tiled=True)
    mine = jnp.broadcast_to(jnp.sum(pieces, axis=0), pieces.shape)
    return lax.all_to_all(mine, ALL, 0, 0, tiled=True).reshape(rows, columns)


def on_device(diag_blocks, off_blocks, col_blocks, sketch):
    block_rows, per_row = col_blocks.shape
    edge = diag_blocks.shape[1]
    layers = lax.axis_size(LINE)
    planes = lax.axis_size(PLANE)
    peers = layers * planes
    requests = block_rows * per_row
    most = max(2, (2 * requests + peers - 1) // peers)
    slots = layers * most
    layer = lax.axis_index(LINE)
    shifts = sorted(range(layers), key=lambda shift: -min(shift, layers - shift))
    halves = math.gcd(layers, 2)

    flat = col_blocks.reshape(requests)
    owners = flat // block_rows
    order = jnp.arange(requests)
    earlier = (owners[:, None] == owners[None, :]) & (order[None, :] < order[:, None])
    ranks = jnp.sum(earlier.astype(jnp.int32), axis=1)
    to_plane = owners % planes
    away = lax.rem(owners // planes - layer + layers, layers)
    turn = sum(jnp.where(away == shift, index, 0) for index, shift in enumerate(shifts))
    to_slot = turn * most + ranks
    place = to_plane * slots + to_slot
    hit = place[:, None] == jnp.arange(planes * slots)[None, :]
    row_label = block_rows + jnp.sum(
        jnp.where(hit, (order // per_row - block_rows)[:, None], 0), axis=0
    )
    col_label = block_rows + jnp.sum(
        jnp.where(hit, (flat % block_rows - block_rows)[:, None], 0), axis=0
    )
    labels = jnp.stack([row_label.reshape(planes, slots), col_label.reshape(planes, slots)], axis=1)
    labels = jnp.pad(labels, ((0, 0), (0, TAIL - 2), (0, edge - slots))).astype(jnp.bfloat16)
    in_part = to_slot // (slots // halves)
    before = jnp.sum(
        (in_part[None, :] < in_part[:, None])
        | ((in_part[None, :] == in_part[:, None]) & (order[None, :] < order[:, None])),
        axis=1,
    )
    pick = before[None, :] == order[:, None]
    route = [
        jnp.sum(jnp.where(pick, values[None, :], 0), axis=1)
        for values in (order, to_plane, to_slot % (slots // halves))
    ]
    counts = jnp.sum(in_part[None, :] < jnp.arange(halves + 1)[:, None], axis=1)
    outgoing = pack(
        off_blocks.reshape(requests, edge, edge), route + [counts], labels, [slots // halves] * halves
    )

    plane_omegas = lax.all_gather(sketch, PLANE)
    line_omegas = []
    for shift in shifts:
        steps = [(z, (z - shift) % layers) for z in range(layers)]
        line_omegas.append(lax.ppermute(sketch, LINE, steps) if shift else sketch)
    parts = []
    for part in outgoing:
        part = hold(part, line_omegas) if parts else part
        parts.append(lax.all_to_all(part, PLANE, 0, 0, tiled=True))
    lines = slots // halves * edge
    rows = parts[0][:, lines, :slots].astype(jnp.int32)
    cols = parts[0][:, lines + 1, :slots].astype(jnp.int32)

    pieces = []
    latest = ()

    def send_mirror(index, after):
        part, inside = divmod(index, layers // halves)
        shift = shifts[index]
        kind = jnp.bfloat16 if shift else jnp.float32
        mirror = mirror_sum(
            parts[part], plane_omegas, rows, cols, inside, index * most, most, block_rows, kind, after
        )
        steps = [(z, (z + shift) % layers) for z in range(layers)]
        pieces.append(lax.ppermute(mirror, LINE, steps) if shift else mirror)
        return (mirror,)

    early = layers // halves
    for index in range(early):
        latest = send_mirror(index, latest)

    cores = lax.axis_size(CORE)
    chips = planes // cores
    chip, core = lax.axis_index(CHIPS), lax.axis_index(CORE)
    away = (chip + jnp.arange(1, chips)) % chips
    far = functools.partial(
        far_sum, parts=parts, omegas=line_omegas, rows=rows, cols=cols, most=most, block_rows=block_rows
    )

    def ask(chips_asked, after):
        if cores == 1:
            return None, after
        count = chips_asked.shape[0]
        other = far(
            chips_asked * cores + 1 - core, jnp.arange(count), count, dtype=jnp.float32, after=after
        )
        return lax.ppermute(other, CORE, [(0, 1), (1, 0)]), (other,)

    other, latest = ask(away, latest)
    for index in range(early, layers - 1):
        latest = send_mirror(index, latest)
    sent = far(away * cores + core, away, chips, dtype=jnp.bfloat16, add=other, after=latest)
    received = lax.all_to_all(sent, CHIPS, 0, 0, tiled=True)
    other, latest = ask(chip.reshape(1), (sent,))
    latest = send_mirror(layers - 1, latest)
    own = far(
        chip.reshape(1) * cores + core, jnp.arange(1), 1, dtype=jnp.float32, add=other, after=latest
    )
    pieces.append(own.reshape(sketch.shape))

    image, part = image_and_gram(
        diag_blocks, sketch, chip, received, pieces, block_rows * edge * peers
    )
    gram = sum_over_devices(part, peers)
    return factor_and_basis(gram, image)


def solution(mesh):
    rows, sub = mesh.devices.shape
    layers, cores = math.gcd(rows, 4), math.gcd(sub, 2)
    devices = mesh.devices.reshape(layers, rows // layers, sub // cores, cores)
    placed = (P(ALL, None, None), P(ALL, None, None, None), P(ALL, None), P(ALL, None))
    return jax.shard_map(
        on_device,
        mesh=Mesh(devices, ALL),
        in_specs=placed,
        out_specs=(P(ALL, None), P()),
        check_vma=False,
    )
```

```python
import functools
import math

import jax
import jax.numpy as jnp
from jax import lax
from jax.experimental import pallas as pl
from jax.experimental.pallas import tpu as pltpu
from jax.sharding import Mesh
from jax.sharding import PartitionSpec as P

LINE = "z"
PLANE = ("x", "y", "c")
ALL = (LINE,) + PLANE
CHIPS, CORE = PLANE[:2], PLANE[2]
VMEM_LIMIT = 48 * 1024 * 1024
COST = pl.CostEstimate(flops=10**12, bytes_accessed=10**11, transcendentals=0)
TAIL = 16


def dot(a, b, contract=((1,), (0,)), precision=None):
    return lax.dot_general(
        a, b, (contract, ((), ())), precision=precision, preferred_element_type=jnp.float32
    )


NT = ((1,), (1,))
TN = ((0,), (0,))


def params():
    return pltpu.CompilerParams(vmem_limit_bytes=VMEM_LIMIT)


def split(a):
    high = a.astype(jnp.bfloat16)
    return high, (a - high.astype(jnp.float32)).astype(jnp.bfloat16)

def dot3(a, b, contract=((1,), (0,))):
    (ah, al), (bh, bl) = a, b
    return dot(ah, bh, contract) + (dot(ah, bl, contract) + dot(al, bh, contract))

def pack_kernel(entry_ref, plane_ref, slot_ref, count_ref, off_ref, label_ref, *rest):
    *out_refs, sem, label_sem = rest
    _, edge, _ = off_ref.shape
    tail = label_ref.shape[1]
    first = out_refs[0]
    labels = pltpu.make_async_copy(
        label_ref, first.at[:, pl.ds(first.shape[1] - tail, tail), :], label_sem
    )
    labels.start()
    for part, out_ref in enumerate(out_refs):

        def send(place, carry, out_ref=out_ref):
            row = pl.multiple_of(slot_ref[place] * edge, edge)
            pltpu.make_async_copy(
                off_ref.at[entry_ref[place]], out_ref.at[plane_ref[place], pl.ds(row, edge), :], sem
            ).start()
            return carry

        lax.fori_loop(count_ref[part], count_ref[part + 1], send, 0)
    pltpu.make_async_copy(off_ref, off_ref, sem).wait()
    labels.wait()


def pack(off, route, labels, parts):
    count, edge, _ = off.shape
    planes, tail, _ = labels.shape
    lengths = [slots * edge + (tail if index == 0 else 0) for index, slots in enumerate(parts)]
    anywhere = pl.BlockSpec(memory_space=pl.ANY)
    return pl.pallas_call(
        pack_kernel,
        out_shape=[jax.ShapeDtypeStruct((planes, length, edge), off.dtype) for length in lengths],
        grid_spec=pltpu.PrefetchScalarGridSpec(
            num_scalar_prefetch=len(route),
            grid=(),
            in_specs=[pl.BlockSpec(memory_space=pltpu.VMEM), anywhere],
            out_specs=[anywhere] * len(parts),
            scratch_shapes=[pltpu.SemaphoreType.DMA, pltpu.SemaphoreType.DMA],
        ),
        compiler_params=params(),
        cost_estimate=COST,
        name="pack",
    )(*route, off, labels)


def hold_kernel(x_ref, *rest):
    del x_ref, rest


def hold(x, after):
    anywhere = pl.BlockSpec(memory_space=pl.ANY)
    return pl.pallas_call(
        hold_kernel,
        out_shape=jax.ShapeDtypeStruct(x.shape, x.dtype),
        in_specs=[anywhere] * (1 + len(after)),
        out_specs=anywhere,
        input_output_aliases={0: 0},
        cost_estimate=COST,
        name="hold",
    )(x, *after)


def join_kernel(*refs):
    count = (len(refs) - 2) // 2
    in_refs, out_ref, held, sems = refs[:count], refs[count], refs[count + 1], refs[count + 2 :]
    begin, moves = 0, []
    for in_ref, sem in zip(in_refs, sems, strict=True):
        rows = pl.ds(begin, in_ref.shape[0])
        moves.append((rows, pltpu.make_async_copy(in_ref, held.at[rows, :], sem), sem))
        moves[-1][1].start()
        begin += in_ref.shape[0]
    out = []
    for rows, move, sem in moves:
        move.wait()
        out.append(pltpu.make_async_copy(held.at[rows, :], out_ref.at[rows, :], sem))
        out[-1].start()
    for move in out:
        move.wait()


def join(arrays):
    shape = (sum(array.shape[0] for array in arrays), arrays[0].shape[1])
    anywhere = pl.BlockSpec(memory_space=pl.ANY)
    return pl.pallas_call(
        join_kernel,
        out_shape=jax.ShapeDtypeStruct(shape, arrays[0].dtype),
        in_specs=[anywhere] * len(arrays),
        out_specs=anywhere,
        scratch_shapes=[pltpu.VMEM(shape, arrays[0].dtype)] + [pltpu.SemaphoreType.DMA] * len(arrays),
        compiler_params=params(),
        cost_estimate=COST,
        name="join",
    )(*arrays)


def plane_kernel(begin, most, counts, mirrored, source_ref, row_ref, col_ref, block_ref, *rest):
    omega_refs, (out_ref, total) = rest[: len(counts)], rest[-2:]
    step = pl.program_id(0)
    source = source_ref[step]
    edge = block_ref.shape[2]
    spare = total.shape[0] - 1

    @pl.when(step == 0)
    def _():
        total[...] = jnp.zeros_like(total)

    first = 0
    for omega_ref, count in zip(omega_refs, counts, strict=True):

        @pl.when((step >= first) & (step < first + count))
        def _(omega_ref=omega_ref):
            for m in range(most):
                row = row_ref[source, begin + m]
                col = col_ref[source, begin + m]
                here, there = (row, col) if mirrored else (col, row)
                here = pl.multiple_of(jnp.minimum(here, spare - 1) * edge, edge)
                block = block_ref[0, m * edge : (m + 1) * edge, :]
                omega = omega_ref[0, pl.ds(here, edge), :]
                if mirrored:
                    product = dot(block, omega, TN).astype(jnp.bfloat16).astype(jnp.float32)
                else:
                    product = dot(block, omega)
                total[there] += product

        first += count

    @pl.when(step == pl.num_programs(0) - 1)
    def _():
        out_ref[...] = total[:spare].reshape(out_ref.shape).astype(out_ref.dtype)


def plane_sum(
    blocks, omegas, sources, rows, cols, inside, begin, most, block_rows, dtype, mirrored, after=()
):
    planes, _, edge = blocks.shape
    _, height, columns = omegas[0].shape
    counts = [omega.shape[0] for omega in omegas]

    def held(index):
        first, last = sum(counts[:index]), counts[index] - 1
        return lambda step, *_: (jnp.clip(step - first, 0, last), 0, 0)

    return pl.pallas_call(
        functools.partial(plane_kernel, begin, most, counts, mirrored),
        out_shape=jax.ShapeDtypeStruct((height, columns), dtype),
        grid_spec=pltpu.PrefetchScalarGridSpec(
            num_scalar_prefetch=3,
            grid=(planes,),
            in_specs=[
                pl.BlockSpec((1, most * edge, edge), lambda p, source, *_: (source[p], inside, 0))
            ]
            + [pl.BlockSpec((1, height, columns), held(index)) for index in range(len(counts))]
            + [pl.BlockSpec(memory_space=pl.ANY)] * len(after),
            out_specs=pl.BlockSpec((height, columns), lambda p, *_: (0, 0)),
            scratch_shapes=[pltpu.VMEM((block_rows + 1, edge, columns), jnp.float32)],
        ),
        compiler_params=params(),
        cost_estimate=COST,
        name="mirror" if mirrored else "home",
    )(sources, rows, cols, blocks, *omegas, *after)


def far_kernel(most, parts, lines, added, source_ref, place_ref, row_ref, col_ref, *rest):
    del place_ref
    part_refs, omega_refs = rest[:parts], rest[parts : parts + lines]
    out_ref, total = rest[-2:]
    source = source_ref[pl.program_id(0)]
    edge = part_refs[0].shape[2]
    spare = total.shape[0] - 1
    if added:
        total[:spare] = rest[parts + lines][0].reshape(spare, edge, -1)
    else:
        total[...] = jnp.zeros_like(total)
    places = [
        (part_ref, inside)
        for part_ref in part_refs
        for inside in range(part_ref.shape[1] // (most * edge))
    ]
    for index, (omega_ref, (part_ref, inside)) in enumerate(zip(omega_refs, places, strict=True)):
        for m in range(most):
            row = row_ref[source, index * most + m]
            col = jnp.minimum(col_ref[source, index * most + m], spare - 1)
            slot = inside * most + m
            block = part_ref[0, slot * edge : (slot + 1) * edge, :]
            omega = omega_ref[pl.ds(pl.multiple_of(col * edge, edge), edge), :]
            total[row] += dot(block, omega)
    out_ref[0] = total[:spare].reshape(out_ref.shape[1:]).astype(out_ref.dtype)


def far_sum(
    sources, places, slots, parts, omegas, rows, cols, most, block_rows, dtype, add=None, after=()
):
    edge = parts[0].shape[2]
    height, columns = omegas[0].shape
    more = [] if add is None else [add]
    return pl.pallas_call(
        functools.partial(far_kernel, most, len(parts), len(omegas), len(more)),
        out_shape=jax.ShapeDtypeStruct((slots, height, columns), dtype),
        grid_spec=pltpu.PrefetchScalarGridSpec(
            num_scalar_prefetch=4,
            grid=sources.shape,
            in_specs=[
                pl.BlockSpec((1, part.shape[1], edge), lambda k, source, *_: (source[k], 0, 0))
                for part in parts
            ]
            + [pl.BlockSpec((height, columns), lambda k, *_: (0, 0))] * len(omegas)
            + [pl.BlockSpec((1, height, columns), lambda k, *_: (k, 0, 0))] * len(more)
            + [pl.BlockSpec(memory_space=pl.ANY)] * len(after),
            out_specs=pl.BlockSpec(
                (1, height, columns), lambda k, source, place, *_: (place[k], 0, 0)
            ),
            scratch_shapes=[pltpu.VMEM((block_rows + 1, edge, columns), jnp.float32)],
        ),
        compiler_params=params(),
        cost_estimate=COST,
        name="far",
    )(sources, places, rows, cols, *parts, *omegas, *more, *after)


def base_kernel(diag_ref, omega_ref, *rest):
    *piece_refs, out_ref = rest
    edge = diag_ref.shape[1]
    near = [
        dot(diag_ref[b], omega_ref[b * edge : (b + 1) * edge, :]) for b in range(diag_ref.shape[0])
    ]
    total = jnp.concatenate(near, axis=0)
    for piece_ref in piece_refs:
        total += piece_ref[...].astype(jnp.float32)
    out_ref[...] = total


def base_sum(diag, sketch, pieces):
    block_rows, edge, _ = diag.shape
    height, columns = sketch.shape
    together = math.gcd(block_rows, 2)
    rows = pl.BlockSpec((together * edge, columns), lambda b: (b, 0))
    return pl.pallas_call(
        base_kernel,
        out_shape=jax.ShapeDtypeStruct((height, columns), jnp.float32),
        grid=(block_rows // together,),
        in_specs=[pl.BlockSpec((together, edge, edge), lambda b: (b, 0, 0)), rows]
        + [rows] * len(pieces),
        out_specs=rows,
        compiler_params=params(),
        cost_estimate=COST,
        name="base",
    )(diag, sketch, *pieces)


def image_kernel(scale, chip_ref, base_ref, far_ref, *rest):
    *piece_refs, image_ref, gram_ref, cross = rest
    step = pl.program_id(0)
    image = base_ref[...]
    for piece_ref in piece_refs:
        image += piece_ref[...].astype(jnp.float32)
    for chip in range(far_ref.shape[0]):
        piece = far_ref[chip].astype(jnp.float32)
        image += jnp.where(chip == chip_ref[0], 0.0, piece)
    image_ref[...] = image

    @pl.when(step == 0)
    def _():
        gram_ref[...] = jnp.zeros_like(gram_ref)
        cross[...] = jnp.zeros_like(cross)

    high, low = split(image)
    gram_ref[...] += dot(high, high, TN)
    cross[...] += dot(high, low, TN)

    @pl.when(step == pl.num_programs(0) - 1)
    def _():
        gram_ref[...] = (gram_ref[...] + (cross[...] + cross[...].T)) * scale


def image_and_gram(base, chip, far, pieces, total_rows):
    height, columns = base.shape
    tile = math.gcd(height, 256)
    rows = pl.BlockSpec((tile, columns), lambda b, _: (b, 0))
    return pl.pallas_call(
        functools.partial(image_kernel, 1.0 / total_rows),
        out_shape=(
            jax.ShapeDtypeStruct((height, columns), jnp.float32),
            jax.ShapeDtypeStruct((columns, columns), jnp.float32),
        ),
        grid_spec=pltpu.PrefetchScalarGridSpec(
            num_scalar_prefetch=1,
            grid=(height // tile,),
            in_specs=[rows, pl.BlockSpec((far.shape[0], tile, columns), lambda b, _: (0, b, 0))]
            + [rows] * len(pieces),
            out_specs=(rows, pl.BlockSpec((columns, columns), lambda b, _: (0, 0))),
            scratch_shapes=[pltpu.VMEM((columns, columns), jnp.float32)],
        ),
        compiler_params=params(),
        cost_estimate=COST,
        name="image",
    )(chip.reshape(1), base, far, *pieces)


def factor_kernel(rounds, gram_ref, image_ref, basis_ref, factor_ref, inverse, work):
    n = gram_ref.shape[0]
    exact = lax.Precision.HIGHEST

    @pl.when(pl.program_id(0) == 0)
    def _():
        gram = gram_ref[...]
        row = lax.broadcasted_iota(jnp.int32, (n, n), 0)
        col = lax.broadcasted_iota(jnp.int32, (n, n), 1)
        weight = jnp.where(row > col, 1.0, jnp.where(row == col, 0.5, 0.0))
        one = jnp.where(row == col, 1.0, 0.0)
        diagonal = jnp.where(row == col, gram, 0.0)
        down = lax.rsqrt(jnp.sum(diagonal, axis=1, keepdims=True))
        across = lax.rsqrt(jnp.sum(diagonal, axis=0, keepdims=True))
        scaled = gram * down * across
        step = one - weight * (scaled - one)
        guess = step
        for turn in range(rounds):
            if turn == rounds - 1:
                error = dot(dot(guess, scaled, precision=exact), guess, NT, precision=exact) - one
                step = weight * error
                guess = guess - dot(step, guess, precision=exact)
            else:
                g3 = split(guess)
                error = dot3(split(dot3(g3, split(scaled))), g3, NT) - one
                guess = guess - dot3(split(weight * error), g3)
        guess = jnp.where(row >= col, guess, 0.0)
        inverse[...] = guess * across
        factor_ref[...] = jnp.where(row <= col, dot(inverse[...], gram, precision=exact), 0.0)
        size = jnp.sum(error * error)

        @pl.when(jnp.logical_not(size < 1e-6))
        def _():
            work[...] = gram
            inverse[...] = one
            lane = lax.broadcasted_iota(jnp.int32, (1, n), 1)

            def eliminate(j, carry):
                line = work[pl.ds(j, 1), :]
                pivot = jnp.sum(jnp.where(lane == j, line, 0.0), axis=1, keepdims=True)
                scale = lax.rsqrt(pivot)
                line = jnp.where(lane >= j, line * scale, 0.0)
                other = inverse[pl.ds(j, 1), :] * scale
                below = jnp.where(lane > j, line, 0.0)
                work[...] -= dot(below, line, TN, exact)
                inverse[...] -= dot(below, other, TN, exact)
                inverse[pl.ds(j, 1), :] = other
                factor_ref[pl.ds(j, 1), :] = line
                return carry

            lax.fori_loop(0, n, eliminate, 0)

    basis_ref[...] = dot3(split(image_ref[...]), split(inverse[...]), NT)

def factor_and_basis(gram, image, tile=256, rounds=3):
    height, n = image.shape
    whole = pl.BlockSpec((n, n), lambda b: (0, 0))
    tiles = pl.BlockSpec((tile, n), lambda b: (b, 0))
    return pl.pallas_call(
        functools.partial(factor_kernel, rounds),
        out_shape=(jax.ShapeDtypeStruct((height, n), jnp.float32), jax.ShapeDtypeStruct((n, n), jnp.float32)),
        grid=(height // tile,),
        in_specs=[whole, tiles],
        out_specs=(tiles, whole),
        scratch_shapes=[pltpu.VMEM((n, n), jnp.float32)] * 2,
        compiler_params=params(),
        name="factor",
    )(gram, image)


def sum_over_devices(part, peers):
    rows, columns = part.shape
    pieces = lax.all_to_all(part.reshape(peers, rows // peers, columns), ALL, 0, 0, tiled=True)
    mine = jnp.broadcast_to(jnp.sum(pieces, axis=0), pieces.shape)
    return lax.all_to_all(mine, ALL, 0, 0, tiled=True).reshape(rows, columns)


def on_device(diag_blocks, off_blocks, col_blocks, sketch):
    block_rows, per_row = col_blocks.shape
    edge = diag_blocks.shape[1]
    layers = lax.axis_size(LINE)
    planes = lax.axis_size(PLANE)
    peers = layers * planes
    requests = block_rows * per_row
    most = max(2, (2 * requests + peers - 1) // peers)
    slots = layers * most
    layer = lax.axis_index(LINE)
    shifts = sorted(range(layers), key=lambda shift: -min(shift, layers - shift))
    cut = layers // 2
    groups = [group for group in (shifts[:cut], shifts[cut:-1], shifts[-1:]) if group]
    flat = col_blocks.reshape(requests)
    owners = flat // block_rows
    order = jnp.arange(requests)
    earlier = (owners[:, None] == owners[None, :]) & (order[None, :] < order[:, None])
    ranks = jnp.sum(earlier.astype(jnp.int32), axis=1)
    to_plane = owners % planes
    away = lax.rem(owners // planes - layer + layers, layers)
    turn = sum(jnp.where(away == shift, index, 0) for index, shift in enumerate(shifts))
    to_slot = turn * most + ranks
    place = to_plane * slots + to_slot
    hit = place[:, None] == jnp.arange(planes * slots)[None, :]
    row_label = block_rows + jnp.sum(
        jnp.where(hit, (order // per_row - block_rows)[:, None], 0), axis=0
    )
    col_label = block_rows + jnp.sum(
        jnp.where(hit, (flat % block_rows - block_rows)[:, None], 0), axis=0
    )
    labels = jnp.stack([row_label.reshape(planes, slots), col_label.reshape(planes, slots)], axis=1)
    labels = jnp.pad(labels, ((0, 0), (0, TAIL - 2), (0, edge - slots))).astype(jnp.bfloat16)
    sizes = [len(group) * most for group in groups]
    ends = [sum(sizes[: index + 1]) for index in range(len(sizes))]
    in_part = sum((to_slot >= end).astype(jnp.int32) for end in ends)
    begins = sum(jnp.where(in_part == index + 1, end, 0) for index, end in enumerate(ends))
    before = jnp.sum(
        (in_part[None, :] < in_part[:, None])
        | ((in_part[None, :] == in_part[:, None]) & (order[None, :] < order[:, None])),
        axis=1,
    )
    pick = before[None, :] == order[:, None]
    route = [
        jnp.sum(jnp.where(pick, values[None, :], 0), axis=1)
        for values in (order, to_plane, to_slot - begins)
    ]
    counts = jnp.sum(in_part[None, :] < jnp.arange(len(sizes) + 1)[:, None], axis=1)
    outgoing = list(
        pack(off_blocks.reshape(requests, edge, edge), route + [counts], labels, sizes)
    )

    line_omegas = []
    for shift in shifts[:-1]:
        steps = [(z, (z - shift) % layers) for z in range(layers)]
        line_omegas.append(lax.ppermute(sketch, LINE, steps))
    chip, core = lax.axis_index(CHIPS), lax.axis_index(CORE)
    if [lax.axis_size(axis) for axis in PLANE] == [2, 2, 2]:
        swap = [(0, 1), (1, 0)]
        by_x, by_y = (lax.ppermute(sketch, axis, swap) for axis in CHIPS)
        half = sketch.shape[0] // 2
        across = [
            lax.ppermute(by_y[:half], CHIPS[0], swap),
            lax.ppermute(by_x[half:], CHIPS[1], swap),
        ]
        outgoing[0] = hold(outgoing[0], [by_x, by_y])
        mine = join([sketch, by_y, by_x] + across)
        plane_omegas = [
            array.reshape((4,) + sketch.shape) for array in (mine, lax.ppermute(mine, CORE, swap))
        ]
        near_chips = (chip ^ jnp.arange(4)) * 2
        sources = jnp.concatenate([near_chips + core, near_chips + 1 - core])
    else:
        plane_omegas = [lax.all_gather(sketch, PLANE)]
        sources = jnp.arange(planes)
    outgoing[1] = hold(outgoing[1], line_omegas)
    parts = [lax.all_to_all(part, PLANE, 0, 0, tiled=True) for part in outgoing]
    lines = sizes[0] * edge
    rows = parts[0][:, lines, :slots].astype(jnp.int32)
    cols = parts[0][:, lines + 1, :slots].astype(jnp.int32)

    def send_mirror(index, after):
        part = sum(index * most >= end for end in ends)
        inside = index - (ends[part] - sizes[part]) // most
        shift = shifts[index]
        kind = jnp.bfloat16 if shift else jnp.float32
        mirror = plane_sum(
            parts[part],
            plane_omegas,
            sources,
            rows,
            cols,
            inside,
            index * most,
            most,
            block_rows,
            kind,
            True,
            after,
        )
        steps = [(z, (z + shift) % layers) for z in range(layers)]
        return lax.ppermute(mirror, LINE, steps) if shift else mirror, (mirror,)

    pieces, latest = [], ()
    for index in range(cut):
        piece, latest = send_mirror(index, latest)
        pieces.append(piece)

    cores = lax.axis_size(CORE)
    chips = planes // cores
    away = (chip + jnp.arange(1, chips)) % chips
    far = functools.partial(
        far_sum,
        parts=parts[:-1],
        omegas=line_omegas,
        rows=rows,
        cols=cols,
        most=most,
        block_rows=block_rows,
    )

    def ask(chips_asked, after):
        if cores == 1:
            return None, after
        count = chips_asked.shape[0]
        other = far(
            chips_asked * cores + 1 - core, jnp.arange(count), count, dtype=jnp.float32, after=after
        )
        return lax.ppermute(other, CORE, [(0, 1), (1, 0)]), (other,)

    other, latest = ask(away, latest)
    late = []
    for index in range(cut, layers - 1):
        piece, latest = send_mirror(index, latest)
        late.append(piece)
    sent = far(away * cores + core, away, chips, dtype=jnp.bfloat16, add=other, after=latest)
    received = lax.all_to_all(hold(sent, parts[-1:]), CHIPS, 0, 0, tiled=True)
    other, latest = ask(chip.reshape(1), (sent,))
    mirror, latest = send_mirror(layers - 1, latest)
    home = plane_sum(
        outgoing[-1],
        plane_omegas,
        sources,
        row_label.reshape(planes, slots),
        col_label.reshape(planes, slots),
        0,
        slots - most,
        most,
        block_rows,
        jnp.float32,
        False,
        latest,
    )
    own = far(
        chip.reshape(1) * cores + core, jnp.arange(1), 1, dtype=jnp.float32, add=other, after=(home,)
    )
    base = base_sum(diag_blocks, sketch, [home, mirror, own.reshape(sketch.shape)] + pieces)
    image, part = image_and_gram(base, chip, received, late, block_rows * edge * peers)
    gram = sum_over_devices(part, peers)
    return factor_and_basis(gram, image)


def solution(mesh):
    rows, sub = mesh.devices.shape
    layers, cores = math.gcd(rows, 4), math.gcd(sub, 2)
    devices = mesh.devices.reshape(layers, rows // layers, sub // cores, cores)
    placed = (P(ALL, None, None), P(ALL, None, None, None), P(ALL, None), P(ALL, None))
    return jax.shard_map(
        on_device,
        mesh=Mesh(devices, ALL),
        in_specs=placed,
        out_specs=(P(ALL, None), P()),
        check_vma=False,
    )
```

```python
import functools
import math

import jax
import jax.numpy as jnp
from jax import lax
from jax.experimental import pallas as pl
from jax.experimental.pallas import tpu as pltpu
from jax.sharding import Mesh
from jax.sharding import PartitionSpec as P

LINE = "z"
PLANE = ("x", "y", "c")
ALL = (LINE,) + PLANE
CHIPS, CORE = PLANE[:2], PLANE[2]
VMEM_LIMIT = 48 * 1024 * 1024
VMEM_ALL = 60 * 1024 * 1024
COST = pl.CostEstimate(flops=10**12, bytes_accessed=10**11, transcendentals=0)
TAIL = 16


def dot(a, b, contract=((1,), (0,)), precision=None):
    return lax.dot_general(
        a, b, (contract, ((), ())), precision=precision, preferred_element_type=jnp.float32
    )


NT = ((1,), (1,))
TN = ((0,), (0,))


def params(limit=VMEM_LIMIT):
    return pltpu.CompilerParams(vmem_limit_bytes=limit)


def split(a):
    high = a.astype(jnp.bfloat16)
    return high, (a - high.astype(jnp.float32)).astype(jnp.bfloat16)

def dot3(a, b, contract=((1,), (0,))):
    (ah, al), (bh, bl) = a, b
    return dot(ah, bh, contract) + (dot(ah, bl, contract) + dot(al, bh, contract))

def pack_kernel(entry_ref, plane_ref, slot_ref, count_ref, off_ref, label_ref, *rest):
    *out_refs, sem, label_sem = rest
    _, edge, _ = off_ref.shape
    tail = label_ref.shape[1]
    first = out_refs[0]
    labels = pltpu.make_async_copy(
        label_ref, first.at[:, pl.ds(first.shape[1] - tail, tail), :], label_sem
    )
    labels.start()
    for part, out_ref in enumerate(out_refs):

        def send(place, carry, out_ref=out_ref):
            row = pl.multiple_of(slot_ref[place] * edge, edge)
            pltpu.make_async_copy(
                off_ref.at[entry_ref[place]], out_ref.at[plane_ref[place], pl.ds(row, edge), :], sem
            ).start()
            return carry

        lax.fori_loop(count_ref[part], count_ref[part + 1], send, 0)
    pltpu.make_async_copy(off_ref, off_ref, sem).wait()
    labels.wait()


def pack(off, route, labels, parts):
    count, edge, _ = off.shape
    planes, tail, _ = labels.shape
    lengths = [slots * edge + (tail if index == 0 else 0) for index, slots in enumerate(parts)]
    anywhere = pl.BlockSpec(memory_space=pl.ANY)
    return pl.pallas_call(
        pack_kernel,
        out_shape=[jax.ShapeDtypeStruct((planes, length, edge), off.dtype) for length in lengths],
        grid_spec=pltpu.PrefetchScalarGridSpec(
            num_scalar_prefetch=len(route),
            grid=(),
            in_specs=[pl.BlockSpec(memory_space=pltpu.VMEM), anywhere],
            out_specs=[anywhere] * len(parts),
            scratch_shapes=[pltpu.SemaphoreType.DMA, pltpu.SemaphoreType.DMA],
        ),
        compiler_params=params(),
        cost_estimate=COST,
        name="pack",
    )(*route, off, labels)


def hold_kernel(x_ref, *rest):
    del x_ref, rest


def hold(x, after):
    anywhere = pl.BlockSpec(memory_space=pl.ANY)
    return pl.pallas_call(
        hold_kernel,
        out_shape=jax.ShapeDtypeStruct(x.shape, x.dtype),
        in_specs=[anywhere] * (1 + len(after)),
        out_specs=anywhere,
        input_output_aliases={0: 0},
        cost_estimate=COST,
        name="hold",
    )(x, *after)


def join_kernel(*refs):
    count = (len(refs) - 2) // 2
    in_refs, out_ref, held, sems = refs[:count], refs[count], refs[count + 1], refs[count + 2 :]
    begin, moves = 0, []
    for in_ref, sem in zip(in_refs, sems, strict=True):
        rows = pl.ds(begin, in_ref.shape[0])
        moves.append((rows, pltpu.make_async_copy(in_ref, held.at[rows, :], sem), sem))
        moves[-1][1].start()
        begin += in_ref.shape[0]
    out = []
    for rows, move, sem in moves:
        move.wait()
        out.append(pltpu.make_async_copy(held.at[rows, :], out_ref.at[rows, :], sem))
        out[-1].start()
    for move in out:
        move.wait()


def join(arrays):
    shape = (sum(array.shape[0] for array in arrays), arrays[0].shape[1])
    anywhere = pl.BlockSpec(memory_space=pl.ANY)
    return pl.pallas_call(
        join_kernel,
        out_shape=jax.ShapeDtypeStruct(shape, arrays[0].dtype),
        in_specs=[anywhere] * len(arrays),
        out_specs=anywhere,
        scratch_shapes=[pltpu.VMEM(shape, arrays[0].dtype)] + [pltpu.SemaphoreType.DMA] * len(arrays),
        compiler_params=params(),
        cost_estimate=COST,
        name="join",
    )(*arrays)


def plane_kernel(inside, begin, most, counts, mirrored, source_ref, row_ref, col_ref, *rest):
    block_ref, *omega_refs = rest[: 1 + len(counts)]
    out_ref, total, blocks, omegas, block_sem, omega_sem = rest[-6:]
    edge = blocks.shape[2]
    spare = total.shape[0] - 1
    places = [(omega_ref, k) for omega_ref, count in zip(omega_refs, counts) for k in range(count)]
    moves = []
    for step, (omega_ref, k) in enumerate(places):
        rows = pl.ds(inside * most * edge, most * edge)
        moves.append(
            (
                pltpu.make_async_copy(
                    block_ref.at[source_ref[step], rows, :], blocks.at[step], block_sem.at[step]
                ),
                pltpu.make_async_copy(omega_ref.at[k], omegas.at[step], omega_sem.at[step]),
            )
        )
        for move in moves[-1]:
            move.start()
    total[...] = jnp.zeros_like(total)
    for step in range(len(places)):
        source = source_ref[step]
        for move in moves[step]:
            move.wait()
        for m in range(most):
            row = row_ref[source, begin + m]
            col = col_ref[source, begin + m]
            here, there = (row, col) if mirrored else (col, row)
            here = pl.multiple_of(jnp.minimum(here, spare - 1) * edge, edge)
            block = blocks[step, m * edge : (m + 1) * edge, :]
            omega = omegas[step, pl.ds(here, edge), :]
            if mirrored:
                product = dot(block, omega, TN).astype(jnp.bfloat16).astype(jnp.float32)
            else:
                product = dot(block, omega)
            total[there] += product
    out_ref[...] = total[:spare].reshape(out_ref.shape).astype(out_ref.dtype)


def plane_sum(
    blocks, omegas, sources, rows, cols, inside, begin, most, block_rows, dtype, mirrored, after=()
):
    planes, _, edge = blocks.shape
    _, height, columns = omegas[0].shape
    counts = [omega.shape[0] for omega in omegas]
    anywhere = pl.BlockSpec(memory_space=pl.ANY)
    return pl.pallas_call(
        functools.partial(plane_kernel, inside, begin, most, counts, mirrored),
        out_shape=jax.ShapeDtypeStruct((height, columns), dtype),
        grid_spec=pltpu.PrefetchScalarGridSpec(
            num_scalar_prefetch=3,
            grid=(),
            in_specs=[anywhere] * (1 + len(omegas) + len(after)),
            out_specs=pl.BlockSpec(memory_space=pltpu.VMEM),
            scratch_shapes=[
                pltpu.VMEM((block_rows + 1, edge, columns), jnp.float32),
                pltpu.VMEM((planes, most * edge, edge), blocks.dtype),
                pltpu.VMEM((planes, height, columns), omegas[0].dtype),
                pltpu.SemaphoreType.DMA((planes,)),
                pltpu.SemaphoreType.DMA((planes,)),
            ],
        ),
        compiler_params=params(VMEM_ALL),
        cost_estimate=COST,
        name="mirror" if mirrored else "home",
    )(sources, rows, cols, blocks, *omegas, *after)


def far_kernel(most, sizes, lines, added, source_ref, place_ref, row_ref, col_ref, *rest):
    parts = len(sizes)
    part_refs, omega_refs = rest[:parts], rest[parts : parts + lines]
    out_ref, total, omegas, omega_sem, adds, add_sem, outs, out_sem, part_sem, *blocks = rest[-9 - parts :]
    edge = total.shape[1]
    spare = total.shape[0] - 1
    count, depth = source_ref.shape[0], outs.shape[0]

    def arrive(k):
        slot, source = k % depth, source_ref[k]
        moves = [
            pltpu.make_async_copy(
                part_refs[p].at[source, pl.ds(0, sizes[p] * edge), :],
                blocks[p].at[slot],
                part_sem.at[p, slot],
            )
            for p in range(parts)
        ]
        if added:
            moves.append(
                pltpu.make_async_copy(rest[parts + lines].at[k], adds.at[slot], add_sem.at[slot])
            )
        return moves

    def leave(k):
        slot = k % depth
        return pltpu.make_async_copy(outs.at[slot], out_ref.at[place_ref[k]], out_sem.at[slot])

    lead = [
        pltpu.make_async_copy(omega_refs[index], omegas.at[index], omega_sem.at[index])
        for index in range(lines)
    ]
    for k in range(min(depth, count)):
        for move in arrive(k):
            move.start()
        if k == 0:
            for move in lead:
                move.start()
    for k in range(count):
        slot, source = k % depth, source_ref[k]
        for move in arrive(k):
            move.wait()
        if added:
            total[:spare] = adds[slot].reshape(spare, edge, -1)
        else:
            total[...] = jnp.zeros_like(total)
        index = 0
        for p in range(parts):
            for place in range(sizes[p]):
                line = index // most
                if k == 0 and index % most == 0:
                    lead[line].wait()
                row = row_ref[source, index]
                col = pl.multiple_of(jnp.minimum(col_ref[source, index], spare - 1) * edge, edge)
                block = blocks[p][slot, place * edge : (place + 1) * edge, :]
                total[row] += dot(block, omegas[line, pl.ds(col, edge), :])
                index += 1
        if k >= depth:
            leave(k - depth).wait()
        outs[slot] = total[:spare].reshape(outs.shape[1:]).astype(outs.dtype)
        leave(k).start()
        if k + depth < count:
            for move in arrive(k + depth):
                move.start()
    for k in range(max(0, count - depth), count):
        leave(k).wait()


def far_sum(
    sources, places, slots, parts, omegas, rows, cols, most, block_rows, dtype, add=None, after=()
):
    edge = parts[0].shape[2]
    height, columns = omegas[0].shape
    more = [] if add is None else [add]
    lines = len(omegas)
    sizes = [part.shape[1] // (most * edge) * most for part in parts]
    depth = min(3, sources.shape[0])
    anywhere = pl.BlockSpec(memory_space=pl.ANY)
    return pl.pallas_call(
        functools.partial(far_kernel, most, sizes, lines, len(more)),
        out_shape=jax.ShapeDtypeStruct((slots, height, columns), dtype),
        grid_spec=pltpu.PrefetchScalarGridSpec(
            num_scalar_prefetch=4,
            grid=(),
            in_specs=[anywhere] * (len(parts) + lines + len(more) + len(after)),
            out_specs=anywhere,
            scratch_shapes=[
                pltpu.VMEM((block_rows + 1, edge, columns), jnp.float32),
                pltpu.VMEM((lines, height, columns), omegas[0].dtype),
                pltpu.SemaphoreType.DMA((lines,)),
                pltpu.VMEM((depth if more else 1, height, columns), jnp.float32),
                pltpu.SemaphoreType.DMA((depth,)),
                pltpu.VMEM((depth, height, columns), dtype),
                pltpu.SemaphoreType.DMA((depth,)),
                pltpu.SemaphoreType.DMA((len(parts), depth)),
            ]
            + [pltpu.VMEM((depth, size * edge, edge), parts[0].dtype) for size in sizes],
        ),
        compiler_params=params(VMEM_ALL),
        cost_estimate=COST,
        name="far",
    )(sources, places, rows, cols, *parts, *omegas, *more, *after)


def base_kernel(diag_ref, omega_ref, *rest):
    *piece_refs, out_ref = rest
    edge = diag_ref.shape[1]
    near = [
        dot(diag_ref[b], omega_ref[b * edge : (b + 1) * edge, :]) for b in range(diag_ref.shape[0])
    ]
    total = jnp.concatenate(near, axis=0)
    for piece_ref in piece_refs:
        total += piece_ref[...].astype(jnp.float32)
    out_ref[...] = total


def base_sum(diag, sketch, pieces):
    block_rows, edge, _ = diag.shape
    height, columns = sketch.shape
    together = math.gcd(block_rows, 2)
    rows = pl.BlockSpec((together * edge, columns), lambda b: (b, 0))
    return pl.pallas_call(
        base_kernel,
        out_shape=jax.ShapeDtypeStruct((height, columns), jnp.float32),
        grid=(block_rows // together,),
        in_specs=[pl.BlockSpec((together, edge, edge), lambda b: (b, 0, 0)), rows]
        + [rows] * len(pieces),
        out_specs=rows,
        compiler_params=params(),
        cost_estimate=COST,
        name="base",
    )(diag, sketch, *pieces)


def image_kernel(scale, chip_ref, base_ref, far_ref, *rest):
    *piece_refs, image_ref, gram_ref, cross = rest
    step = pl.program_id(0)
    image = base_ref[...]
    for piece_ref in piece_refs:
        image += piece_ref[...].astype(jnp.float32)
    for chip in range(far_ref.shape[0]):
        piece = far_ref[chip].astype(jnp.float32)
        image += jnp.where(chip == chip_ref[0], 0.0, piece)
    image_ref[...] = image

    @pl.when(step == 0)
    def _():
        gram_ref[...] = jnp.zeros_like(gram_ref)
        cross[...] = jnp.zeros_like(cross)

    high, low = split(image)
    gram_ref[...] += dot(high, high, TN)
    cross[...] += dot(high, low, TN)

    @pl.when(step == pl.num_programs(0) - 1)
    def _():
        gram_ref[...] = (gram_ref[...] + (cross[...] + cross[...].T)) * scale


def image_and_gram(base, chip, far, pieces, total_rows):
    height, columns = base.shape
    tile = math.gcd(height, 256)
    rows = pl.BlockSpec((tile, columns), lambda b, _: (b, 0))
    return pl.pallas_call(
        functools.partial(image_kernel, 1.0 / total_rows),
        out_shape=(
            jax.ShapeDtypeStruct((height, columns), jnp.float32),
            jax.ShapeDtypeStruct((columns, columns), jnp.float32),
        ),
        grid_spec=pltpu.PrefetchScalarGridSpec(
            num_scalar_prefetch=1,
            grid=(height // tile,),
            in_specs=[rows, pl.BlockSpec((far.shape[0], tile, columns), lambda b, _: (0, b, 0))]
            + [rows] * len(pieces),
            out_specs=(rows, pl.BlockSpec((columns, columns), lambda b, _: (0, 0))),
            scratch_shapes=[pltpu.VMEM((columns, columns), jnp.float32)],
        ),
        compiler_params=params(),
        cost_estimate=COST,
        name="image",
    )(chip.reshape(1), base, far, *pieces)


def factor_kernel(rounds, gram_ref, image_ref, basis_ref, factor_ref, inverse, work):
    n = gram_ref.shape[0]
    exact = lax.Precision.HIGHEST

    @pl.when(pl.program_id(0) == 0)
    def _():
        gram = gram_ref[...]
        row = lax.broadcasted_iota(jnp.int32, (n, n), 0)
        col = lax.broadcasted_iota(jnp.int32, (n, n), 1)
        weight = jnp.where(row > col, 1.0, jnp.where(row == col, 0.5, 0.0))
        one = jnp.where(row == col, 1.0, 0.0)
        diagonal = jnp.where(row == col, gram, 0.0)
        down = lax.rsqrt(jnp.sum(diagonal, axis=1, keepdims=True))
        across = lax.rsqrt(jnp.sum(diagonal, axis=0, keepdims=True))
        scaled = gram * down * across
        step = one - weight * (scaled - one)
        guess = step
        for turn in range(rounds):
            if turn == rounds - 1:
                error = dot(dot(guess, scaled, precision=exact), guess, NT, precision=exact) - one
                step = weight * error
                guess = guess - dot(step, guess, precision=exact)
            else:
                g3 = split(guess)
                error = dot3(split(dot3(g3, split(scaled))), g3, NT) - one
                guess = guess - dot3(split(weight * error), g3)
        guess = jnp.where(row >= col, guess, 0.0)
        inverse[...] = guess * across
        factor_ref[...] = jnp.where(row <= col, dot(inverse[...], gram, precision=exact), 0.0)
        size = jnp.sum(error * error)

        @pl.when(jnp.logical_not(size < 1e-6))
        def _():
            work[...] = gram
            inverse[...] = one
            lane = lax.broadcasted_iota(jnp.int32, (1, n), 1)

            def eliminate(j, carry):
                line = work[pl.ds(j, 1), :]
                pivot = jnp.sum(jnp.where(lane == j, line, 0.0), axis=1, keepdims=True)
                scale = lax.rsqrt(pivot)
                line = jnp.where(lane >= j, line * scale, 0.0)
                other = inverse[pl.ds(j, 1), :] * scale
                below = jnp.where(lane > j, line, 0.0)
                work[...] -= dot(below, line, TN, exact)
                inverse[...] -= dot(below, other, TN, exact)
                inverse[pl.ds(j, 1), :] = other
                factor_ref[pl.ds(j, 1), :] = line
                return carry

            lax.fori_loop(0, n, eliminate, 0)

    basis_ref[...] = dot3(split(image_ref[...]), split(inverse[...]), NT)

def factor_and_basis(gram, image, tile=256, rounds=3):
    height, n = image.shape
    whole = pl.BlockSpec((n, n), lambda b: (0, 0))
    tiles = pl.BlockSpec((tile, n), lambda b: (b, 0))
    return pl.pallas_call(
        functools.partial(factor_kernel, rounds),
        out_shape=(jax.ShapeDtypeStruct((height, n), jnp.float32), jax.ShapeDtypeStruct((n, n), jnp.float32)),
        grid=(height // tile,),
        in_specs=[whole, tiles],
        out_specs=(tiles, whole),
        scratch_shapes=[pltpu.VMEM((n, n), jnp.float32)] * 2,
        compiler_params=params(),
        name="factor",
    )(gram, image)


def sum_over_devices(part, peers):
    rows, columns = part.shape
    pieces = lax.all_to_all(part.reshape(peers, rows // peers, columns), ALL, 0, 0, tiled=True)
    mine = jnp.broadcast_to(jnp.sum(pieces, axis=0), pieces.shape)
    return lax.all_to_all(mine, ALL, 0, 0, tiled=True).reshape(rows, columns)


def on_device(diag_blocks, off_blocks, col_blocks, sketch):
    block_rows, per_row = col_blocks.shape
    edge = diag_blocks.shape[1]
    layers = lax.axis_size(LINE)
    planes = lax.axis_size(PLANE)
    peers = layers * planes
    requests = block_rows * per_row
    most = max(2, (2 * requests + peers - 1) // peers)
    slots = layers * most
    layer = lax.axis_index(LINE)
    shifts = sorted(range(layers), key=lambda shift: -min(shift, layers - shift))
    cut = layers // 2
    groups = [group for group in (shifts[:cut], shifts[cut:-1], shifts[-1:]) if group]
    flat = col_blocks.reshape(requests)
    owners = flat // block_rows
    order = jnp.arange(requests)
    earlier = (owners[:, None] == owners[None, :]) & (order[None, :] < order[:, None])
    ranks = jnp.sum(earlier.astype(jnp.int32), axis=1)
    to_plane = owners % planes
    away = lax.rem(owners // planes - layer + layers, layers)
    turn = sum(jnp.where(away == shift, index, 0) for index, shift in enumerate(shifts))
    to_slot = turn * most + ranks
    place = to_plane * slots + to_slot
    hit = place[:, None] == jnp.arange(planes * slots)[None, :]
    row_label = block_rows + jnp.sum(
        jnp.where(hit, (order // per_row - block_rows)[:, None], 0), axis=0
    )
    col_label = block_rows + jnp.sum(
        jnp.where(hit, (flat % block_rows - block_rows)[:, None], 0), axis=0
    )
    labels = jnp.stack([row_label.reshape(planes, slots), col_label.reshape(planes, slots)], axis=1)
    labels = jnp.pad(labels, ((0, 0), (0, TAIL - 2), (0, edge - slots))).astype(jnp.bfloat16)
    sizes = [len(group) * most for group in groups]
    ends = [sum(sizes[: index + 1]) for index in range(len(sizes))]
    in_part = sum((to_slot >= end).astype(jnp.int32) for end in ends)
    begins = sum(jnp.where(in_part == index + 1, end, 0) for index, end in enumerate(ends))
    before = jnp.sum(
        (in_part[None, :] < in_part[:, None])
        | ((in_part[None, :] == in_part[:, None]) & (order[None, :] < order[:, None])),
        axis=1,
    )
    pick = before[None, :] == order[:, None]
    route = [
        jnp.sum(jnp.where(pick, values[None, :], 0), axis=1)
        for values in (order, to_plane, to_slot - begins)
    ]
    counts = jnp.sum(in_part[None, :] < jnp.arange(len(sizes) + 1)[:, None], axis=1)
    outgoing = list(
        pack(off_blocks.reshape(requests, edge, edge), route + [counts], labels, sizes)
    )

    line_omegas = []
    for shift in shifts[:-1]:
        steps = [(z, (z - shift) % layers) for z in range(layers)]
        line_omegas.append(lax.ppermute(sketch, LINE, steps))
    chip, core = lax.axis_index(CHIPS), lax.axis_index(CORE)
    if [lax.axis_size(axis) for axis in PLANE] == [2, 2, 2]:
        swap = [(0, 1), (1, 0)]
        by_x, by_y = (lax.ppermute(sketch, axis, swap) for axis in CHIPS)
        half = sketch.shape[0] // 2
        across = [
            lax.ppermute(by_y[:half], CHIPS[0], swap),
            lax.ppermute(by_x[half:], CHIPS[1], swap),
        ]
        outgoing[0] = hold(outgoing[0], [by_x, by_y])
        mine = join([sketch, by_y, by_x] + across)
        plane_omegas = [
            array.reshape((4,) + sketch.shape) for array in (mine, lax.ppermute(mine, CORE, swap))
        ]
        near_chips = (chip ^ jnp.arange(4)) * 2
        sources = jnp.concatenate([near_chips + core, near_chips + 1 - core])
    else:
        plane_omegas = [lax.all_gather(sketch, PLANE)]
        sources = jnp.arange(planes)
    outgoing[1] = hold(outgoing[1], line_omegas[1:])
    parts = [lax.all_to_all(part, PLANE, 0, 0, tiled=True) for part in outgoing]
    lines = sizes[0] * edge
    rows = parts[0][:, lines, :slots].astype(jnp.int32)
    cols = parts[0][:, lines + 1, :slots].astype(jnp.int32)

    def send_mirror(index, after):
        part = sum(index * most >= end for end in ends)
        inside = index - (ends[part] - sizes[part]) // most
        shift = shifts[index]
        kind = jnp.bfloat16 if shift else jnp.float32
        mirror = plane_sum(
            parts[part],
            plane_omegas,
            sources,
            rows,
            cols,
            inside,
            index * most,
            most,
            block_rows,
            kind,
            True,
            after,
        )
        steps = [(z, (z + shift) % layers) for z in range(layers)]
        return lax.ppermute(mirror, LINE, steps) if shift else mirror, (mirror,)

    pieces, latest = [], ()
    for index in range(cut):
        piece, latest = send_mirror(index, latest)
        pieces.append(piece)

    cores = lax.axis_size(CORE)
    chips = planes // cores
    away = (chip + jnp.arange(1, chips)) % chips
    far = functools.partial(
        far_sum,
        parts=parts[:-1],
        omegas=line_omegas,
        rows=rows,
        cols=cols,
        most=most,
        block_rows=block_rows,
    )

    def ask(chips_asked, after):
        if cores == 1:
            return None, after
        count = chips_asked.shape[0]
        other = far(
            chips_asked * cores + 1 - core, jnp.arange(count), count, dtype=jnp.float32, after=after
        )
        return lax.ppermute(other, CORE, [(0, 1), (1, 0)]), (other,)

    other, latest = ask(away, latest)
    late = []
    for index in range(cut, layers - 1):
        piece, latest = send_mirror(index, latest)
        late.append(piece)
    own_other, latest = ask(chip.reshape(1), latest)
    sent = far(away * cores + core, away, chips, dtype=jnp.bfloat16, add=other, after=latest)
    sent = hold(sent, parts[-1:])
    received = lax.all_to_all(sent, CHIPS, 0, 0, tiled=True)
    mirror, latest = send_mirror(layers - 1, (sent,))
    home = plane_sum(
        outgoing[-1],
        plane_omegas,
        sources,
        row_label.reshape(planes, slots),
        col_label.reshape(planes, slots),
        0,
        slots - most,
        most,
        block_rows,
        jnp.float32,
        False,
        latest,
    )
    own = far(
        chip.reshape(1) * cores + core, jnp.arange(1), 1, dtype=jnp.float32, add=own_other, after=(home,)
    )
    base = base_sum(diag_blocks, sketch, [home, mirror, own.reshape(sketch.shape)] + pieces)
    image, part = image_and_gram(base, chip, received, late, block_rows * edge * peers)
    gram = sum_over_devices(part, peers)
    return factor_and_basis(gram, image)


def solution(mesh):
    rows, sub = mesh.devices.shape
    layers, cores = math.gcd(rows, 4), math.gcd(sub, 2)
    devices = mesh.devices.reshape(layers, rows // layers, sub // cores, cores)
    placed = (P(ALL, None, None), P(ALL, None, None, None), P(ALL, None), P(ALL, None))
    return jax.shard_map(
        on_device,
        mesh=Mesh(devices, ALL),
        in_specs=placed,
        out_specs=(P(ALL, None), P()),
        check_vma=False,
    )
```

```python
import functools
import math

import jax
import jax.numpy as jnp
from jax import lax
from jax.experimental import pallas as pl
from jax.experimental.pallas import tpu as pltpu
from jax.sharding import Mesh
from jax.sharding import PartitionSpec as P

LINE = "z"
PLANE = ("x", "y", "c")
ALL = (LINE,) + PLANE
CHIPS, CORE = PLANE[:2], PLANE[2]
VMEM_LIMIT = 48 * 1024 * 1024
VMEM_ALL = 60 * 1024 * 1024
COST = pl.CostEstimate(flops=10**12, bytes_accessed=10**11, transcendentals=0)
TAIL = 16


def dot(a, b, contract=((1,), (0,)), precision=None):
    return lax.dot_general(
        a, b, (contract, ((), ())), precision=precision, preferred_element_type=jnp.float32
    )


NT = ((1,), (1,))
TN = ((0,), (0,))


def params(limit=VMEM_LIMIT):
    return pltpu.CompilerParams(vmem_limit_bytes=limit)


def split(a):
    high = a.astype(jnp.bfloat16)
    return high, (a - high.astype(jnp.float32)).astype(jnp.bfloat16)

def dot3(a, b, contract=((1,), (0,))):
    (ah, al), (bh, bl) = a, b
    return dot(ah, bh, contract) + (dot(ah, bl, contract) + dot(al, bh, contract))

def pack_kernel(entry_ref, plane_ref, slot_ref, count_ref, off_ref, label_ref, *rest):
    *out_refs, sem, label_sem = rest
    _, edge, _ = off_ref.shape
    tail = label_ref.shape[1]
    first = out_refs[0]
    labels = pltpu.make_async_copy(
        label_ref, first.at[:, pl.ds(first.shape[1] - tail, tail), :], label_sem
    )
    labels.start()
    for part, out_ref in enumerate(out_refs):

        def send(place, carry, out_ref=out_ref):
            row = pl.multiple_of(slot_ref[place] * edge, edge)
            pltpu.make_async_copy(
                off_ref.at[entry_ref[place]], out_ref.at[plane_ref[place], pl.ds(row, edge), :], sem
            ).start()
            return carry

        lax.fori_loop(count_ref[part], count_ref[part + 1], send, 0)
    pltpu.make_async_copy(off_ref, off_ref, sem).wait()
    labels.wait()


def pack(off, route, labels, parts):
    count, edge, _ = off.shape
    planes, tail, _ = labels.shape
    lengths = [slots * edge + (tail if index == 0 else 0) for index, slots in enumerate(parts)]
    anywhere = pl.BlockSpec(memory_space=pl.ANY)
    return pl.pallas_call(
        pack_kernel,
        out_shape=[jax.ShapeDtypeStruct((planes, length, edge), off.dtype) for length in lengths],
        grid_spec=pltpu.PrefetchScalarGridSpec(
            num_scalar_prefetch=len(route),
            grid=(),
            in_specs=[pl.BlockSpec(memory_space=pltpu.VMEM), anywhere],
            out_specs=[anywhere] * len(parts),
            scratch_shapes=[pltpu.SemaphoreType.DMA, pltpu.SemaphoreType.DMA],
        ),
        compiler_params=params(),
        cost_estimate=COST,
        name="pack",
    )(*route, off, labels)


def hold_kernel(x_ref, *rest):
    del x_ref, rest


def hold(x, after):
    anywhere = pl.BlockSpec(memory_space=pl.ANY)
    return pl.pallas_call(
        hold_kernel,
        out_shape=jax.ShapeDtypeStruct(x.shape, x.dtype),
        in_specs=[anywhere] * (1 + len(after)),
        out_specs=anywhere,
        input_output_aliases={0: 0},
        cost_estimate=COST,
        name="hold",
    )(x, *after)


def join_kernel(*refs):
    count = (len(refs) - 2) // 2
    in_refs, out_ref, held, sems = refs[:count], refs[count], refs[count + 1], refs[count + 2 :]
    begin, moves = 0, []
    for in_ref, sem in zip(in_refs, sems, strict=True):
        rows = pl.ds(begin, in_ref.shape[0])
        moves.append((rows, pltpu.make_async_copy(in_ref, held.at[rows, :], sem), sem))
        moves[-1][1].start()
        begin += in_ref.shape[0]
    out = []
    for rows, move, sem in moves:
        move.wait()
        out.append(pltpu.make_async_copy(held.at[rows, :], out_ref.at[rows, :], sem))
        out[-1].start()
    for move in out:
        move.wait()


def join(arrays):
    shape = (sum(array.shape[0] for array in arrays), arrays[0].shape[1])
    anywhere = pl.BlockSpec(memory_space=pl.ANY)
    return pl.pallas_call(
        join_kernel,
        out_shape=jax.ShapeDtypeStruct(shape, arrays[0].dtype),
        in_specs=[anywhere] * len(arrays),
        out_specs=anywhere,
        scratch_shapes=[pltpu.VMEM(shape, arrays[0].dtype)] + [pltpu.SemaphoreType.DMA] * len(arrays),
        compiler_params=params(),
        cost_estimate=COST,
        name="join",
    )(*arrays)


def plane_kernel(inside, begin, most, counts, mirrored, source_ref, row_ref, col_ref, *rest):
    block_ref, *omega_refs = rest[: 1 + len(counts)]
    out_ref, total, blocks, omegas, block_sem, omega_sem = rest[-6:]
    edge = blocks.shape[2]
    spare = total.shape[0] - 1
    places = [(omega_ref, k) for omega_ref, count in zip(omega_refs, counts) for k in range(count)]
    moves = []
    for step, (omega_ref, k) in enumerate(places):
        rows = pl.ds(inside * most * edge, most * edge)
        moves.append(
            (
                pltpu.make_async_copy(
                    block_ref.at[source_ref[step], rows, :], blocks.at[step], block_sem.at[step]
                ),
                pltpu.make_async_copy(omega_ref.at[k], omegas.at[step], omega_sem.at[step]),
            )
        )
        for move in moves[-1]:
            move.start()
    total[...] = jnp.zeros_like(total)
    for step in range(len(places)):
        source = source_ref[step]
        for move in moves[step]:
            move.wait()
        for m in range(most):
            row = row_ref[source, begin + m]
            col = col_ref[source, begin + m]
            here, there = (row, col) if mirrored else (col, row)
            here = pl.multiple_of(jnp.minimum(here, spare - 1) * edge, edge)
            block = blocks[step, m * edge : (m + 1) * edge, :]
            omega = omegas[step, pl.ds(here, edge), :]
            if mirrored:
                product = dot(block, omega, TN).astype(jnp.bfloat16).astype(jnp.float32)
            else:
                product = dot(block, omega)
            total[there] += product
    out_ref[...] = total[:spare].reshape(out_ref.shape).astype(out_ref.dtype)


def plane_sum(
    blocks, omegas, sources, rows, cols, inside, begin, most, block_rows, dtype, mirrored, after=()
):
    planes, _, edge = blocks.shape
    _, height, columns = omegas[0].shape
    counts = [omega.shape[0] for omega in omegas]
    anywhere = pl.BlockSpec(memory_space=pl.ANY)
    return pl.pallas_call(
        functools.partial(plane_kernel, inside, begin, most, counts, mirrored),
        out_shape=jax.ShapeDtypeStruct((height, columns), dtype),
        grid_spec=pltpu.PrefetchScalarGridSpec(
            num_scalar_prefetch=3,
            grid=(),
            in_specs=[anywhere] * (1 + len(omegas) + len(after)),
            out_specs=pl.BlockSpec(memory_space=pltpu.VMEM),
            scratch_shapes=[
                pltpu.VMEM((block_rows + 1, edge, columns), jnp.float32),
                pltpu.VMEM((planes, most * edge, edge), blocks.dtype),
                pltpu.VMEM((planes, height, columns), omegas[0].dtype),
                pltpu.SemaphoreType.DMA((planes,)),
                pltpu.SemaphoreType.DMA((planes,)),
            ],
        ),
        compiler_params=params(VMEM_ALL),
        cost_estimate=COST,
        name="mirror" if mirrored else "home",
    )(sources, rows, cols, blocks, *omegas, *after)


def far_kernel(most, begin, sizes, lines, added, at_home, *refs):
    source_ref, place_ref, above_ref, row_ref, col_ref, home_row_ref, home_col_ref, *refs = refs
    part_refs, refs = refs[: len(sizes)], refs[len(sizes) :]
    omega_refs, refs = refs[: 2 * lines], refs[2 * lines :]
    home_refs, refs = refs[: 2 * at_home], refs[2 * at_home :]
    add_refs = refs[:added]
    scratch = refs[len(refs) - 7 - len(sizes) - added - 2 * at_home :]
    out_ref, total, omegas, omega_sem, outs, out_sem, sems, *held = scratch
    blocks, adds, homes = held[: len(sizes)], held[len(sizes) : len(sizes) + added], held[len(sizes) + added :]
    edge = total.shape[1]
    spare = total.shape[0] - 1
    count, depth = source_ref.shape[0], outs.shape[0]

    def arrive(k):
        slot, source = k % depth, source_ref[k]
        pairs = [
            (part_ref.at[source, pl.ds(0, size * edge), :], block.at[slot])
            for part_ref, size, block in zip(part_refs, sizes, blocks)
        ]
        if at_home:
            pairs.append((home_refs[0].at[source], homes[0].at[slot]))
        pairs += [(add_ref.at[k], add.at[slot]) for add_ref, add in zip(add_refs, adds)]
        return [pltpu.make_async_copy(a, b, sems.at[slot, i]) for i, (a, b) in enumerate(pairs)]

    def leave(k):
        slot = k % depth
        return pltpu.make_async_copy(outs.at[slot], out_ref.at[place_ref[k]], out_sem.at[slot])

    lead = [
        [
            pltpu.make_async_copy(omega_ref, omegas.at[index], omega_sem.at[index])
            for omega_ref in omega_refs[2 * index : 2 * index + 2]
        ]
        for index in range(lines)
    ]
    if at_home:
        own = pltpu.make_async_copy(home_refs[1], homes[1], omega_sem.at[lines])
    for k in range(min(depth, count)):
        for move in arrive(k):
            move.start()
        if k == 0:
            if at_home:
                own.start()
            for index, (above, below) in enumerate(lead):
                pl.when(above_ref[index] == 1)(above.start)
                pl.when(above_ref[index] == 0)(below.start)
    for k in range(count):
        slot, source = k % depth, source_ref[k]
        for move in arrive(k):
            move.wait()
        total[...] = jnp.zeros_like(total)
        if at_home:
            if k == 0:
                own.wait()
            for place in range(most):
                row = jnp.minimum(home_row_ref[source, place], spare - 1)
                row = pl.multiple_of(row * edge, edge)
                block = homes[0][slot, place * edge : (place + 1) * edge, :]
                product = dot(block, homes[1][pl.ds(row, edge), :], TN).astype(jnp.bfloat16)
                total[home_col_ref[source, place]] += product.astype(jnp.float32)
        index = 0
        for block_ref, size in zip(blocks, sizes):
            for place in range(size):
                line = index // most
                if k == 0 and index % most == 0:
                    lead[line][0].wait()
                row = row_ref[source, begin + index]
                col = jnp.minimum(col_ref[source, begin + index], spare - 1)
                block = block_ref[slot, place * edge : (place + 1) * edge, :]
                total[row] += dot(block, omegas[line, pl.ds(pl.multiple_of(col * edge, edge), edge), :])
                index += 1
        if k >= depth:
            leave(k - depth).wait()
        result = total[:spare].reshape(outs.shape[1:])
        for add in adds:
            result += add[slot].astype(jnp.float32)
        outs[slot] = result.astype(outs.dtype)
        leave(k).start()
        if k + depth < count:
            for move in arrive(k + depth):
                move.start()
    for k in range(max(0, count - depth), count):
        leave(k).wait()


def far_sum(
    sources, places, slots, begin, parts, omegas, rows, cols, home, most, block_rows, dtype, adds=(), after=()
):
    edge = parts[0].shape[2]
    height, columns = omegas[0][0].shape
    lines = len(omegas)
    above = jnp.stack([choice for _, _, choice in omegas])
    pairs = [omega for pair in omegas for omega in pair[:2]]
    sizes = [part.shape[1] // (most * edge) * most for part in parts]
    depth = min(3, sources.shape[0])
    home_rows, home_cols, *at_home = home if home else (rows[:, :most], cols[:, :most])
    arrays = [*parts, *pairs, *at_home, *adds, *after]
    anywhere = pl.BlockSpec(memory_space=pl.ANY)
    return pl.pallas_call(
        functools.partial(far_kernel, most, begin, sizes, lines, len(adds), 1 if home else 0),
        out_shape=jax.ShapeDtypeStruct((slots, height, columns), dtype),
        grid_spec=pltpu.PrefetchScalarGridSpec(
            num_scalar_prefetch=7,
            grid=(),
            in_specs=[anywhere] * len(arrays),
            out_specs=anywhere,
            scratch_shapes=[
                pltpu.VMEM((block_rows + 1, edge, columns), jnp.float32),
                pltpu.VMEM((lines, height, columns), pairs[0].dtype),
                pltpu.SemaphoreType.DMA((lines + 1,)),
                pltpu.VMEM((depth, height, columns), dtype),
                pltpu.SemaphoreType.DMA((depth,)),
                pltpu.SemaphoreType.DMA((depth, len(parts) + 1 + len(adds))),
            ]
            + [pltpu.VMEM((depth, size * edge, edge), parts[0].dtype) for size in sizes]
            + [pltpu.VMEM((depth, height, columns), add.dtype) for add in adds]
            + [
                pltpu.VMEM(shape, parts[0].dtype)
                for shape in ([(depth, most * edge, edge), (height, columns)] if home else [])
            ],
        ),
        compiler_params=params(VMEM_ALL),
        cost_estimate=COST,
        name="far",
    )(sources, places, above, rows, cols, home_rows, home_cols, *arrays)


def base_kernel(diag_ref, omega_ref, *rest):
    *piece_refs, out_ref = rest
    edge = diag_ref.shape[1]
    near = [
        dot(diag_ref[b], omega_ref[b * edge : (b + 1) * edge, :]) for b in range(diag_ref.shape[0])
    ]
    total = jnp.concatenate(near, axis=0)
    for piece_ref in piece_refs:
        total += piece_ref[...].astype(jnp.float32)
    out_ref[...] = total


def base_sum(diag, sketch, pieces):
    block_rows, edge, _ = diag.shape
    height, columns = sketch.shape
    together = math.gcd(block_rows, 2)
    rows = pl.BlockSpec((together * edge, columns), lambda b: (b, 0))
    return pl.pallas_call(
        base_kernel,
        out_shape=jax.ShapeDtypeStruct((height, columns), jnp.float32),
        grid=(block_rows // together,),
        in_specs=[pl.BlockSpec((together, edge, edge), lambda b: (b, 0, 0)), rows]
        + [rows] * len(pieces),
        out_specs=rows,
        compiler_params=params(),
        cost_estimate=COST,
        name="base",
    )(diag, sketch, *pieces)


def image_kernel(scale, chip_ref, base_ref, far_ref, *rest):
    *piece_refs, image_ref, gram_ref, cross, bases, fars, pieces, images, sems, out_sem = rest
    chips, (tiles, tile, _) = far_ref.shape[0], bases.shape
    from_chips = [lax.rem(chip_ref[0] + step, chips) for step in range(1, chips)]
    waits = []
    for t in range(tiles):
        rows = pl.ds(t * tile, tile)
        pairs = [(base_ref.at[rows, :], bases.at[t])]
        pairs += [(far_ref.at[chip, rows, :], fars.at[t, i]) for i, chip in enumerate(from_chips)]
        pairs += [(ref.at[rows, :], pieces.at[t, i]) for i, ref in enumerate(piece_refs)]
        waits.append([pltpu.make_async_copy(a, b, sems.at[t, i]) for i, (a, b) in enumerate(pairs)])
        for move in waits[-1]:
            move.start()
    gram_ref[...] = jnp.zeros_like(gram_ref)
    cross[...] = jnp.zeros_like(cross)
    leave = []
    for t in range(tiles):
        for move in waits[t]:
            move.wait()
        image = bases[t]
        for i in range(len(piece_refs)):
            image += pieces[t, i].astype(jnp.float32)
        for i in range(chips - 1):
            image += fars[t, i].astype(jnp.float32)
        images[t] = image
        leave.append(
            pltpu.make_async_copy(
                images.at[t], image_ref.at[pl.ds(t * tile, tile), :], out_sem.at[t]
            )
        )
        leave[-1].start()
        high, low = split(image)
        gram_ref[...] += dot(high, high, TN)
        cross[...] += dot(high, low, TN)
    gram_ref[...] = (gram_ref[...] + (cross[...] + cross[...].T)) * scale
    for move in leave:
        move.wait()


def image_and_gram(base, chip, far, pieces, total_rows):
    height, columns = base.shape
    tile = math.gcd(height, 256)
    tiles, chips = height // tile, far.shape[0]
    anywhere = pl.BlockSpec(memory_space=pl.ANY)
    return pl.pallas_call(
        functools.partial(image_kernel, 1.0 / total_rows),
        out_shape=(
            jax.ShapeDtypeStruct((height, columns), jnp.float32),
            jax.ShapeDtypeStruct((columns, columns), jnp.float32),
        ),
        grid_spec=pltpu.PrefetchScalarGridSpec(
            num_scalar_prefetch=1,
            grid=(),
            in_specs=[anywhere] * (2 + len(pieces)),
            out_specs=(anywhere, pl.BlockSpec(memory_space=pltpu.VMEM)),
            scratch_shapes=[
                pltpu.VMEM((columns, columns), jnp.float32),
                pltpu.VMEM((tiles, tile, columns), jnp.float32),
                pltpu.VMEM((tiles, max(1, chips - 1), tile, columns), far.dtype),
                pltpu.VMEM((tiles, len(pieces), tile, columns), pieces[0].dtype),
                pltpu.VMEM((tiles, tile, columns), jnp.float32),
                pltpu.SemaphoreType.DMA((tiles, chips + len(pieces))),
                pltpu.SemaphoreType.DMA((tiles,)),
            ],
        ),
        compiler_params=params(VMEM_ALL),
        cost_estimate=COST,
        name="image",
    )(chip.reshape(1), base, far, *pieces)


def factor_kernel(rounds, gram_ref, image_ref, basis_ref, factor_ref, inverse, work, images, tile_sem, bases, out_sem):
    n = gram_ref.shape[0]
    tiles, tile, _ = images.shape
    arrive = [
        pltpu.make_async_copy(image_ref.at[pl.ds(t * tile, tile), :], images.at[t], tile_sem.at[t])
        for t in range(tiles)
    ]
    for move in arrive:
        move.start()

    gram = gram_ref[...]
    row = lax.broadcasted_iota(jnp.int32, (n, n), 0)
    col = lax.broadcasted_iota(jnp.int32, (n, n), 1)
    weight = jnp.where(row > col, 1.0, jnp.where(row == col, 0.5, 0.0))
    one = jnp.where(row == col, 1.0, 0.0)
    diagonal = jnp.where(row == col, gram, 0.0)
    down = lax.rsqrt(jnp.sum(diagonal, axis=1, keepdims=True))
    across = lax.rsqrt(jnp.sum(diagonal, axis=0, keepdims=True))
    scaled = gram * down * across
    scaled3 = split(scaled)
    guess = one - weight * (scaled - one)
    for _ in range(rounds):
        guess3 = split(guess)
        error = dot3(split(dot3(guess3, scaled3)), guess3, NT) - one
        guess = guess - dot3(split(weight * error), guess3)
    guess = jnp.where(row >= col, guess, 0.0) * across
    inverse[...] = guess
    factor_ref[...] = jnp.where(row <= col, dot3(split(guess), split(gram)), 0.0)
    size = jnp.sum(error * error)

    @pl.when(jnp.logical_not(size < 1e-6))
    def _():
        exact = lax.Precision.HIGHEST
        work[...] = gram
        inverse[...] = one
        lane = lax.broadcasted_iota(jnp.int32, (1, n), 1)

        def eliminate(j, carry):
            line = work[pl.ds(j, 1), :]
            pivot = jnp.sum(jnp.where(lane == j, line, 0.0), axis=1, keepdims=True)
            scale = lax.rsqrt(pivot)
            line = jnp.where(lane >= j, line * scale, 0.0)
            other = inverse[pl.ds(j, 1), :] * scale
            below = jnp.where(lane > j, line, 0.0)
            work[...] -= dot(below, line, TN, exact)
            inverse[...] -= dot(below, other, TN, exact)
            inverse[pl.ds(j, 1), :] = other
            factor_ref[pl.ds(j, 1), :] = line
            return carry

        lax.fori_loop(0, n, eliminate, 0)

    inverse3 = split(inverse[...])
    leave = []
    for t in range(tiles):
        arrive[t].wait()
        bases[t] = dot3(split(images[t]), inverse3, NT)
        leave.append(
            pltpu.make_async_copy(bases.at[t], basis_ref.at[pl.ds(t * tile, tile), :], out_sem.at[t])
        )
        leave[-1].start()
    for move in leave:
        move.wait()


def factor_and_basis(gram, image, rounds=3):
    height, n = image.shape
    tile = math.gcd(height, 256)
    tiles = height // tile
    square, anywhere = pl.BlockSpec(memory_space=pltpu.VMEM), pl.BlockSpec(memory_space=pl.ANY)
    held = pltpu.VMEM((tiles, tile, n), jnp.float32)
    return pl.pallas_call(
        functools.partial(factor_kernel, rounds),
        out_shape=(
            jax.ShapeDtypeStruct((height, n), jnp.float32),
            jax.ShapeDtypeStruct((n, n), jnp.float32),
        ),
        in_specs=[square, anywhere],
        out_specs=(anywhere, square),
        scratch_shapes=[pltpu.VMEM((n, n), jnp.float32)] * 2
        + [held, pltpu.SemaphoreType.DMA((tiles,))] * 2,
        compiler_params=params(VMEM_ALL),
        cost_estimate=COST,
        name="factor",
    )(gram, image)


def sum_over_devices(part, peers):
    rows, columns = part.shape
    pieces = lax.all_to_all(part.reshape(peers, rows // peers, columns), ALL, 0, 0, tiled=True)
    mine = jnp.broadcast_to(jnp.sum(pieces, axis=0), pieces.shape)
    return lax.all_to_all(mine, ALL, 0, 0, tiled=True).reshape(rows, columns)


def on_device(diag_blocks, off_blocks, col_blocks, sketch):
    block_rows, per_row = col_blocks.shape
    edge = diag_blocks.shape[1]
    layers = lax.axis_size(LINE)
    planes = lax.axis_size(PLANE)
    peers = layers * planes
    requests = block_rows * per_row
    most = max(2, (2 * requests + peers - 1) // peers)
    slots = layers * most
    layer = lax.axis_index(LINE)
    shifts = sorted(range(layers), key=lambda shift: -min(shift, layers - shift))
    cut = 1
    groups = [group for group in (shifts[:cut], shifts[cut:-1], shifts[-1:]) if group]
    flat = col_blocks.reshape(requests)
    owners = flat // block_rows
    order = jnp.arange(requests)
    earlier = (owners[:, None] == owners[None, :]) & (order[None, :] < order[:, None])
    ranks = jnp.sum(earlier.astype(jnp.int32), axis=1)
    to_plane = owners % planes
    away = lax.rem(owners // planes - layer + layers, layers)
    turn = sum(jnp.where(away == shift, index, 0) for index, shift in enumerate(shifts))
    to_slot = turn * most + ranks
    place = to_plane * slots + to_slot
    hit = place[:, None] == jnp.arange(planes * slots)[None, :]
    row_label = block_rows + jnp.sum(
        jnp.where(hit, (order // per_row - block_rows)[:, None], 0), axis=0
    )
    col_label = block_rows + jnp.sum(
        jnp.where(hit, (flat % block_rows - block_rows)[:, None], 0), axis=0
    )
    labels = jnp.stack([row_label.reshape(planes, slots), col_label.reshape(planes, slots)], axis=1)
    labels = jnp.pad(labels, ((0, 0), (0, TAIL - 2), (0, edge - slots))).astype(jnp.bfloat16)
    sizes = [len(group) * most for group in groups]
    ends = [sum(sizes[: index + 1]) for index in range(len(sizes))]
    in_part = sum((to_slot >= end).astype(jnp.int32) for end in ends)
    begins = sum(jnp.where(in_part == index + 1, end, 0) for index, end in enumerate(ends))
    before = jnp.sum(
        (in_part[None, :] < in_part[:, None])
        | ((in_part[None, :] == in_part[:, None]) & (order[None, :] < order[:, None])),
        axis=1,
    )
    pick = before[None, :] == order[:, None]
    route = [
        jnp.sum(jnp.where(pick, values[None, :], 0), axis=1)
        for values in (order, to_plane, to_slot - begins)
    ]
    counts = jnp.sum(in_part[None, :] < jnp.arange(len(sizes) + 1)[:, None], axis=1)
    outgoing = list(
        pack(off_blocks.reshape(requests, edge, edge), route + [counts], labels, sizes)
    )

    def planes_off(k):
        return [(z, z - k) for z in range(k, layers)], [(z, z + k) for z in range(layers - k)]

    down, up = planes_off(1)
    above, below = lax.ppermute(sketch, LINE, down), lax.ppermute(sketch, LINE, up)
    by_line = [(above, below)]
    early_lines = [above, below]
    if layers > 2:
        by_line.append((lax.ppermute(above, LINE, down), lax.ppermute(below, LINE, up)))
        both = lax.ppermute(sketch, LINE, sum(planes_off(3), []))
        by_line.append((both, both))
        early_lines.append(both)
    line_omegas = [
        (by_line[shift - 1][0], by_line[layers - shift - 1][1], (layer + shift < layers).astype(jnp.int32))
        for shift in shifts[:-1]
    ]
    chip, core = lax.axis_index(CHIPS), lax.axis_index(CORE)
    if [lax.axis_size(axis) for axis in PLANE] == [2, 2, 2]:
        swap = [(0, 1), (1, 0)]
        by_x, by_y = (lax.ppermute(sketch, axis, swap) for axis in CHIPS)
        half = sketch.shape[0] // 2
        across = [
            lax.ppermute(by_y[:half], CHIPS[0], swap),
            lax.ppermute(by_x[half:], CHIPS[1], swap),
        ]
        outgoing[0] = hold(outgoing[0], [by_x, by_y])
        mine = join([sketch, by_y, by_x] + across)
        plane_omegas = [
            array.reshape((4,) + sketch.shape) for array in (mine, lax.ppermute(mine, CORE, swap))
        ]
        near_chips = (chip ^ jnp.arange(4)) * 2
        sources = jnp.concatenate([near_chips + core, near_chips + 1 - core])
    else:
        plane_omegas = [lax.all_gather(sketch, PLANE)]
        sources = jnp.arange(planes)
    outgoing[1] = hold(outgoing[1], early_lines)
    parts = [lax.all_to_all(part, PLANE, 0, 0, tiled=True) for part in outgoing[:-1]]
    lines = sizes[0] * edge
    rows = parts[0][:, lines, :slots].astype(jnp.int32)
    cols = parts[0][:, lines + 1, :slots].astype(jnp.int32)

    def send_mirror(index, after):
        part = sum(index * most >= end for end in ends)
        inside = index - (ends[part] - sizes[part]) // most
        shift = shifts[index]
        mirror = plane_sum(
            parts[part],
            plane_omegas,
            sources,
            rows,
            cols,
            inside,
            index * most,
            most,
            block_rows,
            jnp.bfloat16,
            True,
            after,
        )
        steps = [(z, (z + shift) % layers) for z in range(layers)]
        return lax.ppermute(mirror, LINE, steps), (mirror,)

    first, latest = send_mirror(0, ())

    home_rows = row_label.reshape(planes, slots)[:, -most:]
    home_cols = col_label.reshape(planes, slots)[:, -most:]
    cores = lax.axis_size(CORE)
    chips = planes // cores
    away = (chip + jnp.arange(1, chips)) % chips
    at_home = (home_rows, home_cols, outgoing[-1], sketch)
    far = functools.partial(far_sum, rows=rows, cols=cols, most=most, block_rows=block_rows)
    everything = dict(begin=0, parts=parts, omegas=line_omegas, home=at_home)
    early = dict(begin=0, parts=parts[:1], omegas=line_omegas[:1], home=at_home)
    late = dict(begin=sizes[0], parts=parts[1:], omegas=line_omegas[1:], home=None)

    def ask(chips_asked, dtype, what, after):
        if cores == 1:
            return [], after
        count = chips_asked.shape[0]
        other = far(
            chips_asked * cores + 1 - core, jnp.arange(count), count, dtype=dtype, after=after, **what
        )
        return [lax.ppermute(other, CORE, [(0, 1), (1, 0)])], (other,)

    other, latest = ask(away, jnp.float32, early, latest)
    home = plane_sum(
        outgoing[-1],
        plane_omegas,
        sources,
        home_rows,
        home_cols,
        0,
        0,
        most,
        block_rows,
        jnp.float32,
        False,
        latest,
    )
    begun = far(
        away * cores + core,
        jnp.arange(chips - 1),
        chips - 1,
        dtype=jnp.float32,
        adds=other,
        after=(home,),
        **early,
    )
    other, latest = ask(away, jnp.bfloat16, late, (begun,))
    second, latest = send_mirror(1, latest)
    sent = far(
        away * cores + core, away, chips, dtype=jnp.bfloat16, adds=[begun] + other, after=latest, **late
    )
    received = lax.all_to_all(sent, CHIPS, 0, 0, tiled=True)
    pieces, latest = [second], (sent,)
    for index in range(2, layers - 1):
        piece, latest = send_mirror(index, latest)
        pieces.append(piece)
    other, _ = ask(chip.reshape(1), jnp.float32, everything, (sent,))
    own = far(
        chip.reshape(1) * cores + core,
        jnp.arange(1),
        1,
        dtype=jnp.float32,
        adds=other,
        after=latest,
        **everything,
    )
    base = base_sum(diag_blocks, sketch, [home, own.reshape(sketch.shape), first])
    image, part = image_and_gram(base, chip, received, pieces, block_rows * edge * peers)
    gram = sum_over_devices(part, peers)
    return factor_and_basis(gram, image)


def solution(mesh):
    rows, sub = mesh.devices.shape
    layers, cores = math.gcd(rows, 4), math.gcd(sub, 2)
    devices = mesh.devices.reshape(layers, rows // layers, sub // cores, cores)
    placed = (P(ALL, None, None), P(ALL, None, None, None), P(ALL, None), P(ALL, None))
    return jax.shard_map(
        on_device,
        mesh=Mesh(devices, ALL),
        in_specs=placed,
        out_specs=(P(ALL, None), P()),
        check_vma=False,
    )
```

```python
import functools
import math

import jax
import jax.numpy as jnp
from jax import lax
from jax.experimental import pallas as pl
from jax.experimental.pallas import tpu as pltpu
from jax.sharding import Mesh
from jax.sharding import PartitionSpec as P

LINE = "z"
PLANE = ("x", "y", "c")
ALL = (LINE,) + PLANE
CHIPS, CORE = PLANE[:2], PLANE[2]
VMEM_LIMIT = 48 * 1024 * 1024
VMEM_ALL = 60 * 1024 * 1024
COST = pl.CostEstimate(flops=10**12, bytes_accessed=10**11, transcendentals=0)
TAIL = 16


def dot(a, b, contract=((1,), (0,)), precision=None):
    return lax.dot_general(
        a, b, (contract, ((), ())), precision=precision, preferred_element_type=jnp.float32
    )


NT = ((1,), (1,))
TN = ((0,), (0,))


def params(limit=VMEM_LIMIT):
    return pltpu.CompilerParams(vmem_limit_bytes=limit)


def split(a):
    high = a.astype(jnp.bfloat16)
    return high, (a - high.astype(jnp.float32)).astype(jnp.bfloat16)

def dot3(a, b, contract=((1,), (0,))):
    (ah, al), (bh, bl) = a, b
    return dot(ah, bh, contract) + (dot(ah, bl, contract) + dot(al, bh, contract))

def pack_kernel(entry_ref, plane_ref, slot_ref, count_ref, off_ref, label_ref, *rest):
    *out_refs, sem, label_sem = rest
    _, edge, _ = off_ref.shape
    tail = label_ref.shape[1]
    first = out_refs[0]
    labels = pltpu.make_async_copy(
        label_ref, first.at[:, pl.ds(first.shape[1] - tail, tail), :], label_sem
    )
    labels.start()
    for part, out_ref in enumerate(out_refs):

        def send(place, carry, out_ref=out_ref):
            row = pl.multiple_of(slot_ref[place] * edge, edge)
            pltpu.make_async_copy(
                off_ref.at[entry_ref[place]], out_ref.at[plane_ref[place], pl.ds(row, edge), :], sem
            ).start()
            return carry

        lax.fori_loop(count_ref[part], count_ref[part + 1], send, 0)
    pltpu.make_async_copy(off_ref, off_ref, sem).wait()
    labels.wait()


def pack(off, route, labels, parts):
    count, edge, _ = off.shape
    planes, tail, _ = labels.shape
    lengths = [slots * edge + (tail if index == 0 else 0) for index, slots in enumerate(parts)]
    anywhere = pl.BlockSpec(memory_space=pl.ANY)
    return pl.pallas_call(
        pack_kernel,
        out_shape=[jax.ShapeDtypeStruct((planes, length, edge), off.dtype) for length in lengths],
        grid_spec=pltpu.PrefetchScalarGridSpec(
            num_scalar_prefetch=len(route),
            grid=(),
            in_specs=[pl.BlockSpec(memory_space=pltpu.VMEM), anywhere],
            out_specs=[anywhere] * len(parts),
            scratch_shapes=[pltpu.SemaphoreType.DMA, pltpu.SemaphoreType.DMA],
        ),
        compiler_params=params(VMEM_ALL),
        cost_estimate=COST,
        name="pack",
    )(*route, off, labels)


def hold_kernel(x_ref, *rest):
    del x_ref, rest


def hold(x, after):
    anywhere = pl.BlockSpec(memory_space=pl.ANY)
    return pl.pallas_call(
        hold_kernel,
        out_shape=jax.ShapeDtypeStruct(x.shape, x.dtype),
        in_specs=[anywhere] * (1 + len(after)),
        out_specs=anywhere,
        input_output_aliases={0: 0},
        cost_estimate=COST,
        name="hold",
    )(x, *after)


def join_kernel(*refs):
    count = (len(refs) - 2) // 2
    in_refs, out_ref, held, sems = refs[:count], refs[count], refs[count + 1], refs[count + 2 :]
    begin, moves = 0, []
    for in_ref, sem in zip(in_refs, sems, strict=True):
        rows = pl.ds(begin, in_ref.shape[0])
        moves.append((rows, pltpu.make_async_copy(in_ref, held.at[rows, :], sem), sem))
        moves[-1][1].start()
        begin += in_ref.shape[0]
    out = []
    for rows, move, sem in moves:
        move.wait()
        out.append(pltpu.make_async_copy(held.at[rows, :], out_ref.at[rows, :], sem))
        out[-1].start()
    for move in out:
        move.wait()


def join(arrays):
    shape = (sum(array.shape[0] for array in arrays), arrays[0].shape[1])
    anywhere = pl.BlockSpec(memory_space=pl.ANY)
    return pl.pallas_call(
        join_kernel,
        out_shape=jax.ShapeDtypeStruct(shape, arrays[0].dtype),
        in_specs=[anywhere] * len(arrays),
        out_specs=anywhere,
        scratch_shapes=[pltpu.VMEM(shape, arrays[0].dtype)] + [pltpu.SemaphoreType.DMA] * len(arrays),
        compiler_params=params(VMEM_ALL),
        cost_estimate=COST,
        name="join",
    )(*arrays)


def halves_kernel(y_ref, x_ref, first_ref, second_ref, held, sems):
    half = first_ref.shape[0]
    first = pltpu.make_async_copy(y_ref.at[pl.ds(0, half), :], held.at[0], sems.at[0])
    second = pltpu.make_async_copy(x_ref.at[pl.ds(half, half), :], held.at[1], sems.at[1])
    first.start()
    second.start()
    first.wait()
    first = pltpu.make_async_copy(held.at[0], first_ref, sems.at[0])
    first.start()
    second.wait()
    second = pltpu.make_async_copy(held.at[1], second_ref, sems.at[1])
    second.start()
    first.wait()
    second.wait()


def halves(by_y, by_x):
    height, columns = by_y.shape
    anywhere = pl.BlockSpec(memory_space=pl.ANY)
    return pl.pallas_call(
        halves_kernel,
        out_shape=[jax.ShapeDtypeStruct((height // 2, columns), by_y.dtype)] * 2,
        in_specs=[anywhere] * 2,
        out_specs=[anywhere] * 2,
        scratch_shapes=[
            pltpu.VMEM((2, height // 2, columns), by_y.dtype),
            pltpu.SemaphoreType.DMA((2,)),
        ],
        compiler_params=params(VMEM_ALL),
        cost_estimate=COST,
        name="halves",
    )(by_y, by_x)


def plane_kernel(inside, begin, most, counts, mirrored, source_ref, row_ref, col_ref, *rest):
    block_ref, *omega_refs = rest[: 1 + len(counts)]
    out_ref, total, blocks, omegas, block_sem, omega_sem = rest[-6:]
    edge = blocks.shape[2]
    spare = total.shape[0] - 1
    places = [(omega_ref, k) for omega_ref, count in zip(omega_refs, counts) for k in range(count)]
    moves = []
    for step, (omega_ref, k) in enumerate(places):
        rows = pl.ds(inside * most * edge, most * edge)
        moves.append(
            (
                pltpu.make_async_copy(
                    block_ref.at[source_ref[step], rows, :], blocks.at[step], block_sem.at[step]
                ),
                pltpu.make_async_copy(omega_ref.at[k], omegas.at[step], omega_sem.at[step]),
            )
        )
        for move in moves[-1]:
            move.start()
    total[...] = jnp.zeros_like(total)
    for step in range(len(places)):
        source = source_ref[step]
        for move in moves[step]:
            move.wait()
        for m in range(most):
            row = row_ref[source, begin + m]
            col = col_ref[source, begin + m]
            here, there = (row, col) if mirrored else (col, row)
            here = pl.multiple_of(jnp.minimum(here, spare - 1) * edge, edge)
            block = blocks[step, m * edge : (m + 1) * edge, :]
            omega = omegas[step, pl.ds(here, edge), :]
            if mirrored:
                product = dot(block, omega, TN).astype(jnp.bfloat16).astype(jnp.float32)
            else:
                product = dot(block, omega)
            total[there] += product
    out_ref[...] = total[:spare].reshape(out_ref.shape).astype(out_ref.dtype)


def plane_sum(
    blocks, omegas, sources, rows, cols, inside, begin, most, block_rows, dtype, mirrored, after=()
):
    planes, _, edge = blocks.shape
    _, height, columns = omegas[0].shape
    counts = [omega.shape[0] for omega in omegas]
    anywhere = pl.BlockSpec(memory_space=pl.ANY)
    return pl.pallas_call(
        functools.partial(plane_kernel, inside, begin, most, counts, mirrored),
        out_shape=jax.ShapeDtypeStruct((height, columns), dtype),
        grid_spec=pltpu.PrefetchScalarGridSpec(
            num_scalar_prefetch=3,
            grid=(),
            in_specs=[anywhere] * (1 + len(omegas) + len(after)),
            out_specs=pl.BlockSpec(memory_space=pltpu.VMEM),
            scratch_shapes=[
                pltpu.VMEM((block_rows + 1, edge, columns), jnp.float32),
                pltpu.VMEM((planes, most * edge, edge), blocks.dtype),
                pltpu.VMEM((planes, height, columns), omegas[0].dtype),
                pltpu.SemaphoreType.DMA((planes,)),
                pltpu.SemaphoreType.DMA((planes,)),
            ],
        ),
        compiler_params=params(VMEM_ALL),
        cost_estimate=COST,
        name="mirror" if mirrored else "home",
    )(sources, rows, cols, blocks, *omegas, *after)


def far_kernel(most, begin, sizes, lines, added, at_home, *refs):
    source_ref, place_ref, above_ref, row_ref, col_ref, home_row_ref, home_col_ref, *refs = refs
    part_refs, refs = refs[: len(sizes)], refs[len(sizes) :]
    omega_refs, refs = refs[: 2 * lines], refs[2 * lines :]
    home_refs, refs = refs[: 2 * at_home], refs[2 * at_home :]
    add_refs = refs[:added]
    scratch = refs[len(refs) - 7 - len(sizes) - added - 2 * at_home :]
    out_ref, total, omegas, omega_sem, outs, out_sem, sems, *held = scratch
    blocks, adds, homes = held[: len(sizes)], held[len(sizes) : len(sizes) + added], held[len(sizes) + added :]
    edge = total.shape[1]
    spare = total.shape[0] - 1
    count, depth = source_ref.shape[0], outs.shape[0]

    def arrive(k):
        slot, source = k % depth, source_ref[k]
        pairs = [
            (part_ref.at[source, pl.ds(0, size * edge), :], block.at[slot])
            for part_ref, size, block in zip(part_refs, sizes, blocks)
        ]
        if at_home:
            pairs.append((home_refs[0].at[source], homes[0].at[slot]))
        pairs += [(add_ref.at[k], add.at[slot]) for add_ref, add in zip(add_refs, adds)]
        return [pltpu.make_async_copy(a, b, sems.at[slot, i]) for i, (a, b) in enumerate(pairs)]

    def leave(k):
        slot = k % depth
        return pltpu.make_async_copy(outs.at[slot], out_ref.at[place_ref[k]], out_sem.at[slot])

    lead = [
        [
            pltpu.make_async_copy(omega_ref, omegas.at[index], omega_sem.at[index])
            for omega_ref in omega_refs[2 * index : 2 * index + 2]
        ]
        for index in range(lines)
    ]
    if at_home:
        own = pltpu.make_async_copy(home_refs[1], homes[1], omega_sem.at[lines])
    for k in range(min(depth, count)):
        for move in arrive(k):
            move.start()
        if k == 0:
            if at_home:
                own.start()
            for index, (above, below) in enumerate(lead):
                pl.when(above_ref[index] == 1)(above.start)
                pl.when(above_ref[index] == 0)(below.start)
    for k in range(count):
        slot, source = k % depth, source_ref[k]
        for move in arrive(k):
            move.wait()
        total[...] = jnp.zeros_like(total)
        if at_home:
            if k == 0:
                own.wait()
            for place in range(most):
                row = jnp.minimum(home_row_ref[source, place], spare - 1)
                row = pl.multiple_of(row * edge, edge)
                block = homes[0][slot, place * edge : (place + 1) * edge, :]
                product = dot(block, homes[1][pl.ds(row, edge), :], TN).astype(jnp.bfloat16)
                total[home_col_ref[source, place]] += product.astype(jnp.float32)
        index = 0
        for block_ref, size in zip(blocks, sizes):
            for place in range(size):
                line = index // most
                if k == 0 and index % most == 0:
                    lead[line][0].wait()
                row = row_ref[source, begin + index]
                col = jnp.minimum(col_ref[source, begin + index], spare - 1)
                block = block_ref[slot, place * edge : (place + 1) * edge, :]
                total[row] += dot(block, omegas[line, pl.ds(pl.multiple_of(col * edge, edge), edge), :])
                index += 1
        if k >= depth:
            leave(k - depth).wait()
        result = total[:spare].reshape(outs.shape[1:])
        for add in adds:
            result += add[slot].astype(jnp.float32)
        outs[slot] = result.astype(outs.dtype)
        leave(k).start()
        if k + depth < count:
            for move in arrive(k + depth):
                move.start()
    for k in range(max(0, count - depth), count):
        leave(k).wait()


def far_sum(
    sources, places, slots, begin, parts, omegas, rows, cols, home, most, block_rows, dtype, adds=(), after=()
):
    edge = parts[0].shape[2]
    height, columns = omegas[0][0].shape
    lines = len(omegas)
    above = jnp.stack([choice for _, _, choice in omegas])
    pairs = [omega for pair in omegas for omega in pair[:2]]
    sizes = [part.shape[1] // (most * edge) * most for part in parts]
    depth = min(3, sources.shape[0])
    home_rows, home_cols, *at_home = home if home else (rows[:, :most], cols[:, :most])
    arrays = [*parts, *pairs, *at_home, *adds, *after]
    anywhere = pl.BlockSpec(memory_space=pl.ANY)
    return pl.pallas_call(
        functools.partial(far_kernel, most, begin, sizes, lines, len(adds), 1 if home else 0),
        out_shape=jax.ShapeDtypeStruct((slots, height, columns), dtype),
        grid_spec=pltpu.PrefetchScalarGridSpec(
            num_scalar_prefetch=7,
            grid=(),
            in_specs=[anywhere] * len(arrays),
            out_specs=anywhere,
            scratch_shapes=[
                pltpu.VMEM((block_rows + 1, edge, columns), jnp.float32),
                pltpu.VMEM((lines, height, columns), pairs[0].dtype),
                pltpu.SemaphoreType.DMA((lines + 1,)),
                pltpu.VMEM((depth, height, columns), dtype),
                pltpu.SemaphoreType.DMA((depth,)),
                pltpu.SemaphoreType.DMA((depth, len(parts) + 1 + len(adds))),
            ]
            + [pltpu.VMEM((depth, size * edge, edge), parts[0].dtype) for size in sizes]
            + [pltpu.VMEM((depth, height, columns), add.dtype) for add in adds]
            + [
                pltpu.VMEM(shape, parts[0].dtype)
                for shape in ([(depth, most * edge, edge), (height, columns)] if home else [])
            ],
        ),
        compiler_params=params(VMEM_ALL),
        cost_estimate=COST,
        name="far",
    )(sources, places, above, rows, cols, home_rows, home_cols, *arrays)


def base_kernel(diag_ref, omega_ref, *rest):
    *piece_refs, out_ref = rest
    edge = diag_ref.shape[1]
    near = [
        dot(diag_ref[b], omega_ref[b * edge : (b + 1) * edge, :]) for b in range(diag_ref.shape[0])
    ]
    total = jnp.concatenate(near, axis=0)
    for piece_ref in piece_refs:
        total += piece_ref[...].astype(jnp.float32)
    out_ref[...] = total


def base_sum(diag, sketch, pieces):
    block_rows, edge, _ = diag.shape
    height, columns = sketch.shape
    together = math.gcd(block_rows, 2)
    rows = pl.BlockSpec((together * edge, columns), lambda b: (b, 0))
    return pl.pallas_call(
        base_kernel,
        out_shape=jax.ShapeDtypeStruct((height, columns), jnp.float32),
        grid=(block_rows // together,),
        in_specs=[pl.BlockSpec((together, edge, edge), lambda b: (b, 0, 0)), rows]
        + [rows] * len(pieces),
        out_specs=rows,
        compiler_params=params(VMEM_ALL),
        cost_estimate=COST,
        name="base",
    )(diag, sketch, *pieces)


def image_kernel(scale, chip_ref, base_ref, far_ref, *rest):
    *piece_refs, image_ref, gram_ref, cross, bases, fars, pieces, images, sems, out_sem = rest
    chips, (tiles, tile, _) = far_ref.shape[0], bases.shape
    from_chips = [lax.rem(chip_ref[0] + step, chips) for step in range(1, chips)]
    waits = []
    for t in range(tiles):
        rows = pl.ds(t * tile, tile)
        pairs = [(base_ref.at[rows, :], bases.at[t])]
        pairs += [(far_ref.at[chip, rows, :], fars.at[t, i]) for i, chip in enumerate(from_chips)]
        pairs += [(ref.at[rows, :], pieces.at[t, i]) for i, ref in enumerate(piece_refs)]
        waits.append([pltpu.make_async_copy(a, b, sems.at[t, i]) for i, (a, b) in enumerate(pairs)])
        for move in waits[-1]:
            move.start()
    gram_ref[...] = jnp.zeros_like(gram_ref)
    cross[...] = jnp.zeros_like(cross)
    leave = []
    for t in range(tiles):
        for move in waits[t]:
            move.wait()
        image = bases[t]
        for i in range(len(piece_refs)):
            image += pieces[t, i].astype(jnp.float32)
        for i in range(chips - 1):
            image += fars[t, i].astype(jnp.float32)
        images[t] = image
        leave.append(
            pltpu.make_async_copy(
                images.at[t], image_ref.at[pl.ds(t * tile, tile), :], out_sem.at[t]
            )
        )
        leave[-1].start()
        high, low = split(image)
        gram_ref[...] += dot(high, high, TN)
        cross[...] += dot(high, low, TN)
    gram_ref[...] = (gram_ref[...] + (cross[...] + cross[...].T)) * scale
    for move in leave:
        move.wait()


def image_and_gram(base, chip, far, pieces, total_rows):
    height, columns = base.shape
    tile = math.gcd(height, 256)
    tiles, chips = height // tile, far.shape[0]
    anywhere = pl.BlockSpec(memory_space=pl.ANY)
    return pl.pallas_call(
        functools.partial(image_kernel, 1.0 / total_rows),
        out_shape=(
            jax.ShapeDtypeStruct((height, columns), jnp.float32),
            jax.ShapeDtypeStruct((columns, columns), jnp.float32),
        ),
        grid_spec=pltpu.PrefetchScalarGridSpec(
            num_scalar_prefetch=1,
            grid=(),
            in_specs=[anywhere] * (2 + len(pieces)),
            out_specs=(anywhere, pl.BlockSpec(memory_space=pltpu.VMEM)),
            scratch_shapes=[
                pltpu.VMEM((columns, columns), jnp.float32),
                pltpu.VMEM((tiles, tile, columns), jnp.float32),
                pltpu.VMEM((tiles, max(1, chips - 1), tile, columns), far.dtype),
                pltpu.VMEM((tiles, len(pieces), tile, columns), pieces[0].dtype),
                pltpu.VMEM((tiles, tile, columns), jnp.float32),
                pltpu.SemaphoreType.DMA((tiles, chips + len(pieces))),
                pltpu.SemaphoreType.DMA((tiles,)),
            ],
        ),
        compiler_params=params(VMEM_ALL),
        cost_estimate=COST,
        name="image",
    )(chip.reshape(1), base, far, *pieces)


def factor_kernel(rounds, gram_ref, image_ref, basis_ref, factor_ref, inverse, work, images, tile_sem, bases, out_sem):
    n = gram_ref.shape[0]
    tiles, tile, _ = images.shape
    arrive = [
        pltpu.make_async_copy(image_ref.at[pl.ds(t * tile, tile), :], images.at[t], tile_sem.at[t])
        for t in range(tiles)
    ]
    for move in arrive:
        move.start()

    gram = gram_ref[...]
    row = lax.broadcasted_iota(jnp.int32, (n, n), 0)
    col = lax.broadcasted_iota(jnp.int32, (n, n), 1)
    weight = jnp.where(row > col, 1.0, jnp.where(row == col, 0.5, 0.0))
    one = jnp.where(row == col, 1.0, 0.0)
    diagonal = jnp.where(row == col, gram, 0.0)
    down = lax.rsqrt(jnp.sum(diagonal, axis=1, keepdims=True))
    across = lax.rsqrt(jnp.sum(diagonal, axis=0, keepdims=True))
    scaled = gram * down * across
    scaled3 = split(scaled)
    guess = one - weight * (scaled - one)
    for _ in range(rounds):
        guess3 = split(guess)
        error = dot3(split(dot3(guess3, scaled3)), guess3, NT) - one
        guess = guess - dot3(split(weight * error), guess3)
    guess = jnp.where(row >= col, guess, 0.0) * across
    inverse[...] = guess
    factor_ref[...] = jnp.where(row <= col, dot3(split(guess), split(gram)), 0.0)
    size = jnp.sum(error * error)

    @pl.when(jnp.logical_not(size < 1e-6))
    def _():
        exact = lax.Precision.HIGHEST
        work[...] = gram
        inverse[...] = one
        lane = lax.broadcasted_iota(jnp.int32, (1, n), 1)

        def eliminate(j, carry):
            line = work[pl.ds(j, 1), :]
            pivot = jnp.sum(jnp.where(lane == j, line, 0.0), axis=1, keepdims=True)
            scale = lax.rsqrt(pivot)
            line = jnp.where(lane >= j, line * scale, 0.0)
            other = inverse[pl.ds(j, 1), :] * scale
            below = jnp.where(lane > j, line, 0.0)
            work[...] -= dot(below, line, TN, exact)
            inverse[...] -= dot(below, other, TN, exact)
            inverse[pl.ds(j, 1), :] = other
            factor_ref[pl.ds(j, 1), :] = line
            return carry

        lax.fori_loop(0, n, eliminate, 0)

    inverse3 = split(inverse[...])
    leave = []
    for t in range(tiles):
        arrive[t].wait()
        bases[t] = dot3(split(images[t]), inverse3, NT)
        leave.append(
            pltpu.make_async_copy(bases.at[t], basis_ref.at[pl.ds(t * tile, tile), :], out_sem.at[t])
        )
        leave[-1].start()
    for move in leave:
        move.wait()


def factor_and_basis(gram, image, rounds=3):
    height, n = image.shape
    tile = math.gcd(height, 256)
    tiles = height // tile
    square, anywhere = pl.BlockSpec(memory_space=pltpu.VMEM), pl.BlockSpec(memory_space=pl.ANY)
    held = pltpu.VMEM((tiles, tile, n), jnp.float32)
    return pl.pallas_call(
        functools.partial(factor_kernel, rounds),
        out_shape=(
            jax.ShapeDtypeStruct((height, n), jnp.float32),
            jax.ShapeDtypeStruct((n, n), jnp.float32),
        ),
        in_specs=[square, anywhere],
        out_specs=(anywhere, square),
        scratch_shapes=[pltpu.VMEM((n, n), jnp.float32)] * 2
        + [held, pltpu.SemaphoreType.DMA((tiles,))] * 2,
        compiler_params=params(VMEM_ALL),
        cost_estimate=COST,
        name="factor",
    )(gram, image)


def sum_over_devices(part, peers):
    rows, columns = part.shape
    pieces = lax.all_to_all(part.reshape(peers, rows // peers, columns), ALL, 0, 0, tiled=True)
    mine = jnp.broadcast_to(jnp.sum(pieces, axis=0), pieces.shape)
    return lax.all_to_all(mine, ALL, 0, 0, tiled=True).reshape(rows, columns)


def on_device(diag_blocks, off_blocks, col_blocks, sketch):
    block_rows, per_row = col_blocks.shape
    edge = diag_blocks.shape[1]
    layers = lax.axis_size(LINE)
    planes = lax.axis_size(PLANE)
    peers = layers * planes
    requests = block_rows * per_row
    most = max(2, (2 * requests + peers - 1) // peers)
    slots = layers * most
    layer = lax.axis_index(LINE)
    shifts = sorted(range(layers), key=lambda shift: -min(shift, layers - shift))
    cut = 1
    groups = [group for group in (shifts[:cut], shifts[cut:-1], shifts[-1:]) if group]
    flat = col_blocks.reshape(requests)
    owners = flat // block_rows
    order = jnp.arange(requests)
    earlier = (owners[:, None] == owners[None, :]) & (order[None, :] < order[:, None])
    ranks = jnp.sum(earlier.astype(jnp.int32), axis=1)
    to_plane = owners % planes
    away = lax.rem(owners // planes - layer + layers, layers)
    turn = sum(jnp.where(away == shift, index, 0) for index, shift in enumerate(shifts))
    to_slot = turn * most + ranks
    place = to_plane * slots + to_slot
    hit = place[:, None] == jnp.arange(planes * slots)[None, :]
    row_label = block_rows + jnp.sum(
        jnp.where(hit, (order // per_row - block_rows)[:, None], 0), axis=0
    )
    col_label = block_rows + jnp.sum(
        jnp.where(hit, (flat % block_rows - block_rows)[:, None], 0), axis=0
    )
    labels = jnp.stack([row_label.reshape(planes, slots), col_label.reshape(planes, slots)], axis=1)
    labels = jnp.pad(labels, ((0, 0), (0, TAIL - 2), (0, edge - slots))).astype(jnp.bfloat16)
    sizes = [len(group) * most for group in groups]
    ends = [sum(sizes[: index + 1]) for index in range(len(sizes))]
    in_part = sum((to_slot >= end).astype(jnp.int32) for end in ends)
    begins = sum(jnp.where(in_part == index + 1, end, 0) for index, end in enumerate(ends))
    before = jnp.sum(
        (in_part[None, :] < in_part[:, None])
        | ((in_part[None, :] == in_part[:, None]) & (order[None, :] < order[:, None])),
        axis=1,
    )
    pick = before[None, :] == order[:, None]
    route = [
        jnp.sum(jnp.where(pick, values[None, :], 0), axis=1)
        for values in (order, to_plane, to_slot - begins)
    ]
    counts = jnp.sum(in_part[None, :] < jnp.arange(len(sizes) + 1)[:, None], axis=1)
    outgoing = list(
        pack(off_blocks.reshape(requests, edge, edge), route + [counts], labels, sizes)
    )

    def planes_off(k):
        return [(z, z - k) for z in range(k, layers)], [(z, z + k) for z in range(layers - k)]

    down, up = planes_off(1)
    above, below = lax.ppermute(sketch, LINE, down), lax.ppermute(sketch, LINE, up)
    by_line = [(above, below)]
    early_lines = [above, below]
    if layers > 2:
        by_line.append((lax.ppermute(above, LINE, down), lax.ppermute(below, LINE, up)))
        both = lax.ppermute(sketch, LINE, sum(planes_off(3), []))
        by_line.append((both, both))
        early_lines.append(both)
    chip, core = lax.axis_index(CHIPS), lax.axis_index(CORE)
    if [lax.axis_size(axis) for axis in PLANE] == [2, 2, 2]:
        swap = [(0, 1), (1, 0)]
        by_x, by_y = (lax.ppermute(sketch, axis, swap) for axis in CHIPS)
        upper, lower = halves(by_y, by_x)
        across = [lax.ppermute(upper, CHIPS[0], swap), lax.ppermute(lower, CHIPS[1], swap)]
        outgoing[0] = hold(outgoing[0], [by_x, by_y])
        mine = join([sketch, by_y, by_x] + across)
        plane_omegas = [
            array.reshape((4,) + sketch.shape) for array in (mine, lax.ppermute(mine, CORE, swap))
        ]
        relative = True
    else:
        plane_omegas = [lax.all_gather(sketch, PLANE)]
        relative = False
    outgoing[1] = hold(outgoing[1], early_lines)
    parts = [lax.all_to_all(part, PLANE, 0, 0, tiled=True) for part in outgoing[:-1]]
    lines = sizes[0] * edge
    rows = parts[0][:, lines, :slots].astype(jnp.int32)
    cols = parts[0][:, lines + 1, :slots].astype(jnp.int32)

    layer, chip, core, row_label, col_label, rows, cols = lax.optimization_barrier(
        (layer, chip, core, row_label, col_label, rows, cols)
    )
    line_omegas = [
        (by_line[shift - 1][0], by_line[layers - shift - 1][1], (layer + shift < layers).astype(jnp.int32))
        for shift in shifts[:-1]
    ]
    sources = jnp.arange(planes)
    if relative:
        near_chips = (chip ^ jnp.arange(4)) * 2
        sources = jnp.concatenate([near_chips + core, near_chips + 1 - core])
    def send_mirror(index, after):
        part = sum(index * most >= end for end in ends)
        inside = index - (ends[part] - sizes[part]) // most
        shift = shifts[index]
        mirror = plane_sum(
            parts[part],
            plane_omegas,
            sources,
            rows,
            cols,
            inside,
            index * most,
            most,
            block_rows,
            jnp.bfloat16,
            True,
            after,
        )
        steps = [(z, (z + shift) % layers) for z in range(layers)]
        return lax.ppermute(mirror, LINE, steps), (mirror,)

    first, latest = send_mirror(0, ())

    home_rows = row_label.reshape(planes, slots)[:, -most:]
    home_cols = col_label.reshape(planes, slots)[:, -most:]
    cores = lax.axis_size(CORE)
    chips = planes // cores
    away = (chip + jnp.arange(1, chips)) % chips
    at_home = (home_rows, home_cols, outgoing[-1], sketch)
    far = functools.partial(far_sum, rows=rows, cols=cols, most=most, block_rows=block_rows)
    everything = dict(begin=0, parts=parts, omegas=line_omegas, home=at_home)
    early = dict(begin=0, parts=parts[:1], omegas=line_omegas[:1], home=at_home)
    late = dict(begin=sizes[0], parts=parts[1:], omegas=line_omegas[1:], home=None)

    def ask(chips_asked, dtype, what, after):
        if cores == 1:
            return [], after
        count = chips_asked.shape[0]
        other = far(
            chips_asked * cores + 1 - core, jnp.arange(count), count, dtype=dtype, after=after, **what
        )
        return [lax.ppermute(other, CORE, [(0, 1), (1, 0)])], (other,)

    other, latest = ask(away, jnp.float32, early, latest)
    home = plane_sum(
        outgoing[-1],
        plane_omegas,
        sources,
        home_rows,
        home_cols,
        0,
        0,
        most,
        block_rows,
        jnp.float32,
        False,
        latest,
    )
    begun = far(
        away * cores + core,
        jnp.arange(chips - 1),
        chips - 1,
        dtype=jnp.float32,
        adds=other,
        after=(home,),
        **early,
    )
    other, latest = ask(away, jnp.bfloat16, late, (begun,))
    second, latest = send_mirror(1, latest)
    sent = far(
        away * cores + core, away, chips, dtype=jnp.bfloat16, adds=[begun] + other, after=latest, **late
    )
    received = lax.all_to_all(sent, CHIPS, 0, 0, tiled=True)
    pieces, latest = [second], (sent,)
    for index in range(2, layers - 1):
        piece, latest = send_mirror(index, latest)
        pieces.append(piece)
    other, _ = ask(chip.reshape(1), jnp.float32, everything, (sent,))
    own = far(
        chip.reshape(1) * cores + core,
        jnp.arange(1),
        1,
        dtype=jnp.float32,
        adds=other,
        after=latest,
        **everything,
    )
    base = base_sum(diag_blocks, sketch, [home, own.reshape(sketch.shape), first])
    image, part = image_and_gram(base, chip, received, pieces, block_rows * edge * peers)
    gram = sum_over_devices(part, peers)
    return factor_and_basis(gram, image)


def solution(mesh):
    rows, sub = mesh.devices.shape
    layers, cores = math.gcd(rows, 4), math.gcd(sub, 2)
    devices = mesh.devices.reshape(layers, rows // layers, sub // cores, cores)
    placed = (P(ALL, None, None), P(ALL, None, None, None), P(ALL, None), P(ALL, None))
    return jax.shard_map(
        on_device,
        mesh=Mesh(devices, ALL),
        in_specs=placed,
        out_specs=(P(ALL, None), P()),
        check_vma=False,
    )
```

```python
import functools
import math

import jax
import jax.numpy as jnp
from jax import lax
from jax.experimental import pallas as pl
from jax.experimental.pallas import tpu as pltpu
from jax.sharding import Mesh
from jax.sharding import PartitionSpec as P

LINE = "z"
PLANE = ("x", "y", "c")
ALL = (LINE,) + PLANE
CHIPS, CORE = PLANE[:2], PLANE[2]
VMEM_LIMIT = 48 * 1024 * 1024
VMEM_ALL = 60 * 1024 * 1024
COST = pl.CostEstimate(flops=10**12, bytes_accessed=10**11, transcendentals=0)
TAIL = 16


def dot(a, b, contract=((1,), (0,)), precision=None):
    return lax.dot_general(
        a, b, (contract, ((), ())), precision=precision, preferred_element_type=jnp.float32
    )


NT = ((1,), (1,))
TN = ((0,), (0,))


def params(limit=VMEM_LIMIT):
    return pltpu.CompilerParams(vmem_limit_bytes=limit)


def split(a):
    high = a.astype(jnp.bfloat16)
    return high, (a - high.astype(jnp.float32)).astype(jnp.bfloat16)

def dot3(a, b, contract=((1,), (0,))):
    (ah, al), (bh, bl) = a, b
    return dot(ah, bh, contract) + (dot(ah, bl, contract) + dot(al, bh, contract))

def pack_kernel(entry_ref, plane_ref, slot_ref, count_ref, off_ref, label_ref, *rest):
    *out_refs, sem, label_sem = rest
    _, edge, _ = off_ref.shape
    tail = label_ref.shape[1]
    first = out_refs[0]
    labels = pltpu.make_async_copy(
        label_ref, first.at[:, pl.ds(first.shape[1] - tail, tail), :], label_sem
    )
    labels.start()
    for part, out_ref in enumerate(out_refs):

        def send(place, carry, out_ref=out_ref):
            row = pl.multiple_of(slot_ref[place] * edge, edge)
            pltpu.make_async_copy(
                off_ref.at[entry_ref[place]], out_ref.at[plane_ref[place], pl.ds(row, edge), :], sem
            ).start()
            return carry

        lax.fori_loop(count_ref[part], count_ref[part + 1], send, 0)
    pltpu.make_async_copy(off_ref, off_ref, sem).wait()
    labels.wait()


def pack(off, route, labels, parts):
    count, edge, _ = off.shape
    planes, tail, _ = labels.shape
    lengths = [slots * edge + (tail if index == 0 else 0) for index, slots in enumerate(parts)]
    anywhere = pl.BlockSpec(memory_space=pl.ANY)
    return pl.pallas_call(
        pack_kernel,
        out_shape=[jax.ShapeDtypeStruct((planes, length, edge), off.dtype) for length in lengths],
        grid_spec=pltpu.PrefetchScalarGridSpec(
            num_scalar_prefetch=len(route),
            grid=(),
            in_specs=[pl.BlockSpec(memory_space=pltpu.VMEM), anywhere],
            out_specs=[anywhere] * len(parts),
            scratch_shapes=[pltpu.SemaphoreType.DMA, pltpu.SemaphoreType.DMA],
        ),
        compiler_params=params(VMEM_ALL),
        cost_estimate=COST,
        name="pack",
    )(*route, off, labels)


def hold_kernel(x_ref, *rest):
    del x_ref, rest


def hold(x, after):
    anywhere = pl.BlockSpec(memory_space=pl.ANY)
    return pl.pallas_call(
        hold_kernel,
        out_shape=jax.ShapeDtypeStruct(x.shape, x.dtype),
        in_specs=[anywhere] * (1 + len(after)),
        out_specs=anywhere,
        input_output_aliases={0: 0},
        cost_estimate=COST,
        name="hold",
    )(x, *after)


def join_kernel(*refs):
    count = (len(refs) - 2) // 2
    in_refs, out_ref, held, sems = refs[:count], refs[count], refs[count + 1], refs[count + 2 :]
    begin, moves = 0, []
    for in_ref, sem in zip(in_refs, sems, strict=True):
        rows = pl.ds(begin, in_ref.shape[0])
        moves.append((rows, pltpu.make_async_copy(in_ref, held.at[rows, :], sem), sem))
        moves[-1][1].start()
        begin += in_ref.shape[0]
    out = []
    for rows, move, sem in moves:
        move.wait()
        out.append(pltpu.make_async_copy(held.at[rows, :], out_ref.at[rows, :], sem))
        out[-1].start()
    for move in out:
        move.wait()


def join(arrays):
    shape = (sum(array.shape[0] for array in arrays), arrays[0].shape[1])
    anywhere = pl.BlockSpec(memory_space=pl.ANY)
    return pl.pallas_call(
        join_kernel,
        out_shape=jax.ShapeDtypeStruct(shape, arrays[0].dtype),
        in_specs=[anywhere] * len(arrays),
        out_specs=anywhere,
        scratch_shapes=[pltpu.VMEM(shape, arrays[0].dtype)] + [pltpu.SemaphoreType.DMA] * len(arrays),
        compiler_params=params(VMEM_ALL),
        cost_estimate=COST,
        name="join",
    )(*arrays)


def halves_kernel(y_ref, x_ref, first_ref, second_ref, held, sems):
    half = first_ref.shape[0]
    first = pltpu.make_async_copy(y_ref.at[pl.ds(0, half), :], held.at[0], sems.at[0])
    second = pltpu.make_async_copy(x_ref.at[pl.ds(half, half), :], held.at[1], sems.at[1])
    first.start()
    second.start()
    first.wait()
    first = pltpu.make_async_copy(held.at[0], first_ref, sems.at[0])
    first.start()
    second.wait()
    second = pltpu.make_async_copy(held.at[1], second_ref, sems.at[1])
    second.start()
    first.wait()
    second.wait()


def halves(by_y, by_x):
    height, columns = by_y.shape
    anywhere = pl.BlockSpec(memory_space=pl.ANY)
    return pl.pallas_call(
        halves_kernel,
        out_shape=[jax.ShapeDtypeStruct((height // 2, columns), by_y.dtype)] * 2,
        in_specs=[anywhere] * 2,
        out_specs=[anywhere] * 2,
        scratch_shapes=[
            pltpu.VMEM((2, height // 2, columns), by_y.dtype),
            pltpu.SemaphoreType.DMA((2,)),
        ],
        compiler_params=params(VMEM_ALL),
        cost_estimate=COST,
        name="halves",
    )(by_y, by_x)


def plane_kernel(inside, begin, most, counts, mirrored, source_ref, row_ref, col_ref, *rest):
    block_ref, *omega_refs = rest[: 1 + len(counts)]
    out_ref, total, blocks, omegas, block_sem, omega_sem = rest[-6:]
    edge = blocks.shape[2]
    spare = total.shape[0] - 1
    places = [(omega_ref, k) for omega_ref, count in zip(omega_refs, counts) for k in range(count)]
    moves = []
    for step, (omega_ref, k) in enumerate(places):
        rows = pl.ds(inside * most * edge, most * edge)
        moves.append(
            (
                pltpu.make_async_copy(
                    block_ref.at[source_ref[step], rows, :], blocks.at[step], block_sem.at[step]
                ),
                pltpu.make_async_copy(omega_ref.at[k], omegas.at[step], omega_sem.at[step]),
            )
        )
        for move in moves[-1]:
            move.start()
    total[...] = jnp.zeros_like(total)
    for step in range(len(places)):
        source = source_ref[step]
        for move in moves[step]:
            move.wait()
        for m in range(most):
            row = row_ref[source, begin + m]
            col = col_ref[source, begin + m]
            here, there = (row, col) if mirrored else (col, row)
            here = pl.multiple_of(jnp.minimum(here, spare - 1) * edge, edge)
            block = blocks[step, m * edge : (m + 1) * edge, :]
            omega = omegas[step, pl.ds(here, edge), :]
            if mirrored:
                product = dot(block, omega, TN).astype(jnp.bfloat16).astype(jnp.float32)
            else:
                product = dot(block, omega)
            total[there] += product
    out_ref[...] = total[:spare].reshape(out_ref.shape).astype(out_ref.dtype)


def plane_sum(
    blocks, omegas, sources, rows, cols, inside, begin, most, block_rows, dtype, mirrored, after=()
):
    planes, _, edge = blocks.shape
    _, height, columns = omegas[0].shape
    counts = [omega.shape[0] for omega in omegas]
    anywhere = pl.BlockSpec(memory_space=pl.ANY)
    return pl.pallas_call(
        functools.partial(plane_kernel, inside, begin, most, counts, mirrored),
        out_shape=jax.ShapeDtypeStruct((height, columns), dtype),
        grid_spec=pltpu.PrefetchScalarGridSpec(
            num_scalar_prefetch=3,
            grid=(),
            in_specs=[anywhere] * (1 + len(omegas) + len(after)),
            out_specs=pl.BlockSpec(memory_space=pltpu.VMEM),
            scratch_shapes=[
                pltpu.VMEM((block_rows + 1, edge, columns), jnp.float32),
                pltpu.VMEM((planes, most * edge, edge), blocks.dtype),
                pltpu.VMEM((planes, height, columns), omegas[0].dtype),
                pltpu.SemaphoreType.DMA((planes,)),
                pltpu.SemaphoreType.DMA((planes,)),
            ],
        ),
        compiler_params=params(VMEM_ALL),
        cost_estimate=COST,
        name="mirror" if mirrored else "home",
    )(sources, rows, cols, blocks, *omegas, *after)


def far_kernel(most, begin, sizes, lines, added, at_home, *refs):
    source_ref, place_ref, above_ref, row_ref, col_ref, home_row_ref, home_col_ref, *refs = refs
    part_refs, refs = refs[: len(sizes)], refs[len(sizes) :]
    omega_refs, refs = refs[: 2 * lines], refs[2 * lines :]
    home_refs, refs = refs[: 2 * at_home], refs[2 * at_home :]
    add_refs = refs[:added]
    scratch = refs[len(refs) - 7 - len(sizes) - added - 2 * at_home :]
    out_ref, total, omegas, omega_sem, outs, out_sem, sems, *held = scratch
    blocks, adds, homes = held[: len(sizes)], held[len(sizes) : len(sizes) + added], held[len(sizes) + added :]
    edge = total.shape[1]
    spare = total.shape[0] - 1
    count, depth = source_ref.shape[0], outs.shape[0]

    def arrive(k):
        slot, source = k % depth, source_ref[k]
        pairs = [
            (part_ref.at[source, pl.ds(0, size * edge), :], block.at[slot])
            for part_ref, size, block in zip(part_refs, sizes, blocks)
        ]
        if at_home:
            pairs.append((home_refs[0].at[source], homes[0].at[slot]))
        pairs += [(add_ref.at[k], add.at[slot]) for add_ref, add in zip(add_refs, adds)]
        return [pltpu.make_async_copy(a, b, sems.at[slot, i]) for i, (a, b) in enumerate(pairs)]

    def leave(k):
        slot = k % depth
        return pltpu.make_async_copy(outs.at[slot], out_ref.at[place_ref[k]], out_sem.at[slot])

    lead = [
        [
            pltpu.make_async_copy(omega_ref, omegas.at[index], omega_sem.at[index])
            for omega_ref in omega_refs[2 * index : 2 * index + 2]
        ]
        for index in range(lines)
    ]
    if at_home:
        own = pltpu.make_async_copy(home_refs[1], homes[1], omega_sem.at[lines])
    for k in range(min(depth, count)):
        for move in arrive(k):
            move.start()
        if k == 0:
            if at_home:
                own.start()
            for index, (above, below) in enumerate(lead):
                pl.when(above_ref[index] == 1)(above.start)
                pl.when(above_ref[index] == 0)(below.start)
    for k in range(count):
        slot, source = k % depth, source_ref[k]
        for move in arrive(k):
            move.wait()
        total[...] = jnp.zeros_like(total)
        if at_home:
            if k == 0:
                own.wait()
            for place in range(most):
                row = jnp.minimum(home_row_ref[source, place], spare - 1)
                row = pl.multiple_of(row * edge, edge)
                block = homes[0][slot, place * edge : (place + 1) * edge, :]
                product = dot(block, homes[1][pl.ds(row, edge), :], TN).astype(jnp.bfloat16)
                total[home_col_ref[source, place]] += product.astype(jnp.float32)
        index = 0
        for block_ref, size in zip(blocks, sizes):
            for place in range(size):
                line = index // most
                if k == 0 and index % most == 0:
                    lead[line][0].wait()
                row = row_ref[source, begin + index]
                col = jnp.minimum(col_ref[source, begin + index], spare - 1)
                block = block_ref[slot, place * edge : (place + 1) * edge, :]
                total[row] += dot(block, omegas[line, pl.ds(pl.multiple_of(col * edge, edge), edge), :])
                index += 1
        if k >= depth:
            leave(k - depth).wait()
        result = total[:spare].reshape(outs.shape[1:])
        for add in adds:
            result += add[slot].astype(jnp.float32)
        outs[slot] = result.astype(outs.dtype)
        leave(k).start()
        if k + depth < count:
            for move in arrive(k + depth):
                move.start()
    for k in range(max(0, count - depth), count):
        leave(k).wait()


def far_sum(
    sources, places, slots, begin, parts, omegas, rows, cols, home, most, block_rows, dtype, adds=(), after=()
):
    edge = parts[0].shape[2]
    height, columns = omegas[0][0].shape
    lines = len(omegas)
    above = jnp.stack([choice for _, _, choice in omegas])
    pairs = [omega for pair in omegas for omega in pair[:2]]
    sizes = [part.shape[1] // (most * edge) * most for part in parts]
    depth = min(3, sources.shape[0])
    home_rows, home_cols, *at_home = home if home else (rows[:, :most], cols[:, :most])
    arrays = [*parts, *pairs, *at_home, *adds, *after]
    anywhere = pl.BlockSpec(memory_space=pl.ANY)
    return pl.pallas_call(
        functools.partial(far_kernel, most, begin, sizes, lines, len(adds), 1 if home else 0),
        out_shape=jax.ShapeDtypeStruct((slots, height, columns), dtype),
        grid_spec=pltpu.PrefetchScalarGridSpec(
            num_scalar_prefetch=7,
            grid=(),
            in_specs=[anywhere] * len(arrays),
            out_specs=anywhere,
            scratch_shapes=[
                pltpu.VMEM((block_rows + 1, edge, columns), jnp.float32),
                pltpu.VMEM((lines, height, columns), pairs[0].dtype),
                pltpu.SemaphoreType.DMA((lines + 1,)),
                pltpu.VMEM((depth, height, columns), dtype),
                pltpu.SemaphoreType.DMA((depth,)),
                pltpu.SemaphoreType.DMA((depth, len(parts) + 1 + len(adds))),
            ]
            + [pltpu.VMEM((depth, size * edge, edge), parts[0].dtype) for size in sizes]
            + [pltpu.VMEM((depth, height, columns), add.dtype) for add in adds]
            + [
                pltpu.VMEM(shape, parts[0].dtype)
                for shape in ([(depth, most * edge, edge), (height, columns)] if home else [])
            ],
        ),
        compiler_params=params(VMEM_ALL),
        cost_estimate=COST,
        name="far",
    )(sources, places, above, rows, cols, home_rows, home_cols, *arrays)


def base_kernel(diag_ref, omega_ref, *rest):
    *piece_refs, out_ref = rest
    edge = diag_ref.shape[1]
    near = [
        dot(diag_ref[b], omega_ref[b * edge : (b + 1) * edge, :]) for b in range(diag_ref.shape[0])
    ]
    total = jnp.concatenate(near, axis=0)
    for piece_ref in piece_refs:
        total += piece_ref[...].astype(jnp.float32)
    out_ref[...] = total


def base_sum(diag, sketch, pieces):
    block_rows, edge, _ = diag.shape
    height, columns = sketch.shape
    together = math.gcd(block_rows, 2)
    rows = pl.BlockSpec((together * edge, columns), lambda b: (b, 0))
    return pl.pallas_call(
        base_kernel,
        out_shape=jax.ShapeDtypeStruct((height, columns), jnp.float32),
        grid=(block_rows // together,),
        in_specs=[pl.BlockSpec((together, edge, edge), lambda b: (b, 0, 0)), rows]
        + [rows] * len(pieces),
        out_specs=rows,
        compiler_params=params(VMEM_ALL),
        cost_estimate=COST,
        name="base",
    )(diag, sketch, *pieces)


def image_kernel(scale, chip_ref, base_ref, far_ref, *rest):
    *piece_refs, image_ref, gram_ref, cross, bases, fars, pieces, images, sems, out_sem = rest
    chips, (tiles, tile, _) = far_ref.shape[0], bases.shape
    from_chips = [lax.rem(chip_ref[0] + step, chips) for step in range(1, chips)]
    waits = []
    for t in range(tiles):
        rows = pl.ds(t * tile, tile)
        pairs = [(base_ref.at[rows, :], bases.at[t])]
        pairs += [(far_ref.at[chip, rows, :], fars.at[t, i]) for i, chip in enumerate(from_chips)]
        pairs += [(ref.at[rows, :], pieces.at[t, i]) for i, ref in enumerate(piece_refs)]
        waits.append([pltpu.make_async_copy(a, b, sems.at[t, i]) for i, (a, b) in enumerate(pairs)])
        for move in waits[-1]:
            move.start()
    gram_ref[...] = jnp.zeros_like(gram_ref)
    cross[...] = jnp.zeros_like(cross)
    leave = []
    for t in range(tiles):
        for move in waits[t]:
            move.wait()
        image = bases[t]
        for i in range(len(piece_refs)):
            image += pieces[t, i].astype(jnp.float32)
        for i in range(chips - 1):
            image += fars[t, i].astype(jnp.float32)
        images[t] = image
        leave.append(
            pltpu.make_async_copy(
                images.at[t], image_ref.at[pl.ds(t * tile, tile), :], out_sem.at[t]
            )
        )
        leave[-1].start()
        high, low = split(image)
        gram_ref[...] += dot(high, high, TN)
        cross[...] += dot(high, low, TN)
    gram_ref[...] = (gram_ref[...] + (cross[...] + cross[...].T)) * scale
    for move in leave:
        move.wait()


def image_and_gram(base, chip, far, pieces, total_rows):
    height, columns = base.shape
    tile = math.gcd(height, 256)
    tiles, chips = height // tile, far.shape[0]
    anywhere = pl.BlockSpec(memory_space=pl.ANY)
    return pl.pallas_call(
        functools.partial(image_kernel, 1.0 / total_rows),
        out_shape=(
            jax.ShapeDtypeStruct((height, columns), jnp.float32),
            jax.ShapeDtypeStruct((columns, columns), jnp.float32),
        ),
        grid_spec=pltpu.PrefetchScalarGridSpec(
            num_scalar_prefetch=1,
            grid=(),
            in_specs=[anywhere] * (2 + len(pieces)),
            out_specs=(anywhere, pl.BlockSpec(memory_space=pltpu.VMEM)),
            scratch_shapes=[
                pltpu.VMEM((columns, columns), jnp.float32),
                pltpu.VMEM((tiles, tile, columns), jnp.float32),
                pltpu.VMEM((tiles, max(1, chips - 1), tile, columns), far.dtype),
                pltpu.VMEM((tiles, len(pieces), tile, columns), pieces[0].dtype),
                pltpu.VMEM((tiles, tile, columns), jnp.float32),
                pltpu.SemaphoreType.DMA((tiles, chips + len(pieces))),
                pltpu.SemaphoreType.DMA((tiles,)),
            ],
        ),
        compiler_params=params(VMEM_ALL),
        cost_estimate=COST,
        name="image",
    )(chip.reshape(1), base, far, *pieces)


def factor_kernel(rounds, gram_ref, image_ref, basis_ref, factor_ref, inverse, work, images, tile_sem, bases, out_sem):
    n = gram_ref.shape[0]
    tiles, tile, _ = images.shape
    arrive = [
        pltpu.make_async_copy(image_ref.at[pl.ds(t * tile, tile), :], images.at[t], tile_sem.at[t])
        for t in range(tiles)
    ]
    for move in arrive:
        move.start()

    gram = gram_ref[...]
    row = lax.broadcasted_iota(jnp.int32, (n, n), 0)
    col = lax.broadcasted_iota(jnp.int32, (n, n), 1)
    weight = jnp.where(row > col, 1.0, jnp.where(row == col, 0.5, 0.0))
    one = jnp.where(row == col, 1.0, 0.0)
    diagonal = jnp.where(row == col, gram, 0.0)
    down = lax.rsqrt(jnp.sum(diagonal, axis=1, keepdims=True))
    across = lax.rsqrt(jnp.sum(diagonal, axis=0, keepdims=True))
    scaled = gram * down * across
    scaled3 = split(scaled)
    guess = one - weight * (scaled - one)
    for _ in range(rounds):
        guess3 = split(guess)
        error = dot3(split(dot3(guess3, scaled3)), guess3, NT) - one
        guess = guess - dot3(split(weight * error), guess3)
    guess = jnp.where(row >= col, guess, 0.0) * across
    inverse[...] = guess
    factor_ref[...] = jnp.where(row <= col, dot3(split(guess), split(gram)), 0.0)
    size = jnp.sum(error * error)

    @pl.when(jnp.logical_not(size < 1e-4))
    def _():
        exact = lax.Precision.HIGHEST
        work[...] = gram
        inverse[...] = one
        lane = lax.broadcasted_iota(jnp.int32, (1, n), 1)

        def eliminate(j, carry):
            line = work[pl.ds(j, 1), :]
            pivot = jnp.sum(jnp.where(lane == j, line, 0.0), axis=1, keepdims=True)
            scale = lax.rsqrt(pivot)
            line = jnp.where(lane >= j, line * scale, 0.0)
            other = inverse[pl.ds(j, 1), :] * scale
            below = jnp.where(lane > j, line, 0.0)
            work[...] -= dot(below, line, TN, exact)
            inverse[...] -= dot(below, other, TN, exact)
            inverse[pl.ds(j, 1), :] = other
            factor_ref[pl.ds(j, 1), :] = line
            return carry

        lax.fori_loop(0, n, eliminate, 0)

    inverse3 = split(inverse[...])
    leave = []
    for t in range(tiles):
        arrive[t].wait()
        bases[t] = dot3(split(images[t]), inverse3, NT)
        leave.append(
            pltpu.make_async_copy(bases.at[t], basis_ref.at[pl.ds(t * tile, tile), :], out_sem.at[t])
        )
        leave[-1].start()
    for move in leave:
        move.wait()


def factor_and_basis(gram, image, rounds=2):
    height, n = image.shape
    tile = math.gcd(height, 256)
    tiles = height // tile
    square, anywhere = pl.BlockSpec(memory_space=pltpu.VMEM), pl.BlockSpec(memory_space=pl.ANY)
    held = pltpu.VMEM((tiles, tile, n), jnp.float32)
    return pl.pallas_call(
        functools.partial(factor_kernel, rounds),
        out_shape=(
            jax.ShapeDtypeStruct((height, n), jnp.float32),
            jax.ShapeDtypeStruct((n, n), jnp.float32),
        ),
        in_specs=[square, anywhere],
        out_specs=(anywhere, square),
        scratch_shapes=[pltpu.VMEM((n, n), jnp.float32)] * 2
        + [held, pltpu.SemaphoreType.DMA((tiles,))] * 2,
        compiler_params=params(VMEM_ALL),
        cost_estimate=COST,
        name="factor",
    )(gram, image)


def sum_over_devices(part):
    rows, columns = part.shape
    planes, layers = lax.axis_size(PLANE), lax.axis_size(LINE)
    pieces = lax.all_to_all(part.reshape(planes, rows // planes, columns), PLANE, 0, 0, tiled=True)
    mine = jnp.sum(pieces, axis=0)
    step = 1
    while step < layers:
        mine += lax.ppermute(mine, LINE, [(z, z ^ step) for z in range(layers)])
        step *= 2
    mine = jnp.broadcast_to(mine, pieces.shape)
    return lax.all_to_all(mine, PLANE, 0, 0, tiled=True).reshape(rows, columns)


def on_device(diag_blocks, off_blocks, col_blocks, sketch):
    block_rows, per_row = col_blocks.shape
    edge = diag_blocks.shape[1]
    layers = lax.axis_size(LINE)
    planes = lax.axis_size(PLANE)
    peers = layers * planes
    requests = block_rows * per_row
    most = max(2, (2 * requests + peers - 1) // peers)
    slots = layers * most
    layer = lax.axis_index(LINE)
    shifts = sorted(range(layers), key=lambda shift: -min(shift, layers - shift))
    cut = 1
    groups = [group for group in (shifts[:cut], shifts[cut:-1], shifts[-1:]) if group]
    flat = col_blocks.reshape(requests)
    owners = flat // block_rows
    order = jnp.arange(requests)
    earlier = (owners[:, None] == owners[None, :]) & (order[None, :] < order[:, None])
    ranks = jnp.sum(earlier.astype(jnp.int32), axis=1)
    to_plane = owners % planes
    away = lax.rem(owners // planes - layer + layers, layers)
    turn = sum(jnp.where(away == shift, index, 0) for index, shift in enumerate(shifts))
    to_slot = turn * most + ranks
    place = to_plane * slots + to_slot
    hit = place[:, None] == jnp.arange(planes * slots)[None, :]
    row_label = block_rows + jnp.sum(
        jnp.where(hit, (order // per_row - block_rows)[:, None], 0), axis=0
    )
    col_label = block_rows + jnp.sum(
        jnp.where(hit, (flat % block_rows - block_rows)[:, None], 0), axis=0
    )
    labels = jnp.stack([row_label.reshape(planes, slots), col_label.reshape(planes, slots)], axis=1)
    labels = jnp.pad(labels, ((0, 0), (0, TAIL - 2), (0, edge - slots))).astype(jnp.bfloat16)
    sizes = [len(group) * most for group in groups]
    ends = [sum(sizes[: index + 1]) for index in range(len(sizes))]
    in_part = sum((to_slot >= end).astype(jnp.int32) for end in ends)
    begins = sum(jnp.where(in_part == index + 1, end, 0) for index, end in enumerate(ends))
    before = jnp.sum(
        (in_part[None, :] < in_part[:, None])
        | ((in_part[None, :] == in_part[:, None]) & (order[None, :] < order[:, None])),
        axis=1,
    )
    pick = before[None, :] == order[:, None]
    route = [
        jnp.sum(jnp.where(pick, values[None, :], 0), axis=1)
        for values in (order, to_plane, to_slot - begins)
    ]
    counts = jnp.sum(in_part[None, :] < jnp.arange(len(sizes) + 1)[:, None], axis=1)
    outgoing = list(
        pack(off_blocks.reshape(requests, edge, edge), route + [counts], labels, sizes)
    )

    def planes_off(k):
        return [(z, z - k) for z in range(k, layers)], [(z, z + k) for z in range(layers - k)]

    down, up = planes_off(1)
    above, below = lax.ppermute(sketch, LINE, down), lax.ppermute(sketch, LINE, up)
    by_line = [(above, below)]
    early_lines = [above, below]
    if layers > 2:
        by_line.append((lax.ppermute(above, LINE, down), lax.ppermute(below, LINE, up)))
        both = lax.ppermute(sketch, LINE, sum(planes_off(3), []))
        by_line.append((both, both))
        early_lines.append(both)
    chip, core = lax.axis_index(CHIPS), lax.axis_index(CORE)
    if [lax.axis_size(axis) for axis in PLANE] == [2, 2, 2]:
        swap = [(0, 1), (1, 0)]
        by_x, by_y = (lax.ppermute(sketch, axis, swap) for axis in CHIPS)
        upper, lower = halves(by_y, by_x)
        across = [lax.ppermute(upper, CHIPS[0], swap), lax.ppermute(lower, CHIPS[1], swap)]
        outgoing[0] = hold(outgoing[0], [by_x, by_y])
        mine = join([sketch, by_y, by_x] + across)
        plane_omegas = [
            array.reshape((4,) + sketch.shape) for array in (mine, lax.ppermute(mine, CORE, swap))
        ]
        relative = True
    else:
        plane_omegas = [lax.all_gather(sketch, PLANE)]
        relative = False
    outgoing[1] = hold(outgoing[1], early_lines)
    parts = [lax.all_to_all(part, PLANE, 0, 0, tiled=True) for part in outgoing[:-1]]
    lines = sizes[0] * edge
    rows = parts[0][:, lines, :slots].astype(jnp.int32)
    cols = parts[0][:, lines + 1, :slots].astype(jnp.int32)

    layer, chip, core, row_label, col_label, rows, cols = lax.optimization_barrier(
        (layer, chip, core, row_label, col_label, rows, cols)
    )
    line_omegas = [
        (by_line[shift - 1][0], by_line[layers - shift - 1][1], (layer + shift < layers).astype(jnp.int32))
        for shift in shifts[:-1]
    ]
    sources = jnp.arange(planes)
    if relative:
        near_chips = (chip ^ jnp.arange(4)) * 2
        sources = jnp.concatenate([near_chips + core, near_chips + 1 - core])
    def send_mirror(index, after):
        part = sum(index * most >= end for end in ends)
        inside = index - (ends[part] - sizes[part]) // most
        shift = shifts[index]
        mirror = plane_sum(
            parts[part],
            plane_omegas,
            sources,
            rows,
            cols,
            inside,
            index * most,
            most,
            block_rows,
            jnp.bfloat16,
            True,
            after,
        )
        steps = [(z, (z + shift) % layers) for z in range(layers)]
        return lax.ppermute(mirror, LINE, steps), (mirror,)

    first, latest = send_mirror(0, ())

    home_rows = row_label.reshape(planes, slots)[:, -most:]
    home_cols = col_label.reshape(planes, slots)[:, -most:]
    cores = lax.axis_size(CORE)
    chips = planes // cores
    away = (chip + jnp.arange(1, chips)) % chips
    at_home = (home_rows, home_cols, outgoing[-1], sketch)
    far = functools.partial(far_sum, rows=rows, cols=cols, most=most, block_rows=block_rows)
    everything = dict(begin=0, parts=parts, omegas=line_omegas, home=at_home)
    early = dict(begin=0, parts=parts[:1], omegas=line_omegas[:1], home=at_home)
    late = dict(begin=sizes[0], parts=parts[1:], omegas=line_omegas[1:], home=None)

    def ask(chips_asked, dtype, what, after):
        if cores == 1:
            return [], after
        count = chips_asked.shape[0]
        other = far(
            chips_asked * cores + 1 - core, jnp.arange(count), count, dtype=dtype, after=after, **what
        )
        return [lax.ppermute(other, CORE, [(0, 1), (1, 0)])], (other,)

    other, latest = ask(away, jnp.float32, early, latest)
    home = plane_sum(
        outgoing[-1],
        plane_omegas,
        sources,
        home_rows,
        home_cols,
        0,
        0,
        most,
        block_rows,
        jnp.float32,
        False,
        latest,
    )
    begun = far(
        away * cores + core,
        jnp.arange(chips - 1),
        chips - 1,
        dtype=jnp.float32,
        adds=other,
        after=(home,),
        **early,
    )
    other, latest = ask(away, jnp.bfloat16, late, (begun,))
    second, latest = send_mirror(1, latest)
    sent = far(
        away * cores + core, away, chips, dtype=jnp.bfloat16, adds=[begun] + other, after=latest, **late
    )
    received = lax.all_to_all(sent, CHIPS, 0, 0, tiled=True)
    pieces, latest = [second], (sent,)
    for index in range(2, layers - 1):
        piece, latest = send_mirror(index, latest)
        pieces.append(piece)
    other, _ = ask(chip.reshape(1), jnp.float32, everything, (sent,))
    own = far(
        chip.reshape(1) * cores + core,
        jnp.arange(1),
        1,
        dtype=jnp.float32,
        adds=other,
        after=latest,
        **everything,
    )
    base = base_sum(diag_blocks, sketch, [home, own.reshape(sketch.shape), first])
    image, part = image_and_gram(base, chip, received, pieces, block_rows * edge * peers)
    gram = sum_over_devices(part)
    return factor_and_basis(gram, image)


def solution(mesh):
    rows, sub = mesh.devices.shape
    layers, cores = math.gcd(rows, 4), math.gcd(sub, 2)
    devices = mesh.devices.reshape(layers, rows // layers, sub // cores, cores)
    placed = (P(ALL, None, None), P(ALL, None, None, None), P(ALL, None), P(ALL, None))
    return jax.shard_map(
        on_device,
        mesh=Mesh(devices, ALL),
        in_specs=placed,
        out_specs=(P(ALL, None), P()),
        check_vma=False,
    )
```

```python
import functools
import math

import jax
import jax.numpy as jnp
from jax import lax
from jax.experimental import pallas as pl
from jax.experimental.pallas import tpu as pltpu
from jax.sharding import Mesh
from jax.sharding import PartitionSpec as P

LINE = "z"
PLANE = ("x", "y", "c")
ALL = (LINE,) + PLANE
CHIPS, CORE = PLANE[:2], PLANE[2]
VMEM_LIMIT = 48 * 1024 * 1024
VMEM_ALL = 60 * 1024 * 1024
COST = pl.CostEstimate(flops=10**12, bytes_accessed=10**11, transcendentals=0)
TAIL = 16


def dot(a, b, contract=((1,), (0,)), precision=None):
    return lax.dot_general(
        a, b, (contract, ((), ())), precision=precision, preferred_element_type=jnp.float32
    )


NT = ((1,), (1,))
TN = ((0,), (0,))


def params(limit=VMEM_LIMIT):
    return pltpu.CompilerParams(vmem_limit_bytes=limit)


def split(a):
    high = a.astype(jnp.bfloat16)
    return high, (a - high.astype(jnp.float32)).astype(jnp.bfloat16)

def dot3(a, b, contract=((1,), (0,))):
    (ah, al), (bh, bl) = a, b
    return dot(ah, bh, contract) + (dot(ah, bl, contract) + dot(al, bh, contract))

def pack_kernel(entry_ref, plane_ref, slot_ref, count_ref, off_ref, label_ref, *rest):
    *out_refs, sem, label_sem = rest
    _, edge, _ = off_ref.shape
    tail = label_ref.shape[1]
    first = out_refs[0]
    labels = pltpu.make_async_copy(
        label_ref, first.at[:, pl.ds(first.shape[1] - tail, tail), :], label_sem
    )
    labels.start()
    for part, out_ref in enumerate(out_refs):

        def send(place, carry, out_ref=out_ref):
            row = pl.multiple_of(slot_ref[place] * edge, edge)
            pltpu.make_async_copy(
                off_ref.at[entry_ref[place]], out_ref.at[plane_ref[place], pl.ds(row, edge), :], sem
            ).start()
            return carry

        lax.fori_loop(count_ref[part], count_ref[part + 1], send, 0)
    pltpu.make_async_copy(off_ref, off_ref, sem).wait()
    labels.wait()


def pack(off, route, labels, parts):
    count, edge, _ = off.shape
    planes, tail, _ = labels.shape
    lengths = [slots * edge + (tail if index == 0 else 0) for index, slots in enumerate(parts)]
    anywhere = pl.BlockSpec(memory_space=pl.ANY)
    return pl.pallas_call(
        pack_kernel,
        out_shape=[jax.ShapeDtypeStruct((planes, length, edge), off.dtype) for length in lengths],
        grid_spec=pltpu.PrefetchScalarGridSpec(
            num_scalar_prefetch=len(route),
            grid=(),
            in_specs=[pl.BlockSpec(memory_space=pltpu.VMEM), anywhere],
            out_specs=[anywhere] * len(parts),
            scratch_shapes=[pltpu.SemaphoreType.DMA, pltpu.SemaphoreType.DMA],
        ),
        compiler_params=params(VMEM_ALL),
        cost_estimate=COST,
        name="pack",
    )(*route, off, labels)


def hold_kernel(x_ref, *rest):
    del x_ref, rest


def hold(x, after):
    anywhere = pl.BlockSpec(memory_space=pl.ANY)
    return pl.pallas_call(
        hold_kernel,
        out_shape=jax.ShapeDtypeStruct(x.shape, x.dtype),
        in_specs=[anywhere] * (1 + len(after)),
        out_specs=anywhere,
        input_output_aliases={0: 0},
        cost_estimate=COST,
        name="hold",
    )(x, *after)


def join_kernel(*refs):
    count = (len(refs) - 2) // 2
    in_refs, out_ref, held, sems = refs[:count], refs[count], refs[count + 1], refs[count + 2 :]
    begin, moves = 0, []
    for in_ref, sem in zip(in_refs, sems, strict=True):
        rows = pl.ds(begin, in_ref.shape[0])
        moves.append((rows, pltpu.make_async_copy(in_ref, held.at[rows, :], sem), sem))
        moves[-1][1].start()
        begin += in_ref.shape[0]
    out = []
    for rows, move, sem in moves:
        move.wait()
        out.append(pltpu.make_async_copy(held.at[rows, :], out_ref.at[rows, :], sem))
        out[-1].start()
    for move in out:
        move.wait()


def join(arrays):
    shape = (sum(array.shape[0] for array in arrays), arrays[0].shape[1])
    anywhere = pl.BlockSpec(memory_space=pl.ANY)
    return pl.pallas_call(
        join_kernel,
        out_shape=jax.ShapeDtypeStruct(shape, arrays[0].dtype),
        in_specs=[anywhere] * len(arrays),
        out_specs=anywhere,
        scratch_shapes=[pltpu.VMEM(shape, arrays[0].dtype)] + [pltpu.SemaphoreType.DMA] * len(arrays),
        compiler_params=params(VMEM_ALL),
        cost_estimate=COST,
        name="join",
    )(*arrays)


def halves_kernel(y_ref, x_ref, first_ref, second_ref, held, sems):
    half = first_ref.shape[0]
    first = pltpu.make_async_copy(y_ref.at[pl.ds(0, half), :], held.at[0], sems.at[0])
    second = pltpu.make_async_copy(x_ref.at[pl.ds(half, half), :], held.at[1], sems.at[1])
    first.start()
    second.start()
    first.wait()
    first = pltpu.make_async_copy(held.at[0], first_ref, sems.at[0])
    first.start()
    second.wait()
    second = pltpu.make_async_copy(held.at[1], second_ref, sems.at[1])
    second.start()
    first.wait()
    second.wait()


def halves(by_y, by_x):
    height, columns = by_y.shape
    anywhere = pl.BlockSpec(memory_space=pl.ANY)
    return pl.pallas_call(
        halves_kernel,
        out_shape=[jax.ShapeDtypeStruct((height // 2, columns), by_y.dtype)] * 2,
        in_specs=[anywhere] * 2,
        out_specs=[anywhere] * 2,
        scratch_shapes=[
            pltpu.VMEM((2, height // 2, columns), by_y.dtype),
            pltpu.SemaphoreType.DMA((2,)),
        ],
        compiler_params=params(VMEM_ALL),
        cost_estimate=COST,
        name="halves",
    )(by_y, by_x)


def plane_kernel(inside, begin, most, counts, mirrored, source_ref, row_ref, col_ref, *rest):
    block_ref, *omega_refs = rest[: 1 + len(counts)]
    out_ref, total, blocks, omegas, block_sem, omega_sem = rest[-6:]
    edge = blocks.shape[2]
    spare = total.shape[0] - 1
    places = [(omega_ref, k) for omega_ref, count in zip(omega_refs, counts) for k in range(count)]
    moves = []
    for step, (omega_ref, k) in enumerate(places):
        rows = pl.ds(inside * most * edge, most * edge)
        moves.append(
            (
                pltpu.make_async_copy(
                    block_ref.at[source_ref[step], rows, :], blocks.at[step], block_sem.at[step]
                ),
                pltpu.make_async_copy(omega_ref.at[k], omegas.at[step], omega_sem.at[step]),
            )
        )
        for move in moves[-1]:
            move.start()
    total[...] = jnp.zeros_like(total)
    for step in range(len(places)):
        source = source_ref[step]
        for move in moves[step]:
            move.wait()
        for m in range(most):
            row = row_ref[source, begin + m]
            col = col_ref[source, begin + m]
            here, there = (row, col) if mirrored else (col, row)
            here = pl.multiple_of(jnp.minimum(here, spare - 1) * edge, edge)
            block = blocks[step, m * edge : (m + 1) * edge, :]
            omega = omegas[step, pl.ds(here, edge), :]
            if mirrored:
                product = dot(block, omega, TN).astype(jnp.bfloat16).astype(jnp.float32)
            else:
                product = dot(block, omega)
            total[there] += product
    out_ref[...] = total[:spare].reshape(out_ref.shape).astype(out_ref.dtype)


def plane_sum(
    blocks, omegas, sources, rows, cols, inside, begin, most, block_rows, dtype, mirrored, after=()
):
    planes, _, edge = blocks.shape
    _, height, columns = omegas[0].shape
    counts = [omega.shape[0] for omega in omegas]
    anywhere = pl.BlockSpec(memory_space=pl.ANY)
    return pl.pallas_call(
        functools.partial(plane_kernel, inside, begin, most, counts, mirrored),
        out_shape=jax.ShapeDtypeStruct((height, columns), dtype),
        grid_spec=pltpu.PrefetchScalarGridSpec(
            num_scalar_prefetch=3,
            grid=(),
            in_specs=[anywhere] * (1 + len(omegas) + len(after)),
            out_specs=pl.BlockSpec(memory_space=pltpu.VMEM),
            scratch_shapes=[
                pltpu.VMEM((block_rows + 1, edge, columns), jnp.float32),
                pltpu.VMEM((planes, most * edge, edge), blocks.dtype),
                pltpu.VMEM((planes, height, columns), omegas[0].dtype),
                pltpu.SemaphoreType.DMA((planes,)),
                pltpu.SemaphoreType.DMA((planes,)),
            ],
        ),
        compiler_params=params(VMEM_ALL),
        cost_estimate=COST,
        name="mirror" if mirrored else "home",
    )(sources, rows, cols, blocks, *omegas, *after)


def far_kernel(most, begin, sizes, lines, added, at_home, *refs):
    source_ref, place_ref, above_ref, row_ref, col_ref, home_row_ref, home_col_ref, *refs = refs
    part_refs, refs = refs[: len(sizes)], refs[len(sizes) :]
    omega_refs, refs = refs[: 2 * lines], refs[2 * lines :]
    home_refs, refs = refs[: 2 * at_home], refs[2 * at_home :]
    add_refs = refs[:added]
    scratch = refs[len(refs) - 7 - len(sizes) - added - 2 * at_home :]
    out_ref, total, omegas, omega_sem, outs, out_sem, sems, *held = scratch
    blocks, adds, homes = held[: len(sizes)], held[len(sizes) : len(sizes) + added], held[len(sizes) + added :]
    edge = total.shape[1]
    spare = total.shape[0] - 1
    count, depth = source_ref.shape[0], outs.shape[0]

    def arrive(k):
        slot, source = k % depth, source_ref[k]
        pairs = [
            (part_ref.at[source, pl.ds(0, size * edge), :], block.at[slot])
            for part_ref, size, block in zip(part_refs, sizes, blocks)
        ]
        if at_home:
            pairs.append((home_refs[0].at[source], homes[0].at[slot]))
        pairs += [(add_ref.at[k], add.at[slot]) for add_ref, add in zip(add_refs, adds)]
        return [pltpu.make_async_copy(a, b, sems.at[slot, i]) for i, (a, b) in enumerate(pairs)]

    def leave(k):
        slot = k % depth
        return pltpu.make_async_copy(outs.at[slot], out_ref.at[place_ref[k]], out_sem.at[slot])

    lead = [
        [
            pltpu.make_async_copy(omega_ref, omegas.at[index], omega_sem.at[index])
            for omega_ref in omega_refs[2 * index : 2 * index + 2]
        ]
        for index in range(lines)
    ]
    if at_home:
        own = pltpu.make_async_copy(home_refs[1], homes[1], omega_sem.at[lines])
    ahead = [arrive(k) for k in range(min(depth, count))]
    for k, moves in enumerate(ahead):
        for move in moves[: len(moves) - added]:
            move.start()
        if k == 0:
            if at_home:
                own.start()
            for index, (above, below) in enumerate(lead):
                pl.when(above_ref[index] == 1)(above.start)
                pl.when(above_ref[index] == 0)(below.start)
    for moves in ahead:
        for move in moves[len(moves) - added :]:
            move.start()
    for k in range(count):
        slot, source = k % depth, source_ref[k]
        moves = arrive(k)
        for move in moves[: len(moves) - added]:
            move.wait()
        total[...] = jnp.zeros_like(total)
        if at_home:
            if k == 0:
                own.wait()
            for place in range(most):
                row = jnp.minimum(home_row_ref[source, place], spare - 1)
                row = pl.multiple_of(row * edge, edge)
                block = homes[0][slot, place * edge : (place + 1) * edge, :]
                product = dot(block, homes[1][pl.ds(row, edge), :], TN).astype(jnp.bfloat16)
                total[home_col_ref[source, place]] += product.astype(jnp.float32)
        index = 0
        for block_ref, size in zip(blocks, sizes):
            for place in range(size):
                line = index // most
                if k == 0 and index % most == 0:
                    lead[line][0].wait()
                row = row_ref[source, begin + index]
                col = jnp.minimum(col_ref[source, begin + index], spare - 1)
                block = block_ref[slot, place * edge : (place + 1) * edge, :]
                total[row] += dot(block, omegas[line, pl.ds(pl.multiple_of(col * edge, edge), edge), :])
                index += 1
        if k >= depth:
            leave(k - depth).wait()
        for move in moves[len(moves) - added :]:
            move.wait()
        result = total[:spare].reshape(outs.shape[1:])
        for add in adds:
            result += add[slot].astype(jnp.float32)
        outs[slot] = result.astype(outs.dtype)
        leave(k).start()
        if k + depth < count:
            for move in arrive(k + depth):
                move.start()
    for k in range(max(0, count - depth), count):
        leave(k).wait()


def far_sum(
    sources, places, slots, begin, parts, omegas, rows, cols, home, most, block_rows, dtype, adds=(), after=()
):
    edge = parts[0].shape[2]
    height, columns = omegas[0][0].shape
    lines = len(omegas)
    above = jnp.stack([choice for _, _, choice in omegas])
    pairs = [omega for pair in omegas for omega in pair[:2]]
    sizes = [part.shape[1] // (most * edge) * most for part in parts]
    depth = min(3, sources.shape[0])
    home_rows, home_cols, *at_home = home if home else (rows[:, :most], cols[:, :most])
    arrays = [*parts, *pairs, *at_home, *adds, *after]
    anywhere = pl.BlockSpec(memory_space=pl.ANY)
    return pl.pallas_call(
        functools.partial(far_kernel, most, begin, sizes, lines, len(adds), 1 if home else 0),
        out_shape=jax.ShapeDtypeStruct((slots, height, columns), dtype),
        grid_spec=pltpu.PrefetchScalarGridSpec(
            num_scalar_prefetch=7,
            grid=(),
            in_specs=[anywhere] * len(arrays),
            out_specs=anywhere,
            scratch_shapes=[
                pltpu.VMEM((block_rows + 1, edge, columns), jnp.float32),
                pltpu.VMEM((lines, height, columns), pairs[0].dtype),
                pltpu.SemaphoreType.DMA((lines + 1,)),
                pltpu.VMEM((depth, height, columns), dtype),
                pltpu.SemaphoreType.DMA((depth,)),
                pltpu.SemaphoreType.DMA((depth, len(parts) + 1 + len(adds))),
            ]
            + [pltpu.VMEM((depth, size * edge, edge), parts[0].dtype) for size in sizes]
            + [pltpu.VMEM((depth, height, columns), add.dtype) for add in adds]
            + [
                pltpu.VMEM(shape, parts[0].dtype)
                for shape in ([(depth, most * edge, edge), (height, columns)] if home else [])
            ],
        ),
        compiler_params=params(VMEM_ALL),
        cost_estimate=COST,
        name="far",
    )(sources, places, above, rows, cols, home_rows, home_cols, *arrays)


def base_kernel(diag_ref, omega_ref, *rest):
    *piece_refs, out_ref = rest
    edge = diag_ref.shape[1]
    near = [
        dot(diag_ref[b], omega_ref[b * edge : (b + 1) * edge, :]) for b in range(diag_ref.shape[0])
    ]
    total = jnp.concatenate(near, axis=0)
    for piece_ref in piece_refs:
        total += piece_ref[...].astype(jnp.float32)
    out_ref[...] = total


def base_sum(diag, sketch, pieces):
    block_rows, edge, _ = diag.shape
    height, columns = sketch.shape
    together = math.gcd(block_rows, 2)
    rows = pl.BlockSpec((together * edge, columns), lambda b: (b, 0))
    return pl.pallas_call(
        base_kernel,
        out_shape=jax.ShapeDtypeStruct((height, columns), jnp.float32),
        grid=(block_rows // together,),
        in_specs=[pl.BlockSpec((together, edge, edge), lambda b: (b, 0, 0)), rows]
        + [rows] * len(pieces),
        out_specs=rows,
        compiler_params=params(VMEM_ALL),
        cost_estimate=COST,
        name="base",
    )(diag, sketch, *pieces)


def image_kernel(scale, chip_ref, base_ref, far_ref, *rest):
    *piece_refs, image_ref, gram_ref, cross, bases, fars, pieces, images, sems, out_sem = rest
    chips, (tiles, tile, _) = far_ref.shape[0], bases.shape
    from_chips = [lax.rem(chip_ref[0] + step, chips) for step in range(1, chips)]
    waits = []
    for t in range(tiles):
        rows = pl.ds(t * tile, tile)
        pairs = [(base_ref.at[rows, :], bases.at[t])]
        pairs += [(far_ref.at[chip, rows, :], fars.at[t, i]) for i, chip in enumerate(from_chips)]
        pairs += [(ref.at[rows, :], pieces.at[t, i]) for i, ref in enumerate(piece_refs)]
        waits.append([pltpu.make_async_copy(a, b, sems.at[t, i]) for i, (a, b) in enumerate(pairs)])
        for move in waits[-1]:
            move.start()
    gram_ref[...] = jnp.zeros_like(gram_ref)
    cross[...] = jnp.zeros_like(cross)
    leave = []
    for t in range(tiles):
        for move in waits[t]:
            move.wait()
        image = bases[t]
        for i in range(len(piece_refs)):
            image += pieces[t, i].astype(jnp.float32)
        for i in range(chips - 1):
            image += fars[t, i].astype(jnp.float32)
        images[t] = image
        leave.append(
            pltpu.make_async_copy(
                images.at[t], image_ref.at[pl.ds(t * tile, tile), :], out_sem.at[t]
            )
        )
        leave[-1].start()
        high, low = split(image)
        gram_ref[...] += dot(high, high, TN)
        cross[...] += dot(high, low, TN)
    gram_ref[...] = (gram_ref[...] + (cross[...] + cross[...].T)) * scale
    for move in leave:
        move.wait()


def image_and_gram(base, chip, far, pieces, total_rows):
    height, columns = base.shape
    tile = math.gcd(height, 256)
    tiles, chips = height // tile, far.shape[0]
    anywhere = pl.BlockSpec(memory_space=pl.ANY)
    return pl.pallas_call(
        functools.partial(image_kernel, 1.0 / total_rows),
        out_shape=(
            jax.ShapeDtypeStruct((height, columns), jnp.float32),
            jax.ShapeDtypeStruct((columns, columns), jnp.float32),
        ),
        grid_spec=pltpu.PrefetchScalarGridSpec(
            num_scalar_prefetch=1,
            grid=(),
            in_specs=[anywhere] * (2 + len(pieces)),
            out_specs=(anywhere, pl.BlockSpec(memory_space=pltpu.VMEM)),
            scratch_shapes=[
                pltpu.VMEM((columns, columns), jnp.float32),
                pltpu.VMEM((tiles, tile, columns), jnp.float32),
                pltpu.VMEM((tiles, max(1, chips - 1), tile, columns), far.dtype),
                pltpu.VMEM((tiles, len(pieces), tile, columns), pieces[0].dtype),
                pltpu.VMEM((tiles, tile, columns), jnp.float32),
                pltpu.SemaphoreType.DMA((tiles, chips + len(pieces))),
                pltpu.SemaphoreType.DMA((tiles,)),
            ],
        ),
        compiler_params=params(VMEM_ALL),
        cost_estimate=COST,
        name="image",
    )(chip.reshape(1), base, far, *pieces)


def factor_kernel(rounds, gram_ref, image_ref, basis_ref, factor_ref, inverse, work, images, tile_sem, bases, out_sem):
    n = gram_ref.shape[0]
    tiles, tile, _ = images.shape
    arrive = [
        pltpu.make_async_copy(image_ref.at[pl.ds(t * tile, tile), :], images.at[t], tile_sem.at[t])
        for t in range(tiles)
    ]
    for move in arrive:
        move.start()

    gram = gram_ref[...]
    row = lax.broadcasted_iota(jnp.int32, (n, n), 0)
    col = lax.broadcasted_iota(jnp.int32, (n, n), 1)
    weight = jnp.where(row > col, 1.0, jnp.where(row == col, 0.5, 0.0))
    one = jnp.where(row == col, 1.0, 0.0)
    diagonal = jnp.where(row == col, gram, 0.0)
    down = lax.rsqrt(jnp.sum(diagonal, axis=1, keepdims=True))
    across = lax.rsqrt(jnp.sum(diagonal, axis=0, keepdims=True))
    scaled = gram * down * across
    scaled3 = split(scaled)
    guess = one - weight * (scaled - one)
    for _ in range(rounds):
        guess3 = split(guess)
        error = dot3(split(dot3(guess3, scaled3)), guess3, NT) - one
        guess = guess - dot3(split(weight * error), guess3)
    guess = jnp.where(row >= col, guess, 0.0) * across
    inverse[...] = guess
    factor_ref[...] = jnp.where(row <= col, dot3(split(guess), split(gram)), 0.0)
    size = jnp.sum(error * error)

    @pl.when(jnp.logical_not(size < 1e-4))
    def _():
        exact = lax.Precision.HIGHEST
        work[...] = gram
        inverse[...] = one
        lane = lax.broadcasted_iota(jnp.int32, (1, n), 1)

        def eliminate(j, carry):
            line = work[pl.ds(j, 1), :]
            pivot = jnp.sum(jnp.where(lane == j, line, 0.0), axis=1, keepdims=True)
            scale = lax.rsqrt(pivot)
            line = jnp.where(lane >= j, line * scale, 0.0)
            other = inverse[pl.ds(j, 1), :] * scale
            below = jnp.where(lane > j, line, 0.0)
            work[...] -= dot(below, line, TN, exact)
            inverse[...] -= dot(below, other, TN, exact)
            inverse[pl.ds(j, 1), :] = other
            factor_ref[pl.ds(j, 1), :] = line
            return carry

        lax.fori_loop(0, n, eliminate, 0)

    inverse3 = split(inverse[...])
    leave = []
    for t in range(tiles):
        arrive[t].wait()
        bases[t] = dot3(split(images[t]), inverse3, NT)
        leave.append(
            pltpu.make_async_copy(bases.at[t], basis_ref.at[pl.ds(t * tile, tile), :], out_sem.at[t])
        )
        leave[-1].start()
    for move in leave:
        move.wait()


def factor_and_basis(gram, image, rounds=2):
    height, n = image.shape
    tile = math.gcd(height, 256)
    tiles = height // tile
    square, anywhere = pl.BlockSpec(memory_space=pltpu.VMEM), pl.BlockSpec(memory_space=pl.ANY)
    held = pltpu.VMEM((tiles, tile, n), jnp.float32)
    return pl.pallas_call(
        functools.partial(factor_kernel, rounds),
        out_shape=(
            jax.ShapeDtypeStruct((height, n), jnp.float32),
            jax.ShapeDtypeStruct((n, n), jnp.float32),
        ),
        in_specs=[square, anywhere],
        out_specs=(anywhere, square),
        scratch_shapes=[pltpu.VMEM((n, n), jnp.float32)] * 2
        + [held, pltpu.SemaphoreType.DMA((tiles,))] * 2,
        compiler_params=params(VMEM_ALL),
        cost_estimate=COST,
        name="factor",
    )(gram, image)


def sum_over_devices(part):
    rows, columns = part.shape
    planes, layers = lax.axis_size(PLANE), lax.axis_size(LINE)
    pieces = lax.all_to_all(part.reshape(planes, rows // planes, columns), PLANE, 0, 0, tiled=True)
    mine = jnp.sum(pieces, axis=0)
    step = 1
    while step < layers:
        mine += lax.ppermute(mine, LINE, [(z, z ^ step) for z in range(layers)])
        step *= 2
    mine = jnp.broadcast_to(mine, pieces.shape)
    return lax.all_to_all(mine, PLANE, 0, 0, tiled=True).reshape(rows, columns)


def on_device(diag_blocks, off_blocks, col_blocks, sketch):
    block_rows, per_row = col_blocks.shape
    edge = diag_blocks.shape[1]
    layers = lax.axis_size(LINE)
    planes = lax.axis_size(PLANE)
    peers = layers * planes
    requests = block_rows * per_row
    most = max(2, (2 * requests + peers - 1) // peers)
    slots = layers * most
    layer = lax.axis_index(LINE)
    shifts = sorted(range(layers), key=lambda shift: -min(shift, layers - shift))
    cut = 1
    groups = [group for group in (shifts[:cut], shifts[cut:-1], shifts[-1:]) if group]
    flat = col_blocks.reshape(requests)
    owners = flat // block_rows
    order = jnp.arange(requests)
    earlier = (owners[:, None] == owners[None, :]) & (order[None, :] < order[:, None])
    ranks = jnp.sum(earlier.astype(jnp.int32), axis=1)
    to_plane = owners % planes
    away = lax.rem(owners // planes - layer + layers, layers)
    turn = sum(jnp.where(away == shift, index, 0) for index, shift in enumerate(shifts))
    to_slot = turn * most + ranks
    place = to_plane * slots + to_slot
    hit = place[:, None] == jnp.arange(planes * slots)[None, :]
    row_label = block_rows + jnp.sum(
        jnp.where(hit, (order // per_row - block_rows)[:, None], 0), axis=0
    )
    col_label = block_rows + jnp.sum(
        jnp.where(hit, (flat % block_rows - block_rows)[:, None], 0), axis=0
    )
    labels = jnp.stack([row_label.reshape(planes, slots), col_label.reshape(planes, slots)], axis=1)
    labels = jnp.pad(labels, ((0, 0), (0, TAIL - 2), (0, edge - slots))).astype(jnp.bfloat16)
    sizes = [len(group) * most for group in groups]
    ends = [sum(sizes[: index + 1]) for index in range(len(sizes))]
    in_part = sum((to_slot >= end).astype(jnp.int32) for end in ends)
    begins = sum(jnp.where(in_part == index + 1, end, 0) for index, end in enumerate(ends))
    before = jnp.sum(
        (in_part[None, :] < in_part[:, None])
        | ((in_part[None, :] == in_part[:, None]) & (order[None, :] < order[:, None])),
        axis=1,
    )
    pick = before[None, :] == order[:, None]
    route = [
        jnp.sum(jnp.where(pick, values[None, :], 0), axis=1)
        for values in (order, to_plane, to_slot - begins)
    ]
    counts = jnp.sum(in_part[None, :] < jnp.arange(len(sizes) + 1)[:, None], axis=1)
    outgoing = list(
        pack(off_blocks.reshape(requests, edge, edge), route + [counts], labels, sizes)
    )

    def planes_off(k):
        return [(z, z - k) for z in range(k, layers)], [(z, z + k) for z in range(layers - k)]

    down, up = planes_off(1)
    above, below = lax.ppermute(sketch, LINE, down), lax.ppermute(sketch, LINE, up)
    by_line = [(above, below)]
    early_lines = [above, below]
    if layers > 2:
        by_line.append((lax.ppermute(above, LINE, down), lax.ppermute(below, LINE, up)))
        both = lax.ppermute(sketch, LINE, sum(planes_off(3), []))
        by_line.append((both, both))
        early_lines.append(both)
    chip, core = lax.axis_index(CHIPS), lax.axis_index(CORE)
    if [lax.axis_size(axis) for axis in PLANE] == [2, 2, 2]:
        swap = [(0, 1), (1, 0)]
        by_x, by_y = (lax.ppermute(sketch, axis, swap) for axis in CHIPS)
        upper, lower = halves(by_y, by_x)
        across = [lax.ppermute(upper, CHIPS[0], swap), lax.ppermute(lower, CHIPS[1], swap)]
        outgoing[0] = hold(outgoing[0], [by_x, by_y])
        mine = join([sketch, by_y, by_x] + across)
        plane_omegas = [
            array.reshape((4,) + sketch.shape) for array in (mine, lax.ppermute(mine, CORE, swap))
        ]
        relative = True
    else:
        plane_omegas = [lax.all_gather(sketch, PLANE)]
        relative = False
    outgoing[1] = hold(outgoing[1], early_lines)
    parts = [lax.all_to_all(part, PLANE, 0, 0, tiled=True) for part in outgoing[:-1]]
    lines = sizes[0] * edge
    rows = parts[0][:, lines, :slots].astype(jnp.int32)
    cols = parts[0][:, lines + 1, :slots].astype(jnp.int32)

    layer, chip, core, row_label, col_label, rows, cols = lax.optimization_barrier(
        (layer, chip, core, row_label, col_label, rows, cols)
    )
    line_omegas = [
        (by_line[shift - 1][0], by_line[layers - shift - 1][1], (layer + shift < layers).astype(jnp.int32))
        for shift in shifts[:-1]
    ]
    sources = jnp.arange(planes)
    if relative:
        near_chips = (chip ^ jnp.arange(4)) * 2
        sources = jnp.concatenate([near_chips + core, near_chips + 1 - core])
    def send_mirror(index, after):
        part = sum(index * most >= end for end in ends)
        inside = index - (ends[part] - sizes[part]) // most
        shift = shifts[index]
        mirror = plane_sum(
            parts[part],
            plane_omegas,
            sources,
            rows,
            cols,
            inside,
            index * most,
            most,
            block_rows,
            jnp.bfloat16,
            True,
            after,
        )
        steps = [(z, (z + shift) % layers) for z in range(layers)]
        return lax.ppermute(mirror, LINE, steps), (mirror,)

    first, latest = send_mirror(0, ())

    home_rows = row_label.reshape(planes, slots)[:, -most:]
    home_cols = col_label.reshape(planes, slots)[:, -most:]
    cores = lax.axis_size(CORE)
    chips = planes // cores
    away = (chip + jnp.arange(1, chips)) % chips
    at_home = (home_rows, home_cols, outgoing[-1], sketch)
    far = functools.partial(far_sum, rows=rows, cols=cols, most=most, block_rows=block_rows)
    everything = dict(begin=0, parts=parts, omegas=line_omegas, home=at_home)
    early = dict(begin=0, parts=parts[:1], omegas=line_omegas[:1], home=at_home)
    late = dict(begin=sizes[0], parts=parts[1:], omegas=line_omegas[1:], home=None)

    def ask(chips_asked, dtype, what, after):
        if cores == 1:
            return [], after
        count = chips_asked.shape[0]
        other = far(
            chips_asked * cores + 1 - core, jnp.arange(count), count, dtype=dtype, after=after, **what
        )
        return [lax.ppermute(other, CORE, [(0, 1), (1, 0)])], (other,)

    other, latest = ask(away, jnp.float32, early, latest)
    home = plane_sum(
        outgoing[-1],
        plane_omegas,
        sources,
        home_rows,
        home_cols,
        0,
        0,
        most,
        block_rows,
        jnp.float32,
        False,
        latest,
    )
    begun = far(
        away * cores + core,
        jnp.arange(chips - 1),
        chips - 1,
        dtype=jnp.float32,
        adds=other,
        after=(home,),
        **early,
    )
    other, latest = ask(away, jnp.bfloat16, late, (begun,))
    second, latest = send_mirror(1, latest)
    sent = far(
        away * cores + core, away, chips, dtype=jnp.bfloat16, adds=[begun] + other, after=latest, **late
    )
    received = lax.all_to_all(sent, CHIPS, 0, 0, tiled=True)
    pieces, latest = [second], (sent,)
    for index in range(2, layers - 1):
        piece, latest = send_mirror(index, latest)
        pieces.append(piece)
    other, _ = ask(chip.reshape(1), jnp.float32, everything, (sent,))
    own = far(
        chip.reshape(1) * cores + core,
        jnp.arange(1),
        1,
        dtype=jnp.float32,
        adds=other,
        after=latest,
        **everything,
    )
    base = base_sum(diag_blocks, sketch, [home, own.reshape(sketch.shape), first])
    image, part = image_and_gram(base, chip, received, pieces, block_rows * edge * peers)
    gram = sum_over_devices(part)
    return factor_and_basis(gram, image)


def solution(mesh):
    rows, sub = mesh.devices.shape
    layers, cores = math.gcd(rows, 4), math.gcd(sub, 2)
    devices = mesh.devices.reshape(layers, rows // layers, sub // cores, cores)
    placed = (P(ALL, None, None), P(ALL, None, None, None), P(ALL, None), P(ALL, None))
    return jax.shard_map(
        on_device,
        mesh=Mesh(devices, ALL),
        in_specs=placed,
        out_specs=(P(ALL, None), P()),
        check_vma=False,
    )
```
